32 devices in a mesh: spec: 4 (over y, x), wave: 8 (over z, core).
Axes of the slice: x: 2, y: 2, z: 4, core: 2. Of those that a mesh axis runs over, the one named last changes fastest.
Arguments:
- pixels: float32 [8, 8, 400, 500], P(None, 'spec', 'wave')
- ivar: float32 [8, 8, 400, 500], P(None, 'spec', 'wave'), may hold values from 0.25 to 4
- mask: int32 [8, 8, 400, 500], P(None, 'spec', 'wave'), may hold values 0 or 1
- psf_left: float32 [8, 8, 400, 500], P(None, 'spec', 'wave'), may hold values from 0.1 to 0.45
- psf_right: float32 [8, 8, 400, 500], P(None, 'spec', 'wave'), may hold values from 0.1 to 0.45
- sky_index: int32 [8, 40], P('spec'), may hold values from 0 to 499, as said below
Outputs:
- cleaned: float32 [8, 8, 400, 500], P(None, 'spec', 'wave')
- sky_model: float32 [8, 400], P(None, 'wave')
The draws below stay inside these ranges and needn't reach their ends.
Inputs may be any that keep to these rules, and one draw needn't show every extreme that they name: `sky_index`: each row names 40 different fibres.
All inputs are finite; a program needn't handle non-finite values. No bound on the sum of `mask` on one device may be relied on, other than what follows from the above.
Results may differ from the reference program's by a relative error of at most 0.0002.
Values sent between devices are 32-bit elements; how exact they have to be, the bound alone decides.
No kernel may reach another device: no remote copies, remote signals or barrier semaphores. Data moves between devices by JAX's collectives and lax.ppermute only.
A program may use at most 128 MiB of HBM per device.

```python
import math
import jax
import jax.numpy as jnp
from jax import lax

F = 500
PW = 50
NSKY = 40
EXPO = 8
SPECS = 8
NW = 400


def draw_pixels(key, part):
    key_sky, key_thru, key_tilt, key_noise = jax.random.split(key, 4)
    sky_level = jnp.exp(jax.random.uniform(key_sky, (EXPO, 1, NW, 1), jnp.float32, jnp.log(0.5), jnp.log(4.0)))
    through = 1.0 + 0.3 * jax.random.normal(key_thru, (EXPO, SPECS, 1, F), jnp.float32)
    tilt = 0.2 * jax.random.normal(key_tilt, (EXPO, SPECS, 1, F), jnp.float32)
    position = 2.0 * jnp.arange(NW).astype(jnp.float32) / max(NW - 1, 1) - 1.0
    noise = jax.random.normal(key_noise, (EXPO, SPECS, NW, F), jnp.float32)
    return sky_level * (through + tilt * position[None, None, :, None]) + noise


def draw_sky_index(key, part):
    keys = jax.random.split(jax.random.fold_in(key, 7), SPECS)
    chosen = jax.vmap(lambda single: jax.random.permutation(single, F)[:NSKY])(keys)
    return chosen.astype(jnp.int32)


def with_ends(entries, own_key, smallest, largest):
    longest = entries.shape.index(max(entries.shape))
    spots = []
    for shift in (0, 1):
        where = [jax.random.randint(jax.random.fold_in(own_key, axis), (), 0, length) for axis, length in enumerate(entries.shape)]
        where[longest] = (where[longest] + shift) % entries.shape[longest]
        spots.append(tuple(where))
    return entries.at[spots[0]].set(smallest).at[spots[1]].set(largest)


def block_scale(rng, dims, cuts, smallest, largest):
    def one(dim, parts):
        heights = jax.random.uniform(jax.random.fold_in(jax.random.fold_in(rng, 6), dim), (parts,), jnp.float32, smallest / len(cuts), largest / len(cuts))
        return jnp.repeat(jnp.exp(heights), dims[dim] // parts).reshape((-1,) + (1,) * (len(dims) - dim - 1))

    level = one(*cuts[0])
    for cut in cuts[1:]:
        level = level * one(*cut)
    return level


def setup_inputs(seed: int = 0) -> dict:
    key_of = jax.random.split(jax.random.key(seed), 7)
    pixels = draw_pixels(jax.random.fold_in(key_of[6], 71), 0)
    ivar = jnp.clip(jnp.exp(math.log(4.0) - 2.7725887 * jax.random.uniform(key_of[1], (EXPO, SPECS, NW, F), jnp.float32) ** block_scale(key_of[1], (EXPO, SPECS, NW, F), ((1, 4), (2, 8)), -0.2, 0.2)), 0.25, 4.0)
    mask = with_ends((jax.random.randint(key_of[2], (EXPO, SPECS, NW, F), 0, 16) < 1).astype(jnp.int32), jax.random.fold_in(key_of[2], 1), 0, 1)
    psf_left = jnp.clip(0.1 + 0.35 * jax.random.uniform(key_of[3], (EXPO, SPECS, NW, F), jnp.float32) ** block_scale(key_of[3], (EXPO, SPECS, NW, F), ((1, 4), (2, 8)), -0.2, 0.2), 0.1, 0.45)
    psf_right = jnp.clip(0.1 + 0.35 * jax.random.uniform(key_of[4], (EXPO, SPECS, NW, F), jnp.float32) ** block_scale(key_of[4], (EXPO, SPECS, NW, F), ((1, 4), (2, 8)), -0.2, 0.2), 0.1, 0.45)
    sky_index = draw_sky_index(jax.random.fold_in(key_of[6], 71), 0)
    return {"pixels": pixels, "ivar": ivar, "mask": mask, "psf_left": psf_left, "psf_right": psf_right, "sky_index": sky_index}


REG = 0.05
RIDGE = 1.0

def shift_up(values):
    return jnp.concatenate([values[1:], jnp.zeros_like(values[:1])], axis=0)

def shift_down(values):
    return jnp.concatenate([jnp.zeros_like(values[:1]), values[:-1]], axis=0)

def band_solve(pixel_rows, weight, left, right):
    diag_main = weight + shift_up(weight * left * left) + shift_down(weight * right * right) + REG
    first_off = weight * right + shift_up(weight * left)
    second_off = shift_up(weight * left * right)
    rhs_rows = weight * pixel_rows + shift_up(weight * left * pixel_rows) + shift_down(weight * right * pixel_rows)
    prev_one = shift_down(first_off)
    prev_two = shift_down(shift_down(second_off))
    length = diag_main.shape[0]
    unit_fill = jnp.ones_like(diag_main[0])
    zero_fill = jnp.zeros_like(diag_main[0])
    pivots, lowers, farther, forward = ([], [], [], [])
    pivot_last, pivot_before = (unit_fill, unit_fill)
    lower_last, forward_last, forward_before = (zero_fill, zero_fill, zero_fill)
    for step_row in range(length):
        far_term = prev_two[step_row] / pivot_before
        lower_term = (prev_one[step_row] - far_term * lower_last) / pivot_last
        pivot_now = jnp.sqrt(diag_main[step_row] - lower_term * lower_term - far_term * far_term)
        forward_now = (rhs_rows[step_row] - lower_term * forward_last - far_term * forward_before) / pivot_now
        pivots.append(pivot_now)
        lowers.append(lower_term)
        farther.append(far_term)
        forward.append(forward_now)
        pivot_before, pivot_last = (pivot_last, pivot_now)
        lower_last = lower_term
        forward_before, forward_last = (forward_last, forward_now)
    solved = [None] * length
    next_one, next_two = (zero_fill, zero_fill)
    for step_row in reversed(range(length)):
        lower_next = lowers[step_row + 1] if step_row + 1 < length else zero_fill
        far_next = farther[step_row + 2] if step_row + 2 < length else zero_fill
        result_now = (forward[step_row] - lower_next * next_one - far_next * next_two) / pivots[step_row]
        solved[step_row] = result_now
        next_two, next_one = (next_one, result_now)
    return (jnp.stack(solved), diag_main)

def extract_rows(extended, patch_count):
    span = PW + 8
    pieces = [extended[..., start * PW:start * PW + span, :] for start in range(patch_count)]
    picked = jnp.moveaxis(jnp.stack(pieces), -2, 0)
    solved, diag_main = band_solve(picked[:, :, 0], picked[:, :, 1], picked[:, :, 2], picked[:, :, 3])
    outputs = []
    for field in (solved, diag_main):
        kept = field[4:4 + PW]
        kept = jnp.moveaxis(jnp.moveaxis(kept, 0, -2), 0, -3)
        outputs.append(kept.reshape(kept.shape[:-3] + (patch_count * PW, kept.shape[-1])))
    return (outputs[0], outputs[1])

def reference(pixels, ivar, mask, psf_left, psf_right, sky_index):
    weight = ivar * (1.0 - mask.astype(jnp.float32))
    stacked = jnp.stack([pixels, weight, psf_left, psf_right])
    padded = jnp.pad(stacked, ((0, 0), (0, 0), (0, 0), (4, 4), (0, 0)))
    padded = jnp.moveaxis(padded, 1, 0)
    patch_count = NW // PW
    flux, precision = lax.map(lambda single: extract_rows(single, patch_count), padded)
    is_sky = lax.optimization_barrier(jnp.sum((sky_index[:, :, None] == jnp.arange(F)[None, None, :]).astype(jnp.float32), axis=1))
    numer = jnp.einsum('eswf,sf->ew', precision * flux, is_sky, precision=lax.Precision.HIGHEST)
    denom = jnp.einsum('eswf,sf->ew', precision, is_sky, precision=lax.Precision.HIGHEST)
    sky_model = numer / denom
    position = 2.0 * jnp.arange(NW).astype(jnp.float32) / (NW - 1) - 1.0
    square = sky_model * sky_model
    moment_zero = lax.optimization_barrier(jnp.sum(square, axis=1))
    moment_one = lax.optimization_barrier(jnp.sum(square * position, axis=1))
    moment_two = lax.optimization_barrier(jnp.sum(square * position * position, axis=1))
    first_sum = jnp.einsum('eswf,ew->esf', flux, sky_model, precision=lax.Precision.HIGHEST)
    second_sum = jnp.einsum('eswf,ew->esf', flux, sky_model * position, precision=lax.Precision.HIGHEST)
    upper_left = (moment_zero + RIDGE)[:, None, None]
    lower_right = (moment_two + RIDGE)[:, None, None]
    cross = moment_one[:, None, None]
    determinant = upper_left * lower_right - cross * cross
    slope_a = (lower_right * first_sum - cross * second_sum) / determinant
    slope_b = (upper_left * second_sum - cross * first_sum) / determinant
    fitted = (slope_a[:, :, None, :] + slope_b[:, :, None, :] * position[None, None, :, None]) * sky_model[:, None, :, None]
    cleaned = flux - fitted
    return (cleaned, sky_model)
```

```python
import functools

import jax
import jax.numpy as jnp
from jax import lax
from jax.experimental import pallas as pl
from jax.experimental.pallas import tpu as pltpu
from jax.sharding import PartitionSpec as P

REG = 0.05
RIDGE = 1.0
HALO = 4
PARTS = 6
LANES = 128

F32 = jnp.float32
VM = pl.BlockSpec(memory_space=pltpu.VMEM)
SM = pl.BlockSpec(memory_space=pltpu.SMEM)
HB = pl.BlockSpec(memory_space=pl.ANY)


def in_vmem(shape, dtype=F32):
    return jax.ShapeDtypeStruct(shape, dtype)


def recip(values):
    return 1.0 / values


def weight_of(ivar, mask):
    return jnp.where(mask == 0, ivar, 0.0)


def edge_message(p, w, l, r):
    wl = [a * b for a, b in zip(w, l)]
    wr = [a * b for a, b in zip(w, r)]
    d0 = w[0] + wl[1] * l[1] + REG
    d1 = w[1] + wr[0] * r[0] + wl[2] * l[2] + REG
    d2 = w[2] + wr[1] * r[1] + wl[3] * l[3] + REG
    d3 = w[3] + wr[2] * r[2]
    d4 = wr[3] * r[3]
    raw = d4
    a01 = wr[0] + wl[1]
    a12 = wr[1] + wl[2]
    a23 = wr[2] + wl[3]
    a34 = wr[3]
    a02 = wl[1] * r[1]
    a13 = wl[2] * r[2]
    a24 = wl[3] * r[3]
    b0 = w[0] * p[0] + wl[1] * p[1]
    b1 = w[1] * p[1] + wr[0] * p[0] + wl[2] * p[2]
    b2 = w[2] * p[2] + wr[1] * p[1] + wl[3] * p[3]
    b3 = w[3] * p[3] + wr[2] * p[2]
    b4 = wr[3] * p[3]
    inv = recip(d0)
    near, far = a01 * inv, a02 * inv
    d1, a12, d2 = d1 - near * a01, a12 - near * a02, d2 - far * a02
    b1, b2 = b1 - near * b0, b2 - far * b0
    inv = recip(d1)
    near, far = a12 * inv, a13 * inv
    d2, a23, d3 = d2 - near * a12, a23 - near * a13, d3 - far * a13
    b2, b3 = b2 - near * b1, b3 - far * b1
    inv = recip(d2)
    near, far = a23 * inv, a24 * inv
    d3, a34, d4 = d3 - near * a23, a34 - near * a24, d4 - far * a24
    b3, b4 = b3 - near * b2, b4 - far * b2
    return (d3, a34, d4, b3, b4, raw)


def edge_kernel(pix, iva, msk, lef, rig, near_out, far_out, bufs, mbuf, out_buf, sems, out_sems):
    exposures, rows = pix.shape[0], pix.shape[1]
    odd = lax.rem(lax.axis_index("wave"), 2)
    copies = []
    for end, start in enumerate((0, rows - HALO)):
        for slot, ref in enumerate((pix, iva, lef, rig)):
            copies.append(
                pltpu.make_async_copy(
                    ref.at[:, start : start + HALO], bufs.at[end, slot], sems.at[end, slot]
                )
            )
        copies.append(
            pltpu.make_async_copy(msk.at[:, start : start + HALO], mbuf.at[end], sems.at[end, 4])
        )
    for copy in copies:
        copy.start()
    for end in range(2):
        for copy in copies[5 * end : 5 * end + 5]:
            copy.wait()
        order = range(HALO - 1, -1, -1) if end == 0 else range(HALO)
        for e in range(exposures):
            p = [bufs[end, 0, e, k] for k in order]
            w = [weight_of(bufs[end, 1, e, k], mbuf[end, e, k]) for k in order]
            l = [bufs[end, 2, e, k] for k in order]
            r = [bufs[end, 3, e, k] for k in order]
            if end == 0:
                l, r = r, l
            for slot, part in enumerate(edge_message(p, w, l, r)):
                out_buf[end, slot, e] = part

    def send(end, out, base):
        return [
            pltpu.make_async_copy(out_buf.at[end, :, e], out.at[:, :, e], out_sems.at[base + e])
            for e in range(exposures)
        ]

    for parity in range(2):

        @pl.when(odd == parity)
        def _():
            sends = send(1 - parity, near_out, 0) + send(parity, far_out, exposures)
            for copy in sends:
                copy.start()
            for copy in sends:
                copy.wait()


def edge_call(arrays):
    exposures, rows, specs, fibres = arrays[0].shape
    out = jax.ShapeDtypeStruct((PARTS, specs, exposures, fibres), F32)
    return pl.pallas_call(
        edge_kernel,
        out_shape=(out, out),
        in_specs=[HB] * 5,
        out_specs=(HB, HB),
        scratch_shapes=[
            pltpu.VMEM((2, 4, exposures, HALO, specs, fibres), F32),
            pltpu.VMEM((2, exposures, HALO, specs, fibres), jnp.int32),
            pltpu.VMEM((2, PARTS, exposures, specs, fibres), F32),
            pltpu.SemaphoreType.DMA((2, 5)),
            pltpu.SemaphoreType.DMA((2 * exposures,)),
        ],
        cost_estimate=pl.CostEstimate(flops=10**6, bytes_accessed=10**6, transcendentals=0),
        name="edges",
    )(*arrays)


def band_kernel(pix, iva, msk, lef, rig, sky_index, diag, off_one, off_two, rhs, sky_mask, bufs, mbuf, sems):
    exposures, rows, specs, fibres = pix.shape
    copies = []
    for e in range(exposures):
        for slot, ref in enumerate((pix, iva, lef, rig)):
            copies.append(
                pltpu.make_async_copy(ref.at[e], bufs.at[slot, :, :, e], sems.at[slot, e])
            )
        copies.append(pltpu.make_async_copy(msk.at[e], mbuf.at[:, :, e], sems.at[4, e]))
    for copy in copies:
        copy.start()
    lane = lax.broadcasted_iota(jnp.int32, (exposures, fibres), 1)
    for s in range(specs):
        found = lane == sky_index[s, 0]
        for k in range(1, sky_index.shape[1]):
            found = found | (lane == sky_index[s, k])
        sky_mask[s] = jnp.where(found, 1.0, 0.0)
    for copy in copies:
        copy.wait()

    for s in range(specs):

        def terms(k):
            p, l, r = bufs[0, k, s], bufs[2, k, s], bufs[3, k, s]
            w = weight_of(bufs[1, k, s], mbuf[k, s])
            wl, wr, wp = w * l, w * r, w * p
            return (w, wp, wl, wr, wl * l, wr * r, wl * p, wr * p, wl * r)

        def body(k, carry):
            w1, wp1, wr1, wrr2, wrp2, wrr1, wrp1 = carry
            w, wp, wl, wr, wll, wrr, wlp, wrp, wlr = terms(k)
            diag[k, s] = w1 + wll + (wrr2 + REG)
            off_one[k, s] = wr1 + wl
            off_two[k, s] = wlr
            rhs[k, s] = wp1 + wlp + wrp2
            return (w, wp, wr, wrr1, wrp1, wrr, wrp)

        last = body(1, body(0, (0.0,) * 7))
        last = lax.fori_loop(2, rows, body, last, unroll=4)
        w1, wp1, wr1, wrr2, wrp2, wrr1, wrp1 = last
        diag[rows, s] = w1 + (wrr2 + REG)
        off_one[rows, s] = wr1
        rhs[rows, s] = wp1 + wrp2
        diag[rows + 1, s] = wrr1 + REG
        rhs[rows + 1, s] = wrp1


def band_call(arrays, sky_index):
    exposures, rows, specs, fibres = arrays[0].shape
    grown = in_vmem((rows + 2, specs, exposures, fibres))
    return pl.pallas_call(
        band_kernel,
        out_shape=(grown, grown, grown, grown, in_vmem((specs, exposures, fibres))),
        in_specs=[HB] * 5 + [SM],
        out_specs=(VM,) * 5,
        scratch_shapes=[
            pltpu.VMEM((4, rows, specs, exposures, fibres), F32),
            pltpu.VMEM((rows, specs, exposures, fibres), jnp.int32),
            pltpu.SemaphoreType.DMA((5, exposures)),
        ],
        compiler_params=pltpu.CompilerParams(vmem_limit_bytes=40 * 2**20),
        cost_estimate=pl.CostEstimate(flops=10**7, bytes_accessed=10**7, transcendentals=0),
        name="bands",
    )(*arrays, sky_index)


def solve_kernel(near, far, diag, off_one, off_two, rhs, sky_mask, flux, sums, lower, lower_far, half):
    count, specs, exposures, fibres = diag.shape
    rows = count - 2
    odd = lax.rem(lax.axis_index("wave"), 2)
    is_odd = odd == 1

    def left(part, s):
        return jnp.where(is_odd, near[part, s], far[part, s])

    def right(part, s):
        return jnp.where(is_odd, far[part, s], near[part, s])

    lane = lax.broadcasted_iota(jnp.int32, (exposures, LANES), 1)
    numer = jnp.zeros((exposures, LANES), F32)
    denom = jnp.zeros((exposures, LANES), F32)

    zero = jnp.zeros((exposures, fibres), F32)
    spans = range(specs)

    def step(k, state, d, a, b, far_a):
        inv1, inv2, mult1, y1, y2 = state
        f = far_a * inv2
        upper = a - far_a * mult1
        g = upper * inv1
        pivot = d - f * far_a - g * upper
        y = b - f * y2 - g * y1
        return f, g, y, (recip(pivot), inv1, g, y, y1)

    def put(k, s, f, g, y, state):
        lower_far[k, s] = f
        lower[k, s] = g
        half[k, s] = y * state[0]

    states = []
    for s in spans:
        state = (zero,) * 5
        f, g, y, state = step(0, state, diag[0, s] + left(0, s), zero, rhs[0, s] + left(3, s), zero)
        put(0, s, f, g, y, state)
        f, g, y, state = step(
            1,
            state,
            diag[1, s] + left(2, s),
            off_one[0, s] + left(1, s),
            rhs[1, s] + left(4, s),
            zero,
        )
        put(1, s, f, g, y, state)
        states.append(state)

    def forward(k, states):
        results = []
        for s in spans:
            f, g, y, state = step(
                k, states[s], diag[k, s], off_one[k - 1, s], rhs[k, s], off_two[k - 2, s]
            )
            put(k, s, f, g, y, state)
            results.append(state)
        return tuple(results)

    states = lax.fori_loop(2, rows, forward, tuple(states), unroll=4)

    after = [None] * specs
    for s in spans:
        f, g, y, state = step(
            rows,
            states[s],
            diag[rows, s] + right(2, s),
            off_one[rows - 1, s],
            rhs[rows, s] + right(4, s),
            off_two[rows - 2, s],
        )
        f1, g1, y1, state1 = step(
            rows + 1,
            state,
            diag[rows + 1, s] + right(0, s),
            off_one[rows, s] + right(1, s),
            rhs[rows + 1, s] + right(3, s),
            off_two[rows - 1, s],
        )
        last = y1 * state1[0]
        here = y * state[0] - g1 * last
        flux[rows - 1, s] = here
        after[s] = (here, last, g, f1, f)

    def total(parts):
        return jnp.sum(parts, axis=1, keepdims=True)

    masks = [sky_mask[s] for s in spans]

    def spread(k, numer, denom, precs, values):
        weighted = sum(masks[s] * precs[s] for s in spans)
        valued = sum(masks[s] * precs[s] * values[s] for s in spans)
        return (
            jnp.where(lane == k, total(valued), numer),
            jnp.where(lane == k, total(weighted), denom),
        )

    precs = [diag[rows, s] + right(5, s) for s in spans]
    numer, denom = spread(rows - 1, numer, denom, precs, [after[s][0] for s in spans])

    def backward(step_row, carry):
        k = rows - 1 - step_row
        numer, denom, after = carry
        results = []
        for s in spans:
            x1, x2, g1, f2, f1 = after[s]
            value = half[k, s] - g1 * x1 - f2 * x2
            flux[k - 1, s] = value
            results.append((value, x1, lower[k, s], f1, lower_far[k, s]))
        precs = [diag[k, s] for s in spans]
        numer, denom = spread(k - 1, numer, denom, precs, [r[0] for r in results])
        return (numer, denom, tuple(results))

    numer, denom, after = lax.fori_loop(0, rows - 2, backward, (numer, denom, tuple(after)), unroll=4)
    values = []
    for s in spans:
        x1, x2, g1, f2, f1 = after[s]
        value = half[1, s] - g1 * x1 - f2 * x2
        flux[0, s] = value
        values.append(value)
    precs = [diag[1, s] + left(5, s) for s in spans]
    numer, denom = spread(0, numer, denom, precs, values)
    sums[0] = numer
    sums[1] = denom


def solve_call(near, far, bands):
    count, specs, exposures, fibres = bands[0].shape
    rows = count - 2
    scratch = pltpu.VMEM((count, specs, exposures, fibres), F32)
    return pl.pallas_call(
        solve_kernel,
        out_shape=(in_vmem((rows, specs, exposures, fibres)), in_vmem((2, exposures, LANES))),
        in_specs=[VM] * 7,
        out_specs=(VM, VM),
        scratch_shapes=[scratch] * 3,
        compiler_params=pltpu.CompilerParams(vmem_limit_bytes=40 * 2**20),
        cost_estimate=pl.CostEstimate(flops=10**7, bytes_accessed=10**7, transcendentals=0),
        name="solve",
    )(near, far, *bands)


def position_of(index, total_rows):
    return 2.0 * index.astype(F32) / (total_rows - 1) - 1.0


def regress_kernel(total_rows, flux, other, sums, regress, sky_out):
    rows, specs, exposures, fibres = flux.shape
    device = lax.axis_index("wave")
    lane = lax.broadcasted_iota(jnp.int32, (exposures, LANES), 1)
    valid = lane < rows
    first = [[jnp.zeros((exposures, fibres), F32) for _ in range(specs)] for _ in range(2)]
    moments = [jnp.zeros((exposures, 1), F32) for _ in range(3)]
    for which, (ref, base) in enumerate(((flux, device * rows), (other, (device - 1) * rows))):
        sky = jnp.where(valid, sums[2 * which] / jnp.where(valid, sums[2 * which + 1], 1.0), 0.0)
        position = position_of(base + lane, total_rows)
        tilted = sky * position
        moments[0] += jnp.sum(sky * sky, axis=1, keepdims=True)
        moments[1] += jnp.sum(sky * tilted, axis=1, keepdims=True)
        moments[2] += jnp.sum(tilted * tilted, axis=1, keepdims=True)
        if which == 0:
            sky_out[...] = sky
        for k in range(rows):
            plain_k = jnp.broadcast_to(sky[:, k : k + 1], (exposures, fibres))
            tilted_k = jnp.broadcast_to(tilted[:, k : k + 1], (exposures, fibres))
            for s in range(specs):
                values = ref[k, s]
                first[0][s] += values * plain_k
                first[1][s] += values * tilted_k
    for r in range(2):
        for s in range(specs):
            regress[r * specs + s] = first[r][s]
    wide = lax.broadcasted_iota(jnp.int32, (exposures, fibres), 1)
    regress[2 * specs] = jnp.where(wide == 0, moments[0], jnp.where(wide == 1, moments[1], moments[2]))


def regress_call(total_rows, flux, other, sums):
    rows, specs, exposures, fibres = flux.shape
    return pl.pallas_call(
        functools.partial(regress_kernel, total_rows),
        out_shape=(
            in_vmem((2 * specs + 1, exposures, fibres)),
            in_vmem((exposures, LANES)),
        ),
        in_specs=[VM] * 3,
        out_specs=(VM, VM),
        compiler_params=pltpu.CompilerParams(vmem_limit_bytes=40 * 2**20),
        cost_estimate=pl.CostEstimate(flops=10**6, bytes_accessed=10**6, transcendentals=0),
        name="regress",
    )(flux, other, sums)


def clean_kernel(total_rows, flux, sky_ref, mine, sent, out, buf, sems):
    rows, specs, exposures, fibres = flux.shape
    device = lax.axis_index("wave")
    is_odd = lax.rem(device, 2) == 1

    def got(slot):
        return jnp.where(is_odd, mine[slot], sent[slot])

    moments = got(2 * specs)
    upper_left = moments[:, 0:1] + RIDGE
    cross = moments[:, 1:2]
    lower_right = moments[:, 2:3] + RIDGE
    inverse = 1.0 / (upper_left * lower_right - cross * cross)
    slope_a, slope_b = [], []
    for s in range(specs):
        r1, r2 = got(s), got(specs + s)
        slope_a.append((lower_right * r1 - cross * r2) * inverse)
        slope_b.append((upper_left * r2 - cross * r1) * inverse)
    lane = lax.broadcasted_iota(jnp.int32, (exposures, LANES), 1)
    sky = sky_ref[...]
    tilted = sky * position_of(device * rows + lane, total_rows)
    chunks = sems.shape[0]
    size = -(-rows // chunks)
    copies = []
    for c in range(chunks):
        low, high = c * size, min(rows, (c + 1) * size)
        for k in range(low, high):
            plain_k = jnp.broadcast_to(sky[:, k : k + 1], (exposures, fibres))
            tilted_k = jnp.broadcast_to(tilted[:, k : k + 1], (exposures, fibres))
            for s in range(specs):
                buf[k, s] = flux[k, s] - (slope_a[s] * plain_k + slope_b[s] * tilted_k)
        for e in range(exposures):
            copy = pltpu.make_async_copy(
                buf.at[low:high, :, e], out.at[e, low:high], sems.at[c, e]
            )
            copy.start()
            copies.append(copy)
    for copy in copies:
        copy.wait()


def clean_call(total_rows, flux, sky, mine, sent):
    rows, specs, exposures, fibres = flux.shape
    return pl.pallas_call(
        functools.partial(clean_kernel, total_rows),
        out_shape=jax.ShapeDtypeStruct((exposures, rows, specs, fibres), F32),
        in_specs=[VM] * 4,
        out_specs=HB,
        scratch_shapes=[
            pltpu.VMEM((rows, specs, exposures, fibres), F32),
            pltpu.SemaphoreType.DMA((2, exposures)),
        ],
        compiler_params=pltpu.CompilerParams(vmem_limit_bytes=40 * 2**20),
        cost_estimate=pl.CostEstimate(flops=10**6, bytes_accessed=10**6, transcendentals=0),
        name="clean",
    )(flux, sky, mine, sent)


def powers(low, high):
    steps = []
    while low < high:
        steps.append(low)
        low *= 2
    return steps


def local(pixels, ivar, mask, psf_left, psf_right, sky_index):
    arrays = [jnp.transpose(x, (0, 2, 1, 3)) for x in (pixels, ivar, mask, psf_left, psf_right)]
    rows = pixels.shape[2]
    wave, spec = lax.axis_size("wave"), lax.axis_size("spec")
    total_rows = rows * wave
    near, far = edge_call(arrays)
    far = lax.ppermute(
        far, "wave", [pair for i in range(1, wave - 1, 2) for pair in ((i, i + 1), (i + 1, i))]
    )
    near = lax.ppermute(near, "wave", [(i, i ^ 1) for i in range(wave)])
    bands = band_call(arrays, sky_index)
    flux, sums = solve_call(near, far, bands)
    to_odd = [(i, i + 1) for i in range(0, wave, 2)]
    sums = jnp.concatenate([sums, lax.ppermute(sums, "wave", to_odd)])
    other = lax.ppermute(flux, "wave", to_odd)
    for k in powers(1, spec):
        sums = sums + lax.ppermute(sums, "spec", [(i, i ^ k) for i in range(spec)])
    regress, sky = regress_call(total_rows, flux, other, sums)
    for k in powers(2, wave):
        regress = regress + lax.ppermute(regress, "wave", [(i, i ^ k) for i in range(1, wave, 2)])
    sent = lax.ppermute(regress, "wave", [(i + 1, i) for i in range(0, wave, 2)])
    cleaned = clean_call(total_rows, flux, sky, regress, sent)
    return (jnp.transpose(cleaned, (0, 2, 1, 3)), sky[:, :rows])


def solution(mesh):
    block = P(None, "spec", "wave", None)
    return jax.shard_map(
        local,
        mesh=mesh,
        in_specs=(block,) * 5 + (P("spec", None),),
        out_specs=(block, P(None, "wave")),
        check_vma=False,
    )
```

```python
import functools

import jax
import jax.numpy as jnp
from jax import lax
from jax.experimental import pallas as pl
from jax.experimental.pallas import tpu as pltpu
from jax.sharding import PartitionSpec as P

REG = 0.05
RIDGE = 1.0
HALO = 4
PARTS = 6
LANES = 128

F32 = jnp.float32
VM = pl.BlockSpec(memory_space=pltpu.VMEM)
SM = pl.BlockSpec(memory_space=pltpu.SMEM)
HB = pl.BlockSpec(memory_space=pl.ANY)


def in_vmem(shape, dtype=F32):
    return jax.ShapeDtypeStruct(shape, dtype)


def recip(values):
    return 1.0 / values


def weight_of(ivar, mask):
    return jnp.where(mask == 0, ivar, 0.0)


def edge_message(p, w, l, r):
    wl = [a * b for a, b in zip(w, l)]
    wr = [a * b for a, b in zip(w, r)]
    d0 = w[0] + wl[1] * l[1] + REG
    d1 = w[1] + wr[0] * r[0] + wl[2] * l[2] + REG
    d2 = w[2] + wr[1] * r[1] + wl[3] * l[3] + REG
    d3 = w[3] + wr[2] * r[2]
    d4 = wr[3] * r[3]
    raw = d4
    a01 = wr[0] + wl[1]
    a12 = wr[1] + wl[2]
    a23 = wr[2] + wl[3]
    a34 = wr[3]
    a02 = wl[1] * r[1]
    a13 = wl[2] * r[2]
    a24 = wl[3] * r[3]
    b0 = w[0] * p[0] + wl[1] * p[1]
    b1 = w[1] * p[1] + wr[0] * p[0] + wl[2] * p[2]
    b2 = w[2] * p[2] + wr[1] * p[1] + wl[3] * p[3]
    b3 = w[3] * p[3] + wr[2] * p[2]
    b4 = wr[3] * p[3]
    inv = recip(d0)
    near, far = a01 * inv, a02 * inv
    d1, a12, d2 = d1 - near * a01, a12 - near * a02, d2 - far * a02
    b1, b2 = b1 - near * b0, b2 - far * b0
    inv = recip(d1)
    near, far = a12 * inv, a13 * inv
    d2, a23, d3 = d2 - near * a12, a23 - near * a13, d3 - far * a13
    b2, b3 = b2 - near * b1, b3 - far * b1
    inv = recip(d2)
    near, far = a23 * inv, a24 * inv
    d3, a34, d4 = d3 - near * a23, a34 - near * a24, d4 - far * a24
    b3, b4 = b3 - near * b2, b4 - far * b2
    return (d3, a34, d4, b3, b4, raw)


def prepare_kernel(
    chunks, pix, iva, msk, lef, rig, sky_index, near_out, far_out, diag, off_one, off_two, rhs, sky_mask, bufs, mbuf, sems
):
    exposures, rows, specs, fibres = pix.shape
    odd = lax.rem(lax.axis_index("wave"), 2) == 1
    bounds = [rows * c // chunks for c in range(chunks + 1)]
    for c in range(chunks):
        low, high = bounds[c], bounds[c + 1]
        for e in range(exposures):
            for slot, ref in enumerate((pix, iva, lef, rig)):
                pltpu.make_async_copy(
                    ref.at[e, low:high], bufs.at[slot, low:high, :, e], sems.at[0, c]
                ).start()
            pltpu.make_async_copy(
                msk.at[e, low:high], mbuf.at[low:high, :, e], sems.at[1, c]
            ).start()
    lane = lax.broadcasted_iota(jnp.int32, (exposures, fibres), 1)
    for s in range(specs):
        found = lane == sky_index[s, 0]
        for k in range(1, sky_index.shape[1]):
            found = found | (lane == sky_index[s, k])
        sky_mask[s] = jnp.where(found, 1.0, 0.0)

    def load(k, s):
        return bufs[0, k, s], weight_of(bufs[1, k, s], mbuf[k, s]), bufs[2, k, s], bufs[3, k, s]

    def row(k, s, carry):
        w1, wp1, wr1, wrr2, wrp2, wrr1, wrp1 = carry
        p, w, l, r = load(k, s)
        wl, wr, wp = w * l, w * r, w * p
        diag[k, s] = w1 + wl * l + (wrr2 + REG)
        off_one[k, s] = wr1 + wl
        off_two[k, s] = wl * r
        rhs[k, s] = wp1 + wl * p + wrp2
        return (w, wp, wr, wrr1, wrp1, wr * r, wr * p)

    def message(end, s):
        order = range(HALO - 1, -1, -1) if end == 0 else range(rows - HALO, rows)
        p, w, l, r = zip(*[load(k, s) for k in order])
        return edge_message(p, w, r, l) if end == 0 else edge_message(p, w, l, r)

    carries = [(0.0,) * 7 for _ in range(specs)]
    for c in range(chunks):
        low, high = bounds[c], bounds[c + 1]
        part, mpart = bufs.at[:, low:high], mbuf.at[low:high]
        pltpu.make_async_copy(part, part, sems.at[0, c]).wait()
        pltpu.make_async_copy(mpart, mpart, sems.at[1, c]).wait()
        for s in range(specs):
            for k in range(low, high):
                carries[s] = row(k, s, carries[s])
            if c == 0:
                for slot, value in enumerate(message(0, s)):
                    near_out[slot, s] = value
    for s in range(specs):
        w1, wp1, wr1, wrr2, wrp2, wrr1, wrp1 = carries[s]
        diag[rows, s] = w1 + (wrr2 + REG)
        off_one[rows, s] = wr1
        rhs[rows, s] = wp1 + wrp2
        diag[rows + 1, s] = wrr1 + REG
        rhs[rows + 1, s] = wrp1
        for slot, value in enumerate(message(1, s)):
            top = near_out[slot, s]
            near_out[slot, s] = jnp.where(odd, top, value)
            far_out[slot, s] = jnp.where(odd, value, top)


def prepare_call(arrays, sky_index):
    exposures, rows, specs, fibres = arrays[0].shape
    chunks = 5
    message = in_vmem((PARTS, specs, exposures, fibres))
    grown = in_vmem((rows + 2, specs, exposures, fibres))
    arrays = [pltpu.with_memory_space_constraint(x, pltpu.HBM) for x in arrays]
    return pl.pallas_call(
        functools.partial(prepare_kernel, chunks),
        out_shape=(message, message, grown, grown, grown, grown, in_vmem((specs, exposures, fibres))),
        in_specs=[pl.BlockSpec(memory_space=pltpu.HBM)] * 5 + [SM],
        out_specs=(VM,) * 7,
        scratch_shapes=[
            pltpu.VMEM((4, rows, specs, exposures, fibres), F32),
            pltpu.VMEM((rows, specs, exposures, fibres), jnp.int32),
            pltpu.SemaphoreType.DMA((2, chunks)),
        ],
        compiler_params=pltpu.CompilerParams(vmem_limit_bytes=24 * 2**20),
        cost_estimate=pl.CostEstimate(flops=10**7, bytes_accessed=10**7, transcendentals=0),
        name="prepare",
    )(*arrays, sky_index)


def solve_kernel(near, far, diag, off_one, off_two, rhs, sky_mask, flux, sums, lower, lower_far, half):
    count, specs, exposures, fibres = diag.shape
    rows = count - 2
    odd = lax.rem(lax.axis_index("wave"), 2)
    is_odd = odd == 1

    def left(part, s):
        return jnp.where(is_odd, near[part, s], far[part, s])

    def right(part, s):
        return jnp.where(is_odd, far[part, s], near[part, s])

    lane = lax.broadcasted_iota(jnp.int32, (exposures, LANES), 1)
    numer = jnp.zeros((exposures, LANES), F32)
    denom = jnp.zeros((exposures, LANES), F32)

    zero = jnp.zeros((exposures, fibres), F32)
    spans = range(specs)

    def step(k, state, d, a, b, far_a):
        inv1, inv2, mult1, y1, y2 = state
        f = far_a * inv2
        upper = a - far_a * mult1
        g = upper * inv1
        pivot = d - f * far_a - g * upper
        y = b - f * y2 - g * y1
        return f, g, y, (recip(pivot), inv1, g, y, y1)

    def put(k, s, f, g, y, state):
        lower_far[k, s] = f
        lower[k, s] = g
        half[k, s] = y * state[0]

    states = []
    for s in spans:
        state = (zero,) * 5
        f, g, y, state = step(0, state, diag[0, s] + left(0, s), zero, rhs[0, s] + left(3, s), zero)
        put(0, s, f, g, y, state)
        f, g, y, state = step(
            1,
            state,
            diag[1, s] + left(2, s),
            off_one[0, s] + left(1, s),
            rhs[1, s] + left(4, s),
            zero,
        )
        put(1, s, f, g, y, state)
        states.append(state)

    def forward(k, states):
        results = []
        for s in spans:
            f, g, y, state = step(
                k, states[s], diag[k, s], off_one[k - 1, s], rhs[k, s], off_two[k - 2, s]
            )
            put(k, s, f, g, y, state)
            results.append(state)
        return tuple(results)

    states = lax.fori_loop(2, rows, forward, tuple(states), unroll=4)

    after = [None] * specs
    for s in spans:
        f, g, y, state = step(
            rows,
            states[s],
            diag[rows, s] + right(2, s),
            off_one[rows - 1, s],
            rhs[rows, s] + right(4, s),
            off_two[rows - 2, s],
        )
        f1, g1, y1, state1 = step(
            rows + 1,
            state,
            diag[rows + 1, s] + right(0, s),
            off_one[rows, s] + right(1, s),
            rhs[rows + 1, s] + right(3, s),
            off_two[rows - 1, s],
        )
        last = y1 * state1[0]
        here = y * state[0] - g1 * last
        flux[rows - 1, s] = here
        after[s] = (here, last, g, f1, f)

    def total(parts):
        return jnp.sum(parts, axis=1, keepdims=True)

    masks = [sky_mask[s] for s in spans]

    def spread(k, numer, denom, precs, values):
        weighted = sum(masks[s] * precs[s] for s in spans)
        valued = sum(masks[s] * precs[s] * values[s] for s in spans)
        return (
            jnp.where(lane == k, total(valued), numer),
            jnp.where(lane == k, total(weighted), denom),
        )

    precs = [diag[rows, s] + right(5, s) for s in spans]
    numer, denom = spread(rows - 1, numer, denom, precs, [after[s][0] for s in spans])

    def backward(step_row, carry):
        k = rows - 1 - step_row
        numer, denom, after = carry
        results = []
        for s in spans:
            x1, x2, g1, f2, f1 = after[s]
            value = half[k, s] - g1 * x1 - f2 * x2
            flux[k - 1, s] = value
            results.append((value, x1, lower[k, s], f1, lower_far[k, s]))
        precs = [diag[k, s] for s in spans]
        numer, denom = spread(k - 1, numer, denom, precs, [r[0] for r in results])
        return (numer, denom, tuple(results))

    numer, denom, after = lax.fori_loop(0, rows - 2, backward, (numer, denom, tuple(after)), unroll=4)
    values = []
    for s in spans:
        x1, x2, g1, f2, f1 = after[s]
        value = half[1, s] - g1 * x1 - f2 * x2
        flux[0, s] = value
        values.append(value)
    precs = [diag[1, s] + left(5, s) for s in spans]
    numer, denom = spread(0, numer, denom, precs, values)
    sums[0] = numer
    sums[1] = denom


def solve_call(near, far, bands):
    count, specs, exposures, fibres = bands[0].shape
    rows = count - 2
    scratch = pltpu.VMEM((count, specs, exposures, fibres), F32)
    return pl.pallas_call(
        solve_kernel,
        out_shape=(in_vmem((rows, specs, exposures, fibres)), in_vmem((2, exposures, LANES))),
        in_specs=[VM] * 7,
        out_specs=(VM, VM),
        scratch_shapes=[scratch] * 3,
        compiler_params=pltpu.CompilerParams(vmem_limit_bytes=24 * 2**20),
        cost_estimate=pl.CostEstimate(flops=10**7, bytes_accessed=10**7, transcendentals=0),
        name="solve",
    )(near, far, *bands)


def position_of(index, total_rows):
    return 2.0 * index.astype(F32) / (total_rows - 1) - 1.0


def regress_kernel(total_rows, flux, other, sums, regress, sky_out):
    rows, specs, exposures, fibres = flux.shape
    device = lax.axis_index("wave")
    lane = lax.broadcasted_iota(jnp.int32, (exposures, LANES), 1)
    valid = lane < rows
    first = [[jnp.zeros((exposures, fibres), F32) for _ in range(specs)] for _ in range(2)]
    moments = [jnp.zeros((exposures, 1), F32) for _ in range(3)]
    for which, (ref, base) in enumerate(((flux, device * rows), (other, (device - 1) * rows))):
        sky = jnp.where(valid, sums[2 * which] / jnp.where(valid, sums[2 * which + 1], 1.0), 0.0)
        position = position_of(base + lane, total_rows)
        tilted = sky * position
        moments[0] += jnp.sum(sky * sky, axis=1, keepdims=True)
        moments[1] += jnp.sum(sky * tilted, axis=1, keepdims=True)
        moments[2] += jnp.sum(tilted * tilted, axis=1, keepdims=True)
        if which == 0:
            sky_out[...] = sky
        for k in range(rows):
            plain_k = jnp.broadcast_to(sky[:, k : k + 1], (exposures, fibres))
            tilted_k = jnp.broadcast_to(tilted[:, k : k + 1], (exposures, fibres))
            for s in range(specs):
                values = ref[k, s]
                first[0][s] += values * plain_k
                first[1][s] += values * tilted_k
    for r in range(2):
        for s in range(specs):
            regress[r * specs + s] = first[r][s]
    wide = lax.broadcasted_iota(jnp.int32, (exposures, fibres), 1)
    regress[2 * specs] = jnp.where(wide == 0, moments[0], jnp.where(wide == 1, moments[1], moments[2]))


def regress_call(total_rows, flux, other, sums):
    rows, specs, exposures, fibres = flux.shape
    return pl.pallas_call(
        functools.partial(regress_kernel, total_rows),
        out_shape=(
            in_vmem((2 * specs + 1, exposures, fibres)),
            in_vmem((exposures, LANES)),
        ),
        in_specs=[VM] * 3,
        out_specs=(VM, VM),
        compiler_params=pltpu.CompilerParams(vmem_limit_bytes=24 * 2**20),
        cost_estimate=pl.CostEstimate(flops=10**6, bytes_accessed=10**6, transcendentals=0),
        name="regress",
    )(flux, other, sums)


def clean_kernel(total_rows, flux, sky_ref, mine, sent, out, buf, sems):
    rows, specs, exposures, fibres = flux.shape
    device = lax.axis_index("wave")
    is_odd = lax.rem(device, 2) == 1

    def got(slot):
        return jnp.where(is_odd, mine[slot], sent[slot])

    moments = got(2 * specs)
    upper_left = moments[:, 0:1] + RIDGE
    cross = moments[:, 1:2]
    lower_right = moments[:, 2:3] + RIDGE
    inverse = 1.0 / (upper_left * lower_right - cross * cross)
    slope_a, slope_b = [], []
    for s in range(specs):
        r1, r2 = got(s), got(specs + s)
        slope_a.append((lower_right * r1 - cross * r2) * inverse)
        slope_b.append((upper_left * r2 - cross * r1) * inverse)
    lane = lax.broadcasted_iota(jnp.int32, (exposures, LANES), 1)
    sky = sky_ref[...]
    tilted = sky * position_of(device * rows + lane, total_rows)
    chunks = sems.shape[0]
    size = -(-rows // chunks)
    copies = []
    for c in range(chunks):
        low, high = c * size, min(rows, (c + 1) * size)
        for k in range(low, high):
            plain_k = jnp.broadcast_to(sky[:, k : k + 1], (exposures, fibres))
            tilted_k = jnp.broadcast_to(tilted[:, k : k + 1], (exposures, fibres))
            for s in range(specs):
                buf[k, s] = flux[k, s] - (slope_a[s] * plain_k + slope_b[s] * tilted_k)
        for e in range(exposures):
            copy = pltpu.make_async_copy(
                buf.at[low:high, :, e], out.at[e, low:high], sems.at[c, e]
            )
            copy.start()
            copies.append(copy)
    for copy in copies:
        copy.wait()


def clean_call(total_rows, flux, sky, mine, sent):
    rows, specs, exposures, fibres = flux.shape
    return pl.pallas_call(
        functools.partial(clean_kernel, total_rows),
        out_shape=jax.ShapeDtypeStruct((exposures, rows, specs, fibres), F32),
        in_specs=[VM] * 4,
        out_specs=HB,
        scratch_shapes=[
            pltpu.VMEM((rows, specs, exposures, fibres), F32),
            pltpu.SemaphoreType.DMA((2, exposures)),
        ],
        compiler_params=pltpu.CompilerParams(vmem_limit_bytes=24 * 2**20),
        cost_estimate=pl.CostEstimate(flops=10**6, bytes_accessed=10**6, transcendentals=0),
        name="clean",
    )(flux, sky, mine, sent)


def powers(low, high):
    steps = []
    while low < high:
        steps.append(low)
        low *= 2
    return steps


def local(pixels, ivar, mask, psf_left, psf_right, sky_index):
    arrays = [jnp.transpose(x, (0, 2, 1, 3)) for x in (pixels, ivar, mask, psf_left, psf_right)]
    rows = pixels.shape[2]
    wave, spec = lax.axis_size("wave"), lax.axis_size("spec")
    total_rows = rows * wave
    near, far, *bands = prepare_call(arrays, sky_index)
    far = lax.ppermute(
        far, "wave", [pair for i in range(1, wave - 1, 2) for pair in ((i, i + 1), (i + 1, i))]
    )
    near = lax.ppermute(near, "wave", [(i, i ^ 1) for i in range(wave)])
    flux, sums = solve_call(near, far, bands)
    to_odd = [(i, i + 1) for i in range(0, wave, 2)]
    got = lax.ppermute(sums, "wave", to_odd)
    flux, got = lax.optimization_barrier((flux, got))
    other = lax.ppermute(flux, "wave", to_odd)
    sums = jnp.concatenate([sums, got])
    for k in powers(1, spec):
        sums = sums + lax.ppermute(sums, "spec", [(i, i ^ k) for i in range(spec)])
    regress, sky = regress_call(total_rows, flux, other, sums)
    for k in powers(2, wave):
        regress = regress + lax.ppermute(regress, "wave", [(i, i ^ k) for i in range(1, wave, 2)])
    sent = lax.ppermute(regress, "wave", [(i + 1, i) for i in range(0, wave, 2)])
    cleaned = clean_call(total_rows, flux, sky, regress, sent)
    return (jnp.transpose(cleaned, (0, 2, 1, 3)), sky[:, :rows])


def solution(mesh):
    block = P(None, "spec", "wave", None)
    return jax.shard_map(
        local,
        mesh=mesh,
        in_specs=(block,) * 5 + (P("spec", None),),
        out_specs=(block, P(None, "wave")),
        check_vma=False,
    )
```

```python
import functools

import jax
import jax.numpy as jnp
from jax import lax
from jax.experimental import pallas as pl
from jax.experimental.pallas import tpu as pltpu
from jax.sharding import PartitionSpec as P

REG = 0.05
RIDGE = 1.0
HALO = 4
PARTS = 6
LANES = 128

F32 = jnp.float32
VM = pl.BlockSpec(memory_space=pltpu.VMEM)
SM = pl.BlockSpec(memory_space=pltpu.SMEM)
HB = pl.BlockSpec(memory_space=pltpu.HBM)


def in_vmem(shape, dtype=F32):
    return jax.ShapeDtypeStruct(shape, dtype)


def recip(values):
    return 1.0 / values


def weight_of(ivar, mask):
    return jnp.where(mask == 0, ivar, 0.0)


def edge_message(p, w, l, r):
    wl = [a * b for a, b in zip(w, l)]
    wr = [a * b for a, b in zip(w, r)]
    d0 = w[0] + wl[1] * l[1] + REG
    d1 = w[1] + wr[0] * r[0] + wl[2] * l[2] + REG
    d2 = w[2] + wr[1] * r[1] + wl[3] * l[3] + REG
    d3 = w[3] + wr[2] * r[2]
    d4 = wr[3] * r[3]
    raw = d4
    a01 = wr[0] + wl[1]
    a12 = wr[1] + wl[2]
    a23 = wr[2] + wl[3]
    a34 = wr[3]
    a02 = wl[1] * r[1]
    a13 = wl[2] * r[2]
    a24 = wl[3] * r[3]
    b0 = w[0] * p[0] + wl[1] * p[1]
    b1 = w[1] * p[1] + wr[0] * p[0] + wl[2] * p[2]
    b2 = w[2] * p[2] + wr[1] * p[1] + wl[3] * p[3]
    b3 = w[3] * p[3] + wr[2] * p[2]
    b4 = wr[3] * p[3]
    inv = recip(d0)
    near, far = a01 * inv, a02 * inv
    d1, a12, d2 = d1 - near * a01, a12 - near * a02, d2 - far * a02
    b1, b2 = b1 - near * b0, b2 - far * b0
    inv = recip(d1)
    near, far = a12 * inv, a13 * inv
    d2, a23, d3 = d2 - near * a12, a23 - near * a13, d3 - far * a13
    b2, b3 = b2 - near * b1, b3 - far * b1
    inv = recip(d2)
    near, far = a23 * inv, a24 * inv
    d3, a34, d4 = d3 - near * a23, a34 - near * a24, d4 - far * a24
    b3, b4 = b3 - near * b2, b4 - far * b2
    return (d3, a34, d4, b3, b4, raw)


def edge_kernel(pix, iva, msk, lef, rig, near_out, far_out, bufs, mbuf, sems):
    exposures, rows, specs, fibres = pix.shape
    odd = lax.rem(lax.axis_index("wave"), 2) == 1
    for end, start in enumerate((0, rows - HALO)):
        for e in range(exposures):
            for slot, ref in enumerate((pix, iva, lef, rig)):
                pltpu.make_async_copy(
                    ref.at[e, start : start + HALO], bufs.at[end, slot, :, :, e], sems.at[0, end]
                ).start()
            pltpu.make_async_copy(
                msk.at[e, start : start + HALO], mbuf.at[end, :, :, e], sems.at[1, end]
            ).start()
    for end in range(2):
        pltpu.make_async_copy(bufs.at[end], bufs.at[end], sems.at[0, end]).wait()
        pltpu.make_async_copy(mbuf.at[end], mbuf.at[end], sems.at[1, end]).wait()
        order = range(HALO - 1, -1, -1) if end == 0 else range(HALO)
        for s in range(specs):
            p = [bufs[end, 0, k, s] for k in order]
            w = [weight_of(bufs[end, 1, k, s], mbuf[end, k, s]) for k in order]
            l = [bufs[end, 2, k, s] for k in order]
            r = [bufs[end, 3, k, s] for k in order]
            if end == 0:
                for slot, value in enumerate(edge_message(p, w, r, l)):
                    near_out[slot, s] = value
                continue
            for slot, value in enumerate(edge_message(p, w, l, r)):
                top = near_out[slot, s]
                near_out[slot, s] = jnp.where(odd, top, value)
                far_out[slot, s] = jnp.where(odd, value, top)


def edge_call(arrays):
    exposures, rows, specs, fibres = arrays[0].shape
    message = in_vmem((PARTS, specs, exposures, fibres))
    return pl.pallas_call(
        edge_kernel,
        out_shape=(message, message),
        in_specs=[HB] * 5,
        out_specs=(VM, VM),
        scratch_shapes=[
            pltpu.VMEM((2, 4, HALO, specs, exposures, fibres), F32),
            pltpu.VMEM((2, HALO, specs, exposures, fibres), jnp.int32),
            pltpu.SemaphoreType.DMA((2, 2)),
        ],
        compiler_params=pltpu.CompilerParams(vmem_limit_bytes=8 * 2**20),
        cost_estimate=pl.CostEstimate(flops=10**6, bytes_accessed=10**6, transcendentals=0),
        name="edges",
    )(*arrays)


def prepare_kernel(
    chunks, pix, iva, msk, lef, rig, sky_index, diag, off_one, off_two, rhs, sky_mask, bufs, mbuf, sems
):
    exposures, rows, specs, fibres = pix.shape
    bounds = [rows * c // chunks for c in range(chunks + 1)]
    for c in range(chunks):
        low, high = bounds[c], bounds[c + 1]
        for e in range(exposures):
            for slot, ref in enumerate((pix, iva, lef, rig)):
                pltpu.make_async_copy(
                    ref.at[e, low:high], bufs.at[slot, low:high, :, e], sems.at[0, c]
                ).start()
            pltpu.make_async_copy(
                msk.at[e, low:high], mbuf.at[low:high, :, e], sems.at[1, c]
            ).start()
    lane = lax.broadcasted_iota(jnp.int32, (exposures, fibres), 1)
    for s in range(specs):
        found = lane == sky_index[s, 0]
        for k in range(1, sky_index.shape[1]):
            found = found | (lane == sky_index[s, k])
        sky_mask[s] = jnp.where(found, 1.0, 0.0)

    def row(k, s, carry):
        w1, wp1, wr1, wrr2, wrp2, wrr1, wrp1 = carry
        p, w, l, r = bufs[0, k, s], weight_of(bufs[1, k, s], mbuf[k, s]), bufs[2, k, s], bufs[3, k, s]
        wl, wr, wp = w * l, w * r, w * p
        diag[k, s] = w1 + wl * l + (wrr2 + REG)
        off_one[k, s] = wr1 + wl
        off_two[k, s] = wl * r
        rhs[k, s] = wp1 + wl * p + wrp2
        return (w, wp, wr, wrr1, wrp1, wr * r, wr * p)

    carries = [(0.0,) * 7 for _ in range(specs)]
    for c in range(chunks):
        low, high = bounds[c], bounds[c + 1]
        part, mpart = bufs.at[:, low:high], mbuf.at[low:high]
        pltpu.make_async_copy(part, part, sems.at[0, c]).wait()
        pltpu.make_async_copy(mpart, mpart, sems.at[1, c]).wait()
        for s in range(specs):
            for k in range(low, high):
                carries[s] = row(k, s, carries[s])
    for s in range(specs):
        w1, wp1, wr1, wrr2, wrp2, wrr1, wrp1 = carries[s]
        diag[rows, s] = w1 + (wrr2 + REG)
        off_one[rows, s] = wr1
        rhs[rows, s] = wp1 + wrp2
        diag[rows + 1, s] = wrr1 + REG
        rhs[rows + 1, s] = wrp1


def prepare_call(arrays, sky_index):
    exposures, rows, specs, fibres = arrays[0].shape
    chunks = 5
    grown = in_vmem((rows + 2, specs, exposures, fibres))
    return pl.pallas_call(
        functools.partial(prepare_kernel, chunks),
        out_shape=(grown, grown, grown, grown, in_vmem((specs, exposures, fibres))),
        in_specs=[HB] * 5 + [SM],
        out_specs=(VM,) * 5,
        scratch_shapes=[
            pltpu.VMEM((4, rows, specs, exposures, fibres), F32),
            pltpu.VMEM((rows, specs, exposures, fibres), jnp.int32),
            pltpu.SemaphoreType.DMA((2, chunks)),
        ],
        compiler_params=pltpu.CompilerParams(vmem_limit_bytes=24 * 2**20),
        cost_estimate=pl.CostEstimate(flops=10**7, bytes_accessed=10**7, transcendentals=0),
        name="prepare",
    )(*arrays, sky_index)


def solve_kernel(wave, near, far, diag, off_one, off_two, rhs, sky_mask, flux, sums, lower, lower_far, half):
    count, specs, exposures, fibres = diag.shape
    rows = count - 2
    device = lax.axis_index("wave")
    is_odd = lax.rem(device, 2) == 1
    at_end = (device == 0) | (device == wave - 1)

    def from_far(part, s):
        return jnp.where(at_end, 0.0, far[part, s])

    def left(part, s):
        return jnp.where(is_odd, near[part, s], from_far(part, s))

    def right(part, s):
        return jnp.where(is_odd, from_far(part, s), near[part, s])

    lane = lax.broadcasted_iota(jnp.int32, (exposures, LANES), 1)
    numer = jnp.zeros((exposures, LANES), F32)
    denom = jnp.zeros((exposures, LANES), F32)

    zero = jnp.zeros((exposures, fibres), F32)
    spans = range(specs)

    def step(k, state, d, a, b, far_a):
        inv1, inv2, mult1, y1, y2 = state
        f = far_a * inv2
        upper = a - far_a * mult1
        g = upper * inv1
        pivot = d - f * far_a - g * upper
        y = b - f * y2 - g * y1
        return f, g, y, (recip(pivot), inv1, g, y, y1)

    def put(k, s, f, g, y, state):
        lower_far[k, s] = f
        lower[k, s] = g
        half[k, s] = y * state[0]

    states = []
    for s in spans:
        state = (zero,) * 5
        f, g, y, state = step(0, state, diag[0, s] + left(0, s), zero, rhs[0, s] + left(3, s), zero)
        put(0, s, f, g, y, state)
        f, g, y, state = step(
            1,
            state,
            diag[1, s] + left(2, s),
            off_one[0, s] + left(1, s),
            rhs[1, s] + left(4, s),
            zero,
        )
        put(1, s, f, g, y, state)
        states.append(state)

    def forward(k, states):
        results = []
        for s in spans:
            f, g, y, state = step(
                k, states[s], diag[k, s], off_one[k - 1, s], rhs[k, s], off_two[k - 2, s]
            )
            put(k, s, f, g, y, state)
            results.append(state)
        return tuple(results)

    states = lax.fori_loop(2, rows, forward, tuple(states), unroll=4)

    after = [None] * specs
    for s in spans:
        f, g, y, state = step(
            rows,
            states[s],
            diag[rows, s] + right(2, s),
            off_one[rows - 1, s],
            rhs[rows, s] + right(4, s),
            off_two[rows - 2, s],
        )
        f1, g1, y1, state1 = step(
            rows + 1,
            state,
            diag[rows + 1, s] + right(0, s),
            off_one[rows, s] + right(1, s),
            rhs[rows + 1, s] + right(3, s),
            off_two[rows - 1, s],
        )
        last = y1 * state1[0]
        here = y * state[0] - g1 * last
        flux[rows - 1, s] = here
        after[s] = (here, last, g, f1, f)

    def total(parts):
        return jnp.sum(parts, axis=1, keepdims=True)

    masks = [sky_mask[s] for s in spans]

    def spread(k, numer, denom, precs, values):
        weighted = sum(masks[s] * precs[s] for s in spans)
        valued = sum(masks[s] * precs[s] * values[s] for s in spans)
        return (
            jnp.where(lane == k, total(valued), numer),
            jnp.where(lane == k, total(weighted), denom),
        )

    precs = [diag[rows, s] + right(5, s) for s in spans]
    numer, denom = spread(rows - 1, numer, denom, precs, [after[s][0] for s in spans])

    def backward(step_row, carry):
        k = rows - 1 - step_row
        numer, denom, after = carry
        results = []
        for s in spans:
            x1, x2, g1, f2, f1 = after[s]
            value = half[k, s] - g1 * x1 - f2 * x2
            flux[k - 1, s] = value
            results.append((value, x1, lower[k, s], f1, lower_far[k, s]))
        precs = [diag[k, s] for s in spans]
        numer, denom = spread(k - 1, numer, denom, precs, [r[0] for r in results])
        return (numer, denom, tuple(results))

    numer, denom, after = lax.fori_loop(0, rows - 2, backward, (numer, denom, tuple(after)), unroll=4)
    values = []
    for s in spans:
        x1, x2, g1, f2, f1 = after[s]
        value = half[1, s] - g1 * x1 - f2 * x2
        flux[0, s] = value
        values.append(value)
    precs = [diag[1, s] + left(5, s) for s in spans]
    numer, denom = spread(0, numer, denom, precs, values)
    sums[0] = numer
    sums[1] = denom


def solve_call(wave, near, far, bands):
    count, specs, exposures, fibres = bands[0].shape
    rows = count - 2
    scratch = pltpu.VMEM((count, specs, exposures, fibres), F32)
    return pl.pallas_call(
        functools.partial(solve_kernel, wave),
        out_shape=(in_vmem((rows, specs, exposures, fibres)), in_vmem((2, exposures, LANES))),
        in_specs=[VM] * 7,
        out_specs=(VM, VM),
        scratch_shapes=[scratch] * 3,
        compiler_params=pltpu.CompilerParams(vmem_limit_bytes=24 * 2**20),
        cost_estimate=pl.CostEstimate(flops=10**7, bytes_accessed=10**7, transcendentals=0),
        name="solve",
    )(near, far, *bands)


def position_of(index, total_rows):
    return 2.0 * index.astype(F32) / (total_rows - 1) - 1.0


def regress_kernel(total_rows, flux, other, sums, regress, sky_out, sky_copy):
    rows, specs, exposures, fibres = flux.shape
    device = lax.axis_index("wave")
    partner = device + 1 - 2 * lax.rem(device, 2)
    lane = lax.broadcasted_iota(jnp.int32, (exposures, LANES), 1)
    valid = lane < rows
    first = [[jnp.zeros((exposures, fibres), F32) for _ in range(specs)] for _ in range(2)]
    moments = [jnp.zeros((exposures, 1), F32) for _ in range(3)]
    for which, (ref, base) in enumerate(((flux, device * rows), (other, partner * rows))):
        sky = jnp.where(valid, sums[2 * which] / jnp.where(valid, sums[2 * which + 1], 1.0), 0.0)
        position = position_of(base + lane, total_rows)
        tilted = sky * position
        moments[0] += jnp.sum(sky * sky, axis=1, keepdims=True)
        moments[1] += jnp.sum(sky * tilted, axis=1, keepdims=True)
        moments[2] += jnp.sum(tilted * tilted, axis=1, keepdims=True)
        if which == 0:
            sky_out[...] = sky
            sky_copy[...] = sky
        for k in range(rows):
            plain_k = jnp.broadcast_to(sky[:, k : k + 1], (exposures, fibres))
            tilted_k = jnp.broadcast_to(tilted[:, k : k + 1], (exposures, fibres))
            for s in range(specs):
                values = ref[k, s]
                first[0][s] += values * plain_k
                first[1][s] += values * tilted_k
    for r in range(2):
        for s in range(specs):
            regress[r * specs + s] = first[r][s]
    wide = lax.broadcasted_iota(jnp.int32, (exposures, fibres), 1)
    regress[2 * specs] = jnp.where(wide == 0, moments[0], jnp.where(wide == 1, moments[1], moments[2]))


def regress_call(total_rows, flux, other, sums):
    rows, specs, exposures, fibres = flux.shape
    return pl.pallas_call(
        functools.partial(regress_kernel, total_rows),
        out_shape=(
            in_vmem((2 * specs + 1, exposures, fibres)),
            in_vmem((exposures, LANES)),
            in_vmem((exposures, LANES)),
        ),
        in_specs=[VM] * 3,
        out_specs=(VM, VM, VM),
        compiler_params=pltpu.CompilerParams(vmem_limit_bytes=24 * 2**20),
        cost_estimate=pl.CostEstimate(flops=10**6, bytes_accessed=10**6, transcendentals=0),
        name="regress",
    )(flux, other, sums)


def clean_kernel(total_rows, flux, sky_ref, mine, sent, out, buf, sems):
    rows, specs, exposures, fibres = flux.shape
    device = lax.axis_index("wave")
    is_odd = lax.rem(device, 2) == 1

    def got(slot):
        return jnp.where(is_odd, mine[slot], sent[slot])

    moments = got(2 * specs)
    upper_left = moments[:, 0:1] + RIDGE
    cross = moments[:, 1:2]
    lower_right = moments[:, 2:3] + RIDGE
    inverse = 1.0 / (upper_left * lower_right - cross * cross)
    slope_a, slope_b = [], []
    for s in range(specs):
        r1, r2 = got(s), got(specs + s)
        slope_a.append((lower_right * r1 - cross * r2) * inverse)
        slope_b.append((upper_left * r2 - cross * r1) * inverse)
    lane = lax.broadcasted_iota(jnp.int32, (exposures, LANES), 1)
    sky = sky_ref[...]
    tilted = sky * position_of(device * rows + lane, total_rows)
    chunks = sems.shape[0]
    bounds = [rows * c // chunks for c in range(chunks + 1)]
    for c in range(chunks):
        low, high = bounds[c], bounds[c + 1]
        for k in range(low, high):
            plain_k = jnp.broadcast_to(sky[:, k : k + 1], (exposures, fibres))
            tilted_k = jnp.broadcast_to(tilted[:, k : k + 1], (exposures, fibres))
            for s in range(specs):
                buf[k, s] = flux[k, s] - (slope_a[s] * plain_k + slope_b[s] * tilted_k)
        for e in range(exposures):
            pltpu.make_async_copy(
                buf.at[low:high, :, e], out.at[e, low:high], sems.at[c]
            ).start()
    for c in range(chunks):
        part = buf.at[bounds[c] : bounds[c + 1]]
        pltpu.make_async_copy(part, part, sems.at[c]).wait()


def clean_call(total_rows, flux, sky, mine, sent):
    rows, specs, exposures, fibres = flux.shape
    return pl.pallas_call(
        functools.partial(clean_kernel, total_rows),
        out_shape=jax.ShapeDtypeStruct((exposures, rows, specs, fibres), F32),
        in_specs=[VM] * 4,
        out_specs=HB,
        scratch_shapes=[
            pltpu.VMEM((rows, specs, exposures, fibres), F32),
            pltpu.SemaphoreType.DMA((4,)),
        ],
        compiler_params=pltpu.CompilerParams(vmem_limit_bytes=24 * 2**20),
        cost_estimate=pl.CostEstimate(flops=10**6, bytes_accessed=10**6, transcendentals=0),
        name="clean",
    )(flux, sky, mine, sent)


def powers(low, high):
    steps = []
    while low < high:
        steps.append(low)
        low *= 2
    return steps


def swap(values, partner):
    spec, wave = lax.axis_size("spec"), lax.axis_size("wave")
    pairs = []
    for s in range(spec):
        for i in range(wave):
            t, j = partner(s, i)
            if not 0 <= j < wave:
                t, j = s ^ 1, i
            if t < spec:
                pairs.append((s * wave + i, t * wave + j))
    return lax.ppermute(values, ("spec", "wave"), pairs)


def local(pixels, ivar, mask, psf_left, psf_right, sky_index):
    arrays = [jnp.transpose(x, (0, 2, 1, 3)) for x in (pixels, ivar, mask, psf_left, psf_right)]
    rows = pixels.shape[2]
    wave, spec = lax.axis_size("wave"), lax.axis_size("spec")
    total_rows = rows * wave
    hbm = [pltpu.with_memory_space_constraint(x, pltpu.HBM) for x in arrays]
    near, far = edge_call(hbm)
    far = swap(far, lambda s, i: (s, i + 1 if i % 2 else i - 1))
    near = swap(near, lambda s, i: (s, i ^ 1))
    bands = prepare_call(hbm, sky_index)
    flux, sums = solve_call(wave, near, far, bands)
    got = swap(sums, lambda s, i: (s, i ^ 1))
    flux, got = lax.optimization_barrier((flux, got))
    other = swap(flux, lambda s, i: (s, i ^ 1))
    sums = jnp.concatenate([sums, got])
    for k in powers(1, spec):
        sums = sums + swap(sums, lambda s, i: (s ^ k, i))
    regress, sky, sky_out = regress_call(total_rows, flux, other, sums)
    for k in powers(2, wave):
        regress = regress + swap(regress, lambda s, i: (s, i ^ k if i % 2 else -1))
    sent = swap(regress, lambda s, i: (s, i ^ 1))
    cleaned = clean_call(total_rows, flux, sky, regress, sent)
    return (jnp.transpose(cleaned, (0, 2, 1, 3)), sky_out[:, :rows])


def solution(mesh):
    block = P(None, "spec", "wave", None)
    return jax.shard_map(
        local,
        mesh=mesh,
        in_specs=(block,) * 5 + (P("spec", None),),
        out_specs=(block, P(None, "wave")),
        check_vma=False,
    )
```

```python
import functools

import jax
import jax.numpy as jnp
from jax import lax
from jax.experimental import pallas as pl
from jax.experimental.pallas import tpu as pltpu
from jax.sharding import PartitionSpec as P

REG = 0.05
RIDGE = 1.0
HALO = 4
PARTS = 6
PREFETCH = 3
LANES = 128

F32 = jnp.float32
VM = pl.BlockSpec(memory_space=pltpu.VMEM)
SM = pl.BlockSpec(memory_space=pltpu.SMEM)
HB = pl.BlockSpec(memory_space=pltpu.HBM)


def in_vmem(shape, dtype=F32):
    return jax.ShapeDtypeStruct(shape, dtype)


def recip(values):
    return 1.0 / values


def weight_of(ivar, mask):
    return jnp.where(mask == 0, ivar, 0.0)


def edge_message(p, w, l, r):
    wl = [a * b for a, b in zip(w, l)]
    wr = [a * b for a, b in zip(w, r)]
    d0 = w[0] + wl[1] * l[1] + REG
    d1 = w[1] + wr[0] * r[0] + wl[2] * l[2] + REG
    d2 = w[2] + wr[1] * r[1] + wl[3] * l[3] + REG
    d3 = w[3] + wr[2] * r[2]
    d4 = wr[3] * r[3]
    raw = d4
    a01 = wr[0] + wl[1]
    a12 = wr[1] + wl[2]
    a23 = wr[2] + wl[3]
    a34 = wr[3]
    a02 = wl[1] * r[1]
    a13 = wl[2] * r[2]
    a24 = wl[3] * r[3]
    b0 = w[0] * p[0] + wl[1] * p[1]
    b1 = w[1] * p[1] + wr[0] * p[0] + wl[2] * p[2]
    b2 = w[2] * p[2] + wr[1] * p[1] + wl[3] * p[3]
    b3 = w[3] * p[3] + wr[2] * p[2]
    b4 = wr[3] * p[3]
    inv = recip(d0)
    near, far = a01 * inv, a02 * inv
    d1, a12, d2 = d1 - near * a01, a12 - near * a02, d2 - far * a02
    b1, b2 = b1 - near * b0, b2 - far * b0
    inv = recip(d1)
    near, far = a12 * inv, a13 * inv
    d2, a23, d3 = d2 - near * a12, a23 - near * a13, d3 - far * a13
    b2, b3 = b2 - near * b1, b3 - far * b1
    inv = recip(d2)
    near, far = a23 * inv, a24 * inv
    d3, a34, d4 = d3 - near * a23, a34 - near * a24, d4 - far * a24
    b3, b4 = b3 - near * b2, b4 - far * b2
    return (d3, a34, d4, b3, b4, raw)


def edge_kernel(pix, iva, msk, lef, rig, near_out, far_out, bufs, mbuf, sems):
    exposures, rows, specs, fibres = pix.shape
    odd = lax.rem(lax.axis_index("wave"), 2) == 1
    for end, start in enumerate((0, rows - HALO)):
        for e in range(exposures):
            for slot, ref in enumerate((pix, iva, lef, rig)):
                pltpu.make_async_copy(
                    ref.at[e, start : start + HALO], bufs.at[end, slot, :, :, e], sems.at[0, end]
                ).start()
            pltpu.make_async_copy(
                msk.at[e, start : start + HALO], mbuf.at[end, :, :, e], sems.at[1, end]
            ).start()
    for end in range(2):
        pltpu.make_async_copy(bufs.at[end], bufs.at[end], sems.at[0, end]).wait()
        pltpu.make_async_copy(mbuf.at[end], mbuf.at[end], sems.at[1, end]).wait()
        order = range(HALO - 1, -1, -1) if end == 0 else range(HALO)
        for s in range(specs):
            p = [bufs[end, 0, k, s] for k in order]
            w = [weight_of(bufs[end, 1, k, s], mbuf[end, k, s]) for k in order]
            l = [bufs[end, 2, k, s] for k in order]
            r = [bufs[end, 3, k, s] for k in order]
            if end == 0:
                for slot, value in enumerate(edge_message(p, w, r, l)):
                    near_out[slot, s] = value
                continue
            for slot, value in enumerate(edge_message(p, w, l, r)):
                top = near_out[slot, s]
                near_out[slot, s] = jnp.where(odd, top, value)
                far_out[slot, s] = jnp.where(odd, value, top)


def edge_call(arrays):
    exposures, rows, specs, fibres = arrays[0].shape
    message = in_vmem((PARTS, specs, exposures, fibres))
    return pl.pallas_call(
        edge_kernel,
        out_shape=(message, message),
        in_specs=[HB] * 5,
        out_specs=(VM, VM),
        scratch_shapes=[
            pltpu.VMEM((2, 4, HALO, specs, exposures, fibres), F32),
            pltpu.VMEM((2, HALO, specs, exposures, fibres), jnp.int32),
            pltpu.SemaphoreType.DMA((2, 2)),
        ],
        compiler_params=pltpu.CompilerParams(vmem_limit_bytes=8 * 2**20),
        cost_estimate=pl.CostEstimate(flops=10**6, bytes_accessed=10**6, transcendentals=0),
        name="edges",
    )(*arrays)


def prepare_kernel(
    chunks, pix, iva, msk, lef, rig, sky_index, diag, off_one, off_two, rhs, shares, sky_mask, denom, bufs, mbuf, sems
):
    exposures, rows, specs, fibres = pix.shape
    bounds = [rows * c // chunks for c in range(chunks + 1)]
    for c in range(chunks):
        low, high = bounds[c], bounds[c + 1]
        for e in range(exposures):
            for slot, ref in enumerate((pix, iva, lef, rig)):
                pltpu.make_async_copy(
                    ref.at[e, low:high], bufs.at[slot, low:high, :, e], sems.at[0, c]
                ).start()
            pltpu.make_async_copy(
                msk.at[e, low:high], mbuf.at[low:high, :, e], sems.at[1, c]
            ).start()
    lane = lax.broadcasted_iota(jnp.int32, (exposures, fibres), 1)
    for s in range(specs):
        found = lane == sky_index[s, 0]
        for k in range(1, sky_index.shape[1]):
            found = found | (lane == sky_index[s, k])
        sky_mask[s] = jnp.where(found, 1.0, 0.0)

    spot = lax.broadcasted_iota(jnp.int32, (exposures, LANES), 1)

    def share(k, s, value, total):
        part = sky_mask[s] * value
        shares[k, s] = part
        return jnp.where(spot == k, total + jnp.sum(part, axis=1, keepdims=True), total)

    def row(k, s, carry, total):
        w1, wp1, wr1, wrr2, wrp2, wrr1, wrp1 = carry
        p, w, l, r = bufs[0, k, s], weight_of(bufs[1, k, s], mbuf[k, s]), bufs[2, k, s], bufs[3, k, s]
        wl, wr, wp = w * l, w * r, w * p
        here = w1 + wl * l + (wrr2 + REG)
        diag[k, s] = here
        if k > 0:
            total = share(k - 1, s, here, total)
        off_one[k, s] = wr1 + wl
        off_two[k, s] = wl * r
        rhs[k, s] = wp1 + wl * p + wrp2
        return (w, wp, wr, wrr1, wrp1, wr * r, wr * p), total

    carries = [(0.0,) * 7 for _ in range(specs)]
    total = jnp.zeros((exposures, LANES), F32)
    for c in range(chunks):
        low, high = bounds[c], bounds[c + 1]
        part, mpart = bufs.at[:, low:high], mbuf.at[low:high]
        pltpu.make_async_copy(part, part, sems.at[0, c]).wait()
        pltpu.make_async_copy(mpart, mpart, sems.at[1, c]).wait()
        for s in range(specs):
            for k in range(low, high):
                carries[s], total = row(k, s, carries[s], total)
    for s in range(specs):
        w1, wp1, wr1, wrr2, wrp2, wrr1, wrp1 = carries[s]
        here = w1 + (wrr2 + REG)
        diag[rows, s] = here
        total = share(rows - 1, s, here, total)
        off_one[rows, s] = wr1
        rhs[rows, s] = wp1 + wrp2
        diag[rows + 1, s] = wrr1 + REG
        rhs[rows + 1, s] = wrp1
    denom[...] = total


def prepare_call(arrays, sky_index):
    exposures, rows, specs, fibres = arrays[0].shape
    chunks = 5
    grown = in_vmem((rows + 2, specs, exposures, fibres))
    return pl.pallas_call(
        functools.partial(prepare_kernel, chunks),
        out_shape=(
            grown,
            grown,
            grown,
            grown,
            in_vmem((rows, specs, exposures, fibres)),
            in_vmem((specs, exposures, fibres)),
            in_vmem((exposures, LANES)),
        ),
        in_specs=[pl.BlockSpec(memory_space=pl.ANY)] * 5 + [SM],
        out_specs=(VM,) * 7,
        scratch_shapes=[
            pltpu.VMEM((4, rows, specs, exposures, fibres), F32),
            pltpu.VMEM((rows, specs, exposures, fibres), jnp.int32),
            pltpu.SemaphoreType.DMA((2, chunks)),
        ],
        compiler_params=pltpu.CompilerParams(vmem_limit_bytes=24 * 2**20),
        cost_estimate=pl.CostEstimate(flops=10**7, bytes_accessed=10**7, transcendentals=0),
        name="prepare",
    )(*arrays, sky_index)


def solve_kernel(
    wave, near, far, diag, off_one, off_two, rhs, shares, sky_mask, denom, flux, sums, lower, lower_far, half
):
    count, specs, exposures, fibres = diag.shape
    rows = count - 2
    device = lax.axis_index("wave")
    is_odd = lax.rem(device, 2) == 1
    at_end = (device == 0) | (device == wave - 1)

    def from_far(part, s):
        return jnp.where(at_end, 0.0, far[part, s])

    def left(part, s):
        return jnp.where(is_odd, near[part, s], from_far(part, s))

    def right(part, s):
        return jnp.where(is_odd, from_far(part, s), near[part, s])

    lane = lax.broadcasted_iota(jnp.int32, (exposures, LANES), 1)
    numer = jnp.zeros((exposures, LANES), F32)

    zero = jnp.zeros((exposures, fibres), F32)
    spans = range(specs)

    def step(k, state, d, a, b, far_a):
        inv1, inv2, mult1, y1, y2 = state
        f = far_a * inv2
        upper = a - far_a * mult1
        g = upper * inv1
        pivot = d - f * far_a - g * upper
        y = b - f * y2 - g * y1
        return f, g, y, (recip(pivot), inv1, g, y, y1)

    def put(k, s, f, g, y, state):
        lower_far[k, s] = f
        lower[k, s] = g
        half[k, s] = y * state[0]

    states = []
    for s in spans:
        state = (zero,) * 5
        f, g, y, state = step(0, state, diag[0, s] + left(0, s), zero, rhs[0, s] + left(3, s), zero)
        put(0, s, f, g, y, state)
        f, g, y, state = step(
            1,
            state,
            diag[1, s] + left(2, s),
            off_one[0, s] + left(1, s),
            rhs[1, s] + left(4, s),
            zero,
        )
        put(1, s, f, g, y, state)
        states.append(state)

    def forward(k, states):
        results = []
        for s in spans:
            f, g, y, state = step(
                k, states[s], diag[k, s], off_one[k - 1, s], rhs[k, s], off_two[k - 2, s]
            )
            put(k, s, f, g, y, state)
            results.append(state)
        return tuple(results)

    states = lax.fori_loop(2, rows, forward, tuple(states), unroll=4)

    after = [None] * specs
    for s in spans:
        f, g, y, state = step(
            rows,
            states[s],
            diag[rows, s] + right(2, s),
            off_one[rows - 1, s],
            rhs[rows, s] + right(4, s),
            off_two[rows - 2, s],
        )
        f1, g1, y1, state1 = step(
            rows + 1,
            state,
            diag[rows + 1, s] + right(0, s),
            off_one[rows, s] + right(1, s),
            rhs[rows + 1, s] + right(3, s),
            off_two[rows - 1, s],
        )
        last = y1 * state1[0]
        here = y * state[0] - g1 * last
        flux[rows - 1, s] = here
        after[s] = (here, last, g, f1, f)

    def total(parts):
        return jnp.sum(parts, axis=1, keepdims=True)

    def spread(k, numer, parts, values):
        return jnp.where(lane == k, total(sum(parts[s] * values[s] for s in spans)), numer)

    extra = [sky_mask[s] * right(5, s) for s in spans]
    parts = [shares[rows - 1, s] + extra[s] for s in spans]
    numer = spread(rows - 1, numer, parts, [after[s][0] for s in spans])
    weights = denom[...] + jnp.where(lane == rows - 1, total(sum(extra)), 0.0)

    def backward(step_row, carry):
        k = rows - 1 - step_row
        numer, after = carry
        results = []
        for s in spans:
            x1, x2, g1, f2, f1 = after[s]
            value = half[k, s] - g1 * x1 - f2 * x2
            flux[k - 1, s] = value
            results.append((value, x1, lower[k, s], f1, lower_far[k, s]))
        parts = [shares[k - 1, s] for s in spans]
        return (spread(k - 1, numer, parts, [r[0] for r in results]), tuple(results))

    numer, after = lax.fori_loop(0, rows - 2, backward, (numer, tuple(after)), unroll=4)
    values = []
    for s in spans:
        x1, x2, g1, f2, f1 = after[s]
        value = half[1, s] - g1 * x1 - f2 * x2
        flux[0, s] = value
        values.append(value)
    extra = [sky_mask[s] * left(5, s) for s in spans]
    parts = [shares[0, s] + extra[s] for s in spans]
    sums[0] = spread(0, numer, parts, values)
    sums[1] = weights + jnp.where(lane == 0, total(sum(extra)), 0.0)


def solve_call(wave, near, far, bands):
    count, specs, exposures, fibres = bands[0].shape
    rows = count - 2
    scratch = pltpu.VMEM((count, specs, exposures, fibres), F32)
    return pl.pallas_call(
        functools.partial(solve_kernel, wave),
        out_shape=(in_vmem((rows, specs, exposures, fibres)), in_vmem((2, exposures, LANES))),
        in_specs=[VM] * 9,
        out_specs=(VM, VM),
        scratch_shapes=[scratch] * 3,
        compiler_params=pltpu.CompilerParams(vmem_limit_bytes=24 * 2**20),
        cost_estimate=pl.CostEstimate(flops=10**7, bytes_accessed=10**7, transcendentals=0),
        name="solve",
    )(near, far, *bands)


def position_of(index, total_rows):
    return 2.0 * jnp.asarray(index).astype(F32) / (total_rows - 1) - 1.0


def regress_kernel(total_rows, flux, other, sums, regress, sky_out, sky_copy):
    rows, specs, exposures, fibres = flux.shape
    lanes = regress.shape[2]
    device = lax.axis_index("wave")
    partner = device + 1 - 2 * lax.rem(device, 2)
    lane = lax.broadcasted_iota(jnp.int32, (exposures, LANES), 1)
    valid = lane < rows
    step = 2.0 / (total_rows - 1)
    plain = [0.0] * specs
    tilted = [0.0] * specs
    moments = [0.0] * 3
    for which, (ref, owner) in enumerate(((flux, device), (other, partner))):
        sky = jnp.where(valid, sums[2 * which] / jnp.where(valid, sums[2 * which + 1], 1.0), 0.0)
        position = position_of(owner * rows + lane, total_rows)
        slanted = sky * position
        moments[0] += jnp.sum(sky * sky, axis=1, keepdims=True)
        moments[1] += jnp.sum(sky * slanted, axis=1, keepdims=True)
        moments[2] += jnp.sum(slanted * slanted, axis=1, keepdims=True)
        if which == 0:
            sky_out[...] = sky
            sky_copy[...] = sky
        end = position_of(owner * rows + rows, total_rows)
        running = [None] * specs
        summed = [None] * specs
        for k in range(rows):
            sky_k = jnp.broadcast_to(sky[:, k : k + 1], (exposures, fibres))
            for s in range(specs):
                term = ref[k, s] * sky_k
                running[s] = term if k == 0 else running[s] + term
                summed[s] = running[s] if k == 0 else summed[s] + running[s]
        for s in range(specs):
            plain[s] += running[s]
            tilted[s] += end * running[s] - step * summed[s]
    wide = lax.broadcasted_iota(jnp.int32, (exposures, lanes - fibres), 1)
    held = jnp.where(wide == 0, moments[0], jnp.where(wide == 1, moments[1], moments[2]))
    for s in range(specs):
        regress[s, :, :fibres] = plain[s]
        regress[specs + s, :, :fibres] = tilted[s]
        for r in (s, specs + s):
            regress[r, :, fibres:] = held


def regress_call(total_rows, flux, other, sums):
    rows, specs, exposures, fibres = flux.shape
    lanes = -(-(fibres + 3) // LANES) * LANES
    return pl.pallas_call(
        functools.partial(regress_kernel, total_rows),
        out_shape=(
            in_vmem((2 * specs, exposures, lanes)),
            in_vmem((exposures, LANES)),
            in_vmem((exposures, LANES)),
        ),
        in_specs=[VM] * 3,
        out_specs=(VM, VM, VM),
        compiler_params=pltpu.CompilerParams(vmem_limit_bytes=24 * 2**20),
        cost_estimate=pl.CostEstimate(flops=10**6, bytes_accessed=10**6, transcendentals=0),
        name="regress",
    )(flux, other, sums)


def clean_kernel(total_rows, flux, sky_ref, *refs):
    *terms, out, buf, sems = refs
    rows, specs, exposures, fibres = flux.shape
    device = lax.axis_index("wave")

    def got(slot):
        return sum(term[slot] for term in terms)

    sums = [got(slot) for slot in range(2 * specs)]
    moments = [sums[0][:, fibres + m : fibres + m + 1] for m in range(3)]
    upper_left, cross, lower_right = moments[0] + RIDGE, moments[1], moments[2] + RIDGE
    inverse = 1.0 / (upper_left * lower_right - cross * cross)
    start = position_of(device * rows, total_rows)
    step = 2.0 / (total_rows - 1)
    level, change = [], []
    for s in range(specs):
        r1, r2 = sums[s][:, :fibres], sums[specs + s][:, :fibres]
        slope_a = (lower_right * r1 - cross * r2) * inverse
        slope_b = (upper_left * r2 - cross * r1) * inverse
        level.append(slope_a + slope_b * start)
        change.append(slope_b * step)
    sky = sky_ref[...]
    chunks = sems.shape[0]
    bounds = [rows * c // chunks for c in range(chunks + 1)]
    for c in range(chunks):
        low, high = bounds[c], bounds[c + 1]
        for k in range(low, high):
            sky_k = jnp.broadcast_to(sky[:, k : k + 1], (exposures, fibres))
            for s in range(specs):
                buf[k, s] = flux[k, s] - level[s] * sky_k
                level[s] = level[s] + change[s]
        for e in range(exposures):
            pltpu.make_async_copy(
                buf.at[low:high, :, e], out.at[e, low:high], sems.at[c]
            ).start()
    for c in range(chunks):
        part = buf.at[bounds[c] : bounds[c + 1]]
        pltpu.make_async_copy(part, part, sems.at[c]).wait()


def clean_call(total_rows, flux, sky, terms):
    rows, specs, exposures, fibres = flux.shape
    return pl.pallas_call(
        functools.partial(clean_kernel, total_rows),
        out_shape=jax.ShapeDtypeStruct((exposures, rows, specs, fibres), F32),
        in_specs=[VM] * (2 + len(terms)),
        out_specs=HB,
        scratch_shapes=[
            pltpu.VMEM((rows, specs, exposures, fibres), F32),
            pltpu.SemaphoreType.DMA((5,)),
        ],
        compiler_params=pltpu.CompilerParams(vmem_limit_bytes=24 * 2**20),
        cost_estimate=pl.CostEstimate(flops=10**6, bytes_accessed=10**6, transcendentals=0),
        name="clean",
    )(flux, sky, *terms)


def powers(low, high):
    steps = []
    while low < high:
        steps.append(low)
        low *= 2
    return steps


def swap(values, partner):
    spec, wave = lax.axis_size("spec"), lax.axis_size("wave")
    pairs = []
    for s in range(spec):
        for i in range(wave):
            t, j = partner(s, i)
            if not 0 <= j < wave:
                t, j = s ^ 1, i
            if t < spec:
                pairs.append((s * wave + i, t * wave + j))
    return lax.ppermute(values, ("spec", "wave"), pairs)


def local(pixels, ivar, mask, psf_left, psf_right, sky_index):
    arrays = [jnp.transpose(x, (0, 2, 1, 3)) for x in (pixels, ivar, mask, psf_left, psf_right)]
    rows = pixels.shape[2]
    wave, spec = lax.axis_size("wave"), lax.axis_size("spec")
    total_rows = rows * wave
    hbm = [pltpu.with_memory_space_constraint(x, pltpu.HBM) for x in arrays]
    odd = lax.rem(lax.axis_index("wave"), 2) == 1

    def other_core(s, i):
        return (s, i ^ 1)

    near, far = edge_call(hbm)
    far = swap(far, lambda s, i: (s, i + 1 if i % 2 else i - 1))
    near = swap(near, other_core)
    bands = prepare_call(arrays[:PREFETCH] + hbm[PREFETCH:], sky_index)
    flux, sums = solve_call(wave, near, far, bands)
    got = swap(sums, other_core)
    flux, got = lax.optimization_barrier((flux, got))
    other = swap(flux, other_core)
    sums = jnp.concatenate([sums, got])
    if spec == 4:
        first = swap(sums, lambda s, i: (s ^ (1 if i % 2 else 2), i))
        third = swap(sums, lambda s, i: (s ^ 3, i))
        second = swap(first, other_core)
        second = jnp.concatenate([second[2:], second[:2]])
        sums = (sums + jnp.where(odd, first, second)) + (jnp.where(odd, second, first) + third)
    else:
        for k in powers(1, spec):
            sums = sums + swap(sums, lambda s, i: (s ^ k, i))
    regress, sky, sky_out = regress_call(total_rows, flux, other, sums)
    if wave == 8:
        first = swap(regress, lambda s, i: (s, i ^ (4 if i % 2 else 2)))
        third = swap(regress, lambda s, i: (s, i ^ 6 if i % 2 else -1))
        fetched = first + jnp.where(odd, third, 0.0)
        terms = [regress, fetched, swap(fetched, other_core)]
    else:
        for k in powers(2, wave):
            regress = regress + swap(regress, lambda s, i: (s, i ^ k if i % 2 else -1))
        terms = [jnp.where(odd, regress, swap(regress, other_core))]
    cleaned = clean_call(total_rows, flux, sky, terms)
    return (jnp.transpose(cleaned, (0, 2, 1, 3)), sky_out[:, :rows])


def solution(mesh):
    block = P(None, "spec", "wave", None)
    return jax.shard_map(
        local,
        mesh=mesh,
        in_specs=(block,) * 5 + (P("spec", None),),
        out_specs=(block, P(None, "wave")),
        check_vma=False,
    )
```

```python
import functools

import jax
import jax.numpy as jnp
from jax import lax
from jax.experimental import pallas as pl
from jax.experimental.pallas import tpu as pltpu
from jax.sharding import PartitionSpec as P

REG = 0.05
RIDGE = 1.0
HALO = 4
PARTS = 6
LANES = 128

F32 = jnp.float32
VM = pl.BlockSpec(memory_space=pltpu.VMEM)
SM = pl.BlockSpec(memory_space=pltpu.SMEM)
HB = pl.BlockSpec(memory_space=pltpu.HBM)


def in_vmem(shape, dtype=F32):
    return jax.ShapeDtypeStruct(shape, dtype)


def recip(values):
    return 1.0 / values


def weight_of(ivar, mask):
    return jnp.where(mask == 0, ivar, 0.0)


def edge_message(p, w, l, r):
    wl = [a * b for a, b in zip(w, l)]
    wr = [a * b for a, b in zip(w, r)]
    d0 = w[0] + wl[1] * l[1] + REG
    d1 = w[1] + wr[0] * r[0] + wl[2] * l[2] + REG
    d2 = w[2] + wr[1] * r[1] + wl[3] * l[3] + REG
    d3 = w[3] + wr[2] * r[2]
    d4 = wr[3] * r[3]
    raw = d4
    a01 = wr[0] + wl[1]
    a12 = wr[1] + wl[2]
    a23 = wr[2] + wl[3]
    a34 = wr[3]
    a02 = wl[1] * r[1]
    a13 = wl[2] * r[2]
    a24 = wl[3] * r[3]
    b0 = w[0] * p[0] + wl[1] * p[1]
    b1 = w[1] * p[1] + wr[0] * p[0] + wl[2] * p[2]
    b2 = w[2] * p[2] + wr[1] * p[1] + wl[3] * p[3]
    b3 = w[3] * p[3] + wr[2] * p[2]
    b4 = wr[3] * p[3]
    inv = recip(d0)
    near, far = a01 * inv, a02 * inv
    d1, a12, d2 = d1 - near * a01, a12 - near * a02, d2 - far * a02
    b1, b2 = b1 - near * b0, b2 - far * b0
    inv = recip(d1)
    near, far = a12 * inv, a13 * inv
    d2, a23, d3 = d2 - near * a12, a23 - near * a13, d3 - far * a13
    b2, b3 = b2 - near * b1, b3 - far * b1
    inv = recip(d2)
    near, far = a23 * inv, a24 * inv
    d3, a34, d4 = d3 - near * a23, a34 - near * a24, d4 - far * a24
    b3, b4 = b3 - near * b2, b4 - far * b2
    return (d3, a34, d4, b3, b4, raw)


def edge_kernel(pix, iva, msk, lef, rig, near_out, far_out, bufs, mbuf, sems):
    exposures, rows, specs, fibres = pix.shape
    odd = lax.rem(lax.axis_index("wave"), 2) == 1
    for end, start in enumerate((0, rows - HALO)):
        for e in range(exposures):
            for slot, ref in enumerate((pix, iva, lef, rig)):
                pltpu.make_async_copy(
                    ref.at[e, start : start + HALO], bufs.at[end, slot, :, :, e], sems.at[0, end]
                ).start()
            pltpu.make_async_copy(
                msk.at[e, start : start + HALO], mbuf.at[end, :, :, e], sems.at[1, end]
            ).start()
    for end in range(2):
        pltpu.make_async_copy(bufs.at[end], bufs.at[end], sems.at[0, end]).wait()
        pltpu.make_async_copy(mbuf.at[end], mbuf.at[end], sems.at[1, end]).wait()
        order = range(HALO - 1, -1, -1) if end == 0 else range(HALO)
        for s in range(specs):
            p = [bufs[end, 0, k, s] for k in order]
            w = [weight_of(bufs[end, 1, k, s], mbuf[end, k, s]) for k in order]
            l = [bufs[end, 2, k, s] for k in order]
            r = [bufs[end, 3, k, s] for k in order]
            if end == 0:
                for slot, value in enumerate(edge_message(p, w, r, l)):
                    near_out[slot, s] = value
                continue
            for slot, value in enumerate(edge_message(p, w, l, r)):
                top = near_out[slot, s]
                near_out[slot, s] = jnp.where(odd, top, value)
                far_out[slot, s] = jnp.where(odd, value, top)


def edge_call(arrays):
    exposures, rows, specs, fibres = arrays[0].shape
    message = in_vmem((PARTS, specs, exposures, fibres))
    return pl.pallas_call(
        edge_kernel,
        out_shape=(message, message),
        in_specs=[HB] * 5,
        out_specs=(VM, VM),
        scratch_shapes=[
            pltpu.VMEM((2, 4, HALO, specs, exposures, fibres), F32),
            pltpu.VMEM((2, HALO, specs, exposures, fibres), jnp.int32),
            pltpu.SemaphoreType.DMA((2, 2)),
        ],
        compiler_params=pltpu.CompilerParams(vmem_limit_bytes=8 * 2**20),
        cost_estimate=pl.CostEstimate(flops=10**6, bytes_accessed=10**6, transcendentals=0),
        name="edges",
    )(*arrays)


def prepare_kernel(
    chunks, pix, iva, msk, lef, rig, sky_index, diag, off_one, off_two, rhs, shares, sky_mask, denom, bufs, mbuf, sems
):
    exposures, rows, specs, fibres = pix.shape
    bounds = [rows * c // chunks for c in range(chunks + 1)]
    for c in range(chunks):
        low, high = bounds[c], bounds[c + 1]
        for e in range(exposures):
            for slot, ref in enumerate((pix, iva, lef, rig)):
                pltpu.make_async_copy(
                    ref.at[e, low:high], bufs.at[slot, low:high, :, e], sems.at[0, c]
                ).start()
            pltpu.make_async_copy(
                msk.at[e, low:high], mbuf.at[low:high, :, e], sems.at[1, c]
            ).start()
    lane = lax.broadcasted_iota(jnp.int32, (exposures, fibres), 1)
    for s in range(specs):
        found = lane == sky_index[s, 0]
        for k in range(1, sky_index.shape[1]):
            found = found | (lane == sky_index[s, k])
        sky_mask[s] = jnp.where(found, 1.0, 0.0)

    spot = lax.broadcasted_iota(jnp.int32, (exposures, LANES), 1)

    def share(k, s, value, total):
        part = sky_mask[s] * value
        shares[k, s] = part
        return jnp.where(spot == k, total + jnp.sum(part, axis=1, keepdims=True), total)

    def row(k, s, carry, total):
        w1, wp1, wr1, wrr2, wrp2, wrr1, wrp1 = carry
        p, w, l, r = bufs[0, k, s], weight_of(bufs[1, k, s], mbuf[k, s]), bufs[2, k, s], bufs[3, k, s]
        wl, wr, wp = w * l, w * r, w * p
        here = w1 + wl * l + (wrr2 + REG)
        diag[k, s] = here
        if k > 0:
            total = share(k - 1, s, here, total)
        off_one[k, s] = wr1 + wl
        off_two[k, s] = wl * r
        rhs[k, s] = wp1 + wl * p + wrp2
        return (w, wp, wr, wrr1, wrp1, wr * r, wr * p), total

    carries = [(0.0,) * 7 for _ in range(specs)]
    total = jnp.zeros((exposures, LANES), F32)
    for c in range(chunks):
        low, high = bounds[c], bounds[c + 1]
        part, mpart = bufs.at[:, low:high], mbuf.at[low:high]
        pltpu.make_async_copy(part, part, sems.at[0, c]).wait()
        pltpu.make_async_copy(mpart, mpart, sems.at[1, c]).wait()
        for s in range(specs):
            for k in range(low, high):
                carries[s], total = row(k, s, carries[s], total)
    for s in range(specs):
        w1, wp1, wr1, wrr2, wrp2, wrr1, wrp1 = carries[s]
        here = w1 + (wrr2 + REG)
        diag[rows, s] = here
        total = share(rows - 1, s, here, total)
        off_one[rows, s] = wr1
        rhs[rows, s] = wp1 + wrp2
        diag[rows + 1, s] = wrr1 + REG
        rhs[rows + 1, s] = wrp1
    denom[...] = total


def prepare_call(arrays, sky_index):
    exposures, rows, specs, fibres = arrays[0].shape
    chunks = 5
    grown = in_vmem((rows + 2, specs, exposures, fibres))
    return pl.pallas_call(
        functools.partial(prepare_kernel, chunks),
        out_shape=(
            grown,
            grown,
            grown,
            grown,
            in_vmem((rows, specs, exposures, fibres)),
            in_vmem((specs, exposures, fibres)),
            in_vmem((exposures, LANES)),
        ),
        in_specs=[HB] * 5 + [SM],
        out_specs=(VM,) * 7,
        scratch_shapes=[
            pltpu.VMEM((4, rows, specs, exposures, fibres), F32),
            pltpu.VMEM((rows, specs, exposures, fibres), jnp.int32),
            pltpu.SemaphoreType.DMA((2, chunks)),
        ],
        compiler_params=pltpu.CompilerParams(vmem_limit_bytes=24 * 2**20),
        cost_estimate=pl.CostEstimate(flops=10**7, bytes_accessed=10**7, transcendentals=0),
        name="prepare",
    )(*arrays, sky_index)


def solve_kernel(
    wave, near, far, diag, off_one, off_two, rhs, shares, sky_mask, denom, flux, sums, lower, lower_far, half
):
    count, specs, exposures, fibres = diag.shape
    rows = count - 2
    device = lax.axis_index("wave")
    is_odd = lax.rem(device, 2) == 1
    at_end = (device == 0) | (device == wave - 1)

    def from_far(part, s):
        return jnp.where(at_end, 0.0, far[part, s])

    def left(part, s):
        return jnp.where(is_odd, near[part, s], from_far(part, s))

    def right(part, s):
        return jnp.where(is_odd, from_far(part, s), near[part, s])

    lane = lax.broadcasted_iota(jnp.int32, (exposures, LANES), 1)
    numer = jnp.zeros((exposures, LANES), F32)

    zero = jnp.zeros((exposures, fibres), F32)
    spans = range(specs)

    def step(k, state, d, a, b, far_a):
        inv1, inv2, mult1, y1, y2 = state
        f = far_a * inv2
        upper = a - far_a * mult1
        g = upper * inv1
        pivot = d - f * far_a - g * upper
        y = b - f * y2 - g * y1
        return f, g, y, (recip(pivot), inv1, g, y, y1)

    def put(k, s, f, g, y, state):
        lower_far[k, s] = f
        lower[k, s] = g
        half[k, s] = y * state[0]

    states = []
    for s in spans:
        state = (zero,) * 5
        f, g, y, state = step(0, state, diag[0, s] + left(0, s), zero, rhs[0, s] + left(3, s), zero)
        put(0, s, f, g, y, state)
        f, g, y, state = step(
            1,
            state,
            diag[1, s] + left(2, s),
            off_one[0, s] + left(1, s),
            rhs[1, s] + left(4, s),
            zero,
        )
        put(1, s, f, g, y, state)
        states.append(state)

    def forward(k, states):
        results = []
        for s in spans:
            f, g, y, state = step(
                k, states[s], diag[k, s], off_one[k - 1, s], rhs[k, s], off_two[k - 2, s]
            )
            put(k, s, f, g, y, state)
            results.append(state)
        return tuple(results)

    states = lax.fori_loop(2, rows, forward, tuple(states), unroll=4)

    after = [None] * specs
    for s in spans:
        f, g, y, state = step(
            rows,
            states[s],
            diag[rows, s] + right(2, s),
            off_one[rows - 1, s],
            rhs[rows, s] + right(4, s),
            off_two[rows - 2, s],
        )
        f1, g1, y1, state1 = step(
            rows + 1,
            state,
            diag[rows + 1, s] + right(0, s),
            off_one[rows, s] + right(1, s),
            rhs[rows + 1, s] + right(3, s),
            off_two[rows - 1, s],
        )
        last = y1 * state1[0]
        here = y * state[0] - g1 * last
        flux[rows - 1, s] = here
        after[s] = (here, last, g, f1, f)

    def total(parts):
        return jnp.sum(parts, axis=1, keepdims=True)

    def spread(k, numer, parts, values):
        return jnp.where(lane == k, total(sum(parts[s] * values[s] for s in spans)), numer)

    extra = [sky_mask[s] * right(5, s) for s in spans]
    parts = [shares[rows - 1, s] + extra[s] for s in spans]
    numer = spread(rows - 1, numer, parts, [after[s][0] for s in spans])
    weights = denom[...] + jnp.where(lane == rows - 1, total(sum(extra)), 0.0)

    def backward(step_row, carry):
        k = rows - 1 - step_row
        numer, after = carry
        results = []
        for s in spans:
            x1, x2, g1, f2, f1 = after[s]
            value = half[k, s] - g1 * x1 - f2 * x2
            flux[k - 1, s] = value
            results.append((value, x1, lower[k, s], f1, lower_far[k, s]))
        parts = [shares[k - 1, s] for s in spans]
        return (spread(k - 1, numer, parts, [r[0] for r in results]), tuple(results))

    numer, after = lax.fori_loop(0, rows - 2, backward, (numer, tuple(after)), unroll=4)
    values = []
    for s in spans:
        x1, x2, g1, f2, f1 = after[s]
        value = half[1, s] - g1 * x1 - f2 * x2
        flux[0, s] = value
        values.append(value)
    extra = [sky_mask[s] * left(5, s) for s in spans]
    parts = [shares[0, s] + extra[s] for s in spans]
    sums[0] = spread(0, numer, parts, values)
    sums[1] = weights + jnp.where(lane == 0, total(sum(extra)), 0.0)


def solve_call(wave, near, far, bands):
    count, specs, exposures, fibres = bands[0].shape
    rows = count - 2
    scratch = pltpu.VMEM((count, specs, exposures, fibres), F32)
    return pl.pallas_call(
        functools.partial(solve_kernel, wave),
        out_shape=(in_vmem((rows, specs, exposures, fibres)), in_vmem((2, exposures, LANES))),
        in_specs=[VM] * 9,
        out_specs=(VM, VM),
        scratch_shapes=[scratch] * 3,
        compiler_params=pltpu.CompilerParams(vmem_limit_bytes=24 * 2**20),
        cost_estimate=pl.CostEstimate(flops=10**7, bytes_accessed=10**7, transcendentals=0),
        name="solve",
    )(near, far, *bands)


def position_of(index, total_rows):
    return 2.0 * jnp.asarray(index).astype(F32) / (total_rows - 1) - 1.0


def regress_kernel(total_rows, flux, other, sums, regress, sky_out, sky_copy):
    rows, specs, exposures, fibres = flux.shape
    lanes = regress.shape[2]
    device = lax.axis_index("wave")
    odd = lax.rem(device, 2)
    lane = lax.broadcasted_iota(jnp.int32, (exposures, LANES), 1)
    valid = lane < rows
    step = 2.0 / (total_rows - 1)
    plain = [0.0] * specs
    tilted = [0.0] * specs
    moments = [0.0] * 3
    for which, (ref, core) in enumerate(((flux, odd), (other, 1 - odd))):
        owner = device - odd + core
        sky = jnp.where(valid, sums[2 * core] / jnp.where(valid, sums[2 * core + 1], 1.0), 0.0)
        position = position_of(owner * rows + lane, total_rows)
        slanted = sky * position
        moments[0] += jnp.sum(sky * sky, axis=1, keepdims=True)
        moments[1] += jnp.sum(sky * slanted, axis=1, keepdims=True)
        moments[2] += jnp.sum(slanted * slanted, axis=1, keepdims=True)
        if which == 0:
            sky_out[...] = sky
            sky_copy[...] = sky
        end = position_of(owner * rows + rows, total_rows)
        running = [None] * specs
        summed = [None] * specs
        for k in range(rows):
            sky_k = jnp.broadcast_to(sky[:, k : k + 1], (exposures, fibres))
            for s in range(specs):
                term = ref[k, s] * sky_k
                running[s] = term if k == 0 else running[s] + term
                summed[s] = running[s] if k == 0 else summed[s] + running[s]
        for s in range(specs):
            plain[s] += running[s]
            tilted[s] += end * running[s] - step * summed[s]
    wide = lax.broadcasted_iota(jnp.int32, (exposures, lanes - fibres), 1)
    held = jnp.where(wide == 0, moments[0], jnp.where(wide == 1, moments[1], moments[2]))
    for s in range(specs):
        regress[s, :, :fibres] = plain[s]
        regress[specs + s, :, :fibres] = tilted[s]
        for r in (s, specs + s):
            regress[r, :, fibres:] = held


def regress_call(total_rows, flux, other, sums):
    rows, specs, exposures, fibres = flux.shape
    lanes = -(-(fibres + 3) // LANES) * LANES
    return pl.pallas_call(
        functools.partial(regress_kernel, total_rows),
        out_shape=(
            in_vmem((2 * specs, exposures, lanes)),
            in_vmem((exposures, LANES)),
            in_vmem((exposures, LANES)),
        ),
        in_specs=[VM] * 3,
        out_specs=(VM, VM, VM),
        compiler_params=pltpu.CompilerParams(vmem_limit_bytes=24 * 2**20),
        cost_estimate=pl.CostEstimate(flops=10**6, bytes_accessed=10**6, transcendentals=0),
        name="regress",
    )(flux, other, sums)


def clean_kernel(total_rows, flux, sky_ref, *refs):
    *terms, out, buf, sems = refs
    rows, specs, exposures, fibres = flux.shape
    device = lax.axis_index("wave")

    def got(slot):
        return sum(term[slot] for term in terms)

    sums = [got(slot) for slot in range(2 * specs)]
    moments = [sums[0][:, fibres + m : fibres + m + 1] for m in range(3)]
    upper_left, cross, lower_right = moments[0] + RIDGE, moments[1], moments[2] + RIDGE
    inverse = 1.0 / (upper_left * lower_right - cross * cross)
    start = position_of(device * rows, total_rows)
    step = 2.0 / (total_rows - 1)
    level, change = [], []
    for s in range(specs):
        r1, r2 = sums[s][:, :fibres], sums[specs + s][:, :fibres]
        slope_a = (lower_right * r1 - cross * r2) * inverse
        slope_b = (upper_left * r2 - cross * r1) * inverse
        level.append(slope_a + slope_b * start)
        change.append(slope_b * step)
    sky = sky_ref[...]
    chunks = sems.shape[0]
    bounds = [rows * c // chunks for c in range(chunks + 1)]
    for c in range(chunks):
        low, high = bounds[c], bounds[c + 1]
        for k in range(low, high):
            sky_k = jnp.broadcast_to(sky[:, k : k + 1], (exposures, fibres))
            for s in range(specs):
                buf[k, s] = flux[k, s] - level[s] * sky_k
                level[s] = level[s] + change[s]
        for e in range(exposures):
            pltpu.make_async_copy(
                buf.at[low:high, :, e], out.at[e, low:high], sems.at[c]
            ).start()
    for c in range(chunks):
        part = buf.at[bounds[c] : bounds[c + 1]]
        pltpu.make_async_copy(part, part, sems.at[c]).wait()


def clean_call(total_rows, flux, sky, terms):
    rows, specs, exposures, fibres = flux.shape
    return pl.pallas_call(
        functools.partial(clean_kernel, total_rows),
        out_shape=jax.ShapeDtypeStruct((exposures, rows, specs, fibres), F32),
        in_specs=[VM] * (2 + len(terms)),
        out_specs=HB,
        scratch_shapes=[
            pltpu.VMEM((rows, specs, exposures, fibres), F32),
            pltpu.SemaphoreType.DMA((5,)),
        ],
        compiler_params=pltpu.CompilerParams(vmem_limit_bytes=24 * 2**20),
        cost_estimate=pl.CostEstimate(flops=10**6, bytes_accessed=10**6, transcendentals=0),
        name="clean",
    )(flux, sky, *terms)


def powers(low, high):
    steps = []
    while low < high:
        steps.append(low)
        low *= 2
    return steps


def swap(values, partner):
    spec, wave = lax.axis_size("spec"), lax.axis_size("wave")
    pairs = []
    for s in range(spec):
        for i in range(wave):
            t, j = partner(s, i)
            if not 0 <= j < wave:
                t, j = s ^ 1, i
            if t < spec:
                pairs.append((s * wave + i, t * wave + j))
    return lax.ppermute(values, ("spec", "wave"), pairs)


def local(pixels, ivar, mask, psf_left, psf_right, sky_index):
    arrays = [jnp.transpose(x, (0, 2, 1, 3)) for x in (pixels, ivar, mask, psf_left, psf_right)]
    rows = pixels.shape[2]
    wave, spec = lax.axis_size("wave"), lax.axis_size("spec")
    total_rows = rows * wave
    hbm = [pltpu.with_memory_space_constraint(x, pltpu.HBM) for x in arrays]
    odd = lax.rem(lax.axis_index("wave"), 2) == 1

    def other_core(s, i):
        return (s, i ^ 1)

    near, far = edge_call(hbm)
    far = swap(far, lambda s, i: (s, i + 1 if i % 2 else i - 1))
    near = swap(near, other_core)
    bands = prepare_call(hbm, sky_index)
    flux, sums = solve_call(wave, near, far, bands)
    got = swap(sums, other_core)
    flux, got = lax.optimization_barrier((flux, got))
    other = swap(flux, other_core)
    sums = jnp.where(odd, jnp.concatenate([got, sums]), jnp.concatenate([sums, got]))
    if spec == 4:
        first = swap(sums, lambda s, i: (s ^ (1 if i % 2 else 2), i))
        third = swap(sums, lambda s, i: (s ^ 3, i))
        second = swap(first, other_core)
        sums = (sums + jnp.where(odd, first, second)) + (jnp.where(odd, second, first) + third)
    else:
        for k in powers(1, spec):
            sums = sums + swap(sums, lambda s, i: (s ^ k, i))
    regress, sky, sky_out = regress_call(total_rows, flux, other, sums)
    if wave == 8:
        first = swap(regress, lambda s, i: (s, i ^ (4 if i % 2 else 2)))
        third = swap(regress, lambda s, i: (s, i ^ 6 if i % 2 else -1))
        fetched = first + jnp.where(odd, third, 0.0)
        terms = [regress, fetched, swap(fetched, other_core)]
    else:
        for k in powers(2, wave):
            regress = regress + swap(regress, lambda s, i: (s, i ^ k if i % 2 else -1))
        terms = [jnp.where(odd, regress, swap(regress, other_core))]
    cleaned = clean_call(total_rows, flux, sky, terms)
    return (jnp.transpose(cleaned, (0, 2, 1, 3)), sky_out[:, :rows])


def solution(mesh):
    block = P(None, "spec", "wave", None)
    return jax.shard_map(
        local,
        mesh=mesh,
        in_specs=(block,) * 5 + (P("spec", None),),
        out_specs=(block, P(None, "wave")),
        check_vma=False,
    )
```

```python
import functools

import jax
import jax.numpy as jnp
from jax import lax
from jax.experimental import pallas as pl
from jax.experimental.pallas import tpu as pltpu
from jax.sharding import PartitionSpec as P

REG = 0.05
RIDGE = 1.0
HALO = 4
PARTS = 6
LANES = 128

F32 = jnp.float32
VM = pl.BlockSpec(memory_space=pltpu.VMEM)
SM = pl.BlockSpec(memory_space=pltpu.SMEM)
HB = pl.BlockSpec(memory_space=pltpu.HBM)


def in_vmem(shape, dtype=F32):
    return jax.ShapeDtypeStruct(shape, dtype)


def recip(values):
    return 1.0 / values


def weight_of(ivar, mask):
    return jnp.where(mask == 0, ivar, 0.0)


def edge_message(p, w, l, r):
    wl = [a * b for a, b in zip(w, l)]
    wr = [a * b for a, b in zip(w, r)]
    d0 = w[0] + wl[1] * l[1] + REG
    d1 = w[1] + wr[0] * r[0] + wl[2] * l[2] + REG
    d2 = w[2] + wr[1] * r[1] + wl[3] * l[3] + REG
    d3 = w[3] + wr[2] * r[2]
    d4 = wr[3] * r[3]
    raw = d4
    a01 = wr[0] + wl[1]
    a12 = wr[1] + wl[2]
    a23 = wr[2] + wl[3]
    a34 = wr[3]
    a02 = wl[1] * r[1]
    a13 = wl[2] * r[2]
    a24 = wl[3] * r[3]
    b0 = w[0] * p[0] + wl[1] * p[1]
    b1 = w[1] * p[1] + wr[0] * p[0] + wl[2] * p[2]
    b2 = w[2] * p[2] + wr[1] * p[1] + wl[3] * p[3]
    b3 = w[3] * p[3] + wr[2] * p[2]
    b4 = wr[3] * p[3]
    inv = recip(d0)
    near, far = a01 * inv, a02 * inv
    d1, a12, d2 = d1 - near * a01, a12 - near * a02, d2 - far * a02
    b1, b2 = b1 - near * b0, b2 - far * b0
    inv = recip(d1)
    near, far = a12 * inv, a13 * inv
    d2, a23, d3 = d2 - near * a12, a23 - near * a13, d3 - far * a13
    b2, b3 = b2 - near * b1, b3 - far * b1
    inv = recip(d2)
    near, far = a23 * inv, a24 * inv
    d3, a34, d4 = d3 - near * a23, a34 - near * a24, d4 - far * a24
    b3, b4 = b3 - near * b2, b4 - far * b2
    return (d3, a34, d4, b3, b4, raw)


def edge_kernel(pix, iva, msk, lef, rig, near_out, far_out, bufs, mbuf, sems):
    exposures, rows, specs, fibres = pix.shape
    odd = lax.rem(lax.axis_index("wave"), 2) == 1
    for end, start in enumerate((0, rows - HALO)):
        for e in range(exposures):
            for slot, ref in enumerate((pix, iva, lef, rig)):
                pltpu.make_async_copy(
                    ref.at[e, start : start + HALO], bufs.at[end, slot, :, :, e], sems.at[0, end]
                ).start()
            pltpu.make_async_copy(
                msk.at[e, start : start + HALO], mbuf.at[end, :, :, e], sems.at[1, end]
            ).start()
    for end in range(2):
        pltpu.make_async_copy(bufs.at[end], bufs.at[end], sems.at[0, end]).wait()
        pltpu.make_async_copy(mbuf.at[end], mbuf.at[end], sems.at[1, end]).wait()
        order = range(HALO - 1, -1, -1) if end == 0 else range(HALO)
        for s in range(specs):
            p = [bufs[end, 0, k, s] for k in order]
            w = [weight_of(bufs[end, 1, k, s], mbuf[end, k, s]) for k in order]
            l = [bufs[end, 2, k, s] for k in order]
            r = [bufs[end, 3, k, s] for k in order]
            if end == 0:
                for slot, value in enumerate(edge_message(p, w, r, l)):
                    near_out[slot, s] = value
                continue
            for slot, value in enumerate(edge_message(p, w, l, r)):
                top = near_out[slot, s]
                near_out[slot, s] = jnp.where(odd, top, value)
                far_out[slot, s] = jnp.where(odd, value, top)


def edge_call(arrays):
    exposures, rows, specs, fibres = arrays[0].shape
    message = in_vmem((PARTS, specs, exposures, fibres))
    return pl.pallas_call(
        edge_kernel,
        out_shape=(message, message),
        in_specs=[HB] * 5,
        out_specs=(VM, VM),
        scratch_shapes=[
            pltpu.VMEM((2, 4, HALO, specs, exposures, fibres), F32),
            pltpu.VMEM((2, HALO, specs, exposures, fibres), jnp.int32),
            pltpu.SemaphoreType.DMA((2, 2)),
        ],
        compiler_params=pltpu.CompilerParams(vmem_limit_bytes=8 * 2**20),
        cost_estimate=pl.CostEstimate(flops=10**6, bytes_accessed=10**6, transcendentals=0),
        name="edges",
    )(*arrays)


def forward_kernel(
    chunks, near, pix, iva, msk, lef, rig, sky_index, lower, lower_far, half, shares, tail, sky_mask, denom, bufs, mbuf, sems
):
    exposures, rows, specs, fibres = pix.shape
    odd = lax.rem(lax.axis_index("wave"), 2)
    spans = range(specs)
    bounds = [rows * c // chunks for c in range(chunks + 1)]

    def place(low, high):
        return pl.ds(odd * low + (1 - odd) * (rows - high), high - low)

    for c in range(chunks):
        here = place(bounds[c], bounds[c + 1])
        for e in range(exposures):
            for slot, ref in enumerate((pix, iva, lef, rig)):
                pltpu.make_async_copy(
                    ref.at[e, here], bufs.at[slot, here, :, e], sems.at[0, c]
                ).start()
            pltpu.make_async_copy(msk.at[e, here], mbuf.at[here, :, e], sems.at[1, c]).start()
    lane = lax.broadcasted_iota(jnp.int32, (exposures, fibres), 1)
    for s in spans:
        found = lane == sky_index[s, 0]
        for k in range(1, sky_index.shape[1]):
            found = found | (lane == sky_index[s, k])
        sky_mask[s] = jnp.where(found, 1.0, 0.0)

    spot = lax.broadcasted_iota(jnp.int32, (exposures, LANES), 1)
    before, after = 3 - odd, 2 + odd

    def share(k, parts, total):
        parts = [sky_mask[s] * parts[s] for s in spans]
        for s in spans:
            shares[k, s] = parts[s]
        row = odd * k + (1 - odd) * (rows - 1 - k)
        return jnp.where(spot == row, jnp.sum(sum(parts), axis=1, keepdims=True), total)

    made = [dict(d1=REG, b1=0.0, d2=REG, b2=0.0, r1=0.0) for _ in spans]
    offs = [[] for _ in spans]
    fars = [[] for _ in spans]
    states = [None] * specs
    total = jnp.zeros((exposures, LANES), F32)
    for c in range(chunks):
        here = place(bounds[c], bounds[c + 1])
        part, mpart = bufs.at[:, here], mbuf.at[here]
        pltpu.make_async_copy(part, part, sems.at[0, c]).wait()
        pltpu.make_async_copy(mpart, mpart, sems.at[1, c]).wait()
        for k in range(bounds[c], bounds[c + 1]):
            row = odd * k + (1 - odd) * (rows - 1 - k)
            diags = []
            for s in spans:
                p, l, r = bufs[0, row, s], bufs[before, row, s], bufs[after, row, s]
                w = weight_of(bufs[1, row, s], mbuf[row, s])
                wl, wr, wp = w * l, w * r, w * p
                m = made[s]
                d, b = m["d1"] + wl * l, m["b1"] + wl * p
                offs[s].append(m["r1"] + wl)
                fars[s].append(wl * r)
                made[s] = dict(
                    d1=w + m["d2"], b1=wp + m["b2"], d2=wr * r + REG, b2=wr * p, r1=wr
                )
                if k == 0:
                    d, b = d + near[0, s], b + near[3, s]
                    offs[s][0] = offs[s][0] + near[1, s]
                    inv = recip(d)
                    states[s] = (inv, None, None, b, None)
                elif k == 1:
                    diags.append(d + near[5, s])
                    d, b = d + near[2, s], b + near[4, s]
                    inv1, _, _, y1, _ = states[s]
                    upper = offs[s][0]
                    g = upper * inv1
                    inv, y = recip(d - g * upper), b - g * y1
                    lower[1, s], half[1, s] = g, y * inv
                    states[s] = (inv, inv1, g, y, y1)
                else:
                    diags.append(d)
                    f, g, y, states[s] = eliminate(states[s], d, offs[s][k - 1], b, fars[s][k - 2])
                    lower_far[k, s], lower[k, s], half[k, s] = f, g, y * states[s][0]
            if k > 0:
                total = share(k - 1, diags, total)
    for s in spans:
        m = made[s]
        tail_parts = states[s] + (
            m["d1"], offs[s][rows - 1], m["b1"], fars[s][rows - 2], m["d2"], m["r1"], m["b2"], fars[s][rows - 1]
        )
        for slot, value in enumerate(tail_parts):
            tail[slot, s] = value
    denom[...] = share(rows - 1, [made[s]["d1"] for s in spans], total)


TAIL = 13


def eliminate(state, d, a, b, far_a):
    inv1, inv2, mult1, y1, y2 = state
    f = far_a * inv2
    upper = a - far_a * mult1
    g = upper * inv1
    pivot = d - f * far_a - g * upper
    y = b - f * y2 - g * y1
    return f, g, y, (recip(pivot), inv1, g, y, y1)


def forward_call(near, arrays, sky_index):
    exposures, rows, specs, fibres = arrays[0].shape
    chunks = 5
    whole = in_vmem((rows, specs, exposures, fibres))
    return pl.pallas_call(
        functools.partial(forward_kernel, chunks),
        out_shape=(
            whole,
            whole,
            whole,
            whole,
            in_vmem((TAIL, specs, exposures, fibres)),
            in_vmem((specs, exposures, fibres)),
            in_vmem((exposures, LANES)),
        ),
        in_specs=[VM] + [HB] * 5 + [SM],
        out_specs=(VM,) * 7,
        scratch_shapes=[
            pltpu.VMEM((4, rows, specs, exposures, fibres), F32),
            pltpu.VMEM((rows, specs, exposures, fibres), jnp.int32),
            pltpu.SemaphoreType.DMA((2, chunks)),
        ],
        compiler_params=pltpu.CompilerParams(vmem_limit_bytes=24 * 2**20),
        cost_estimate=pl.CostEstimate(flops=10**7, bytes_accessed=10**7, transcendentals=0),
        name="forward",
    )(near, *arrays, sky_index)


def backward_kernel(wave, far, lower, lower_far, half, shares, tail, sky_mask, denom, flux, sums):
    rows, specs, exposures, fibres = lower.shape
    device = lax.axis_index("wave")
    odd = lax.rem(device, 2)
    at_end = (device == 0) | (device == wave - 1)
    lane = lax.broadcasted_iota(jnp.int32, (exposures, LANES), 1)
    spans = range(specs)

    def message(part, s):
        return jnp.where(at_end, 0.0, far[part, s])

    def place(k):
        return odd * k + (1 - odd) * (rows - 1 - k)

    def total(parts):
        return jnp.sum(parts, axis=1, keepdims=True)

    def spread(k, numer, parts, values):
        return jnp.where(lane == place(k), total(sum(parts[s] * values[s] for s in spans)), numer)

    after, extra = [], []
    for s in spans:
        t = [tail[slot, s] for slot in range(TAIL)]
        f, g, y, state = eliminate(t[:5], t[5] + message(2, s), t[6], t[7] + message(4, s), t[8])
        f1, g1, y1, last = eliminate(
            state, t[9] + message(0, s), t[10] + message(1, s), t[11] + message(3, s), t[12]
        )
        beyond = y1 * last[0]
        value = y * state[0] - g1 * beyond
        flux[place(rows - 1), s] = value
        after.append((value, beyond, g, f1, f))
        extra.append(sky_mask[s] * message(5, s))
    parts = [shares[rows - 1, s] + extra[s] for s in spans]
    numer = jnp.zeros((exposures, LANES), F32)
    numer = spread(rows - 1, numer, parts, [after[s][0] for s in spans])
    sums[1] = denom[...] + jnp.where(lane == place(rows - 1), total(sum(extra)), 0.0)

    def step(k, numer, after, bottom=False):
        results = []
        for s in spans:
            x1, x2, g1, f2, f1 = after[s]
            value = half[k, s] - g1 * x1 - f2 * x2
            flux[place(k - 1), s] = value
            results.append((value, x1) if bottom else (value, x1, lower[k, s], f1, lower_far[k, s]))
        parts = [shares[k - 1, s] for s in spans]
        return spread(k - 1, numer, parts, [r[0] for r in results]), tuple(results)

    numer, after = lax.fori_loop(
        0, rows - 2, lambda i, carry: step(rows - 1 - i, *carry), (numer, tuple(after)), unroll=4
    )
    numer, after = step(1, numer, after, bottom=True)
    sums[0] = numer


def backward_call(wave, far, factors):
    rows, specs, exposures, fibres = factors[0].shape
    return pl.pallas_call(
        functools.partial(backward_kernel, wave),
        out_shape=(in_vmem((rows, specs, exposures, fibres)), in_vmem((2, exposures, LANES))),
        in_specs=[VM] * 8,
        out_specs=(VM, VM),
        compiler_params=pltpu.CompilerParams(vmem_limit_bytes=24 * 2**20),
        cost_estimate=pl.CostEstimate(flops=10**7, bytes_accessed=10**7, transcendentals=0),
        name="backward",
    )(far, *factors)


def position_of(index, total_rows):
    return 2.0 * jnp.asarray(index).astype(F32) / (total_rows - 1) - 1.0


def regress_kernel(total_rows, flux, other, sums, regress, sky_out, sky_copy):
    rows, specs, exposures, fibres = flux.shape
    lanes = regress.shape[2]
    device = lax.axis_index("wave")
    odd = lax.rem(device, 2)
    lane = lax.broadcasted_iota(jnp.int32, (exposures, LANES), 1)
    valid = lane < rows
    step = 2.0 / (total_rows - 1)
    plain = [0.0] * specs
    tilted = [0.0] * specs
    moments = [0.0] * 3
    for which, (ref, core) in enumerate(((flux, odd), (other, 1 - odd))):
        owner = device - odd + core
        sky = jnp.where(valid, sums[2 * core] / jnp.where(valid, sums[2 * core + 1], 1.0), 0.0)
        position = position_of(owner * rows + lane, total_rows)
        slanted = sky * position
        moments[0] += jnp.sum(sky * sky, axis=1, keepdims=True)
        moments[1] += jnp.sum(sky * slanted, axis=1, keepdims=True)
        moments[2] += jnp.sum(slanted * slanted, axis=1, keepdims=True)
        if which == 0:
            sky_out[...] = sky
            sky_copy[...] = sky
        end = position_of(owner * rows + rows, total_rows)
        running = [None] * specs
        summed = [None] * specs
        for k in range(rows):
            sky_k = jnp.broadcast_to(sky[:, k : k + 1], (exposures, fibres))
            for s in range(specs):
                term = ref[k, s] * sky_k
                running[s] = term if k == 0 else running[s] + term
                summed[s] = running[s] if k == 0 else summed[s] + running[s]
        for s in range(specs):
            plain[s] += running[s]
            tilted[s] += end * running[s] - step * summed[s]
    wide = lax.broadcasted_iota(jnp.int32, (exposures, lanes - fibres), 1)
    held = jnp.where(wide == 0, moments[0], jnp.where(wide == 1, moments[1], moments[2]))
    for s in range(specs):
        regress[s, :, :fibres] = plain[s]
        regress[specs + s, :, :fibres] = tilted[s]
        for r in (s, specs + s):
            regress[r, :, fibres:] = held


def regress_call(total_rows, flux, other, sums):
    rows, specs, exposures, fibres = flux.shape
    lanes = -(-(fibres + 3) // LANES) * LANES
    return pl.pallas_call(
        functools.partial(regress_kernel, total_rows),
        out_shape=(
            in_vmem((2 * specs, exposures, lanes)),
            in_vmem((exposures, LANES)),
            in_vmem((exposures, LANES)),
        ),
        in_specs=[VM] * 3,
        out_specs=(VM, VM, VM),
        compiler_params=pltpu.CompilerParams(vmem_limit_bytes=24 * 2**20),
        cost_estimate=pl.CostEstimate(flops=10**6, bytes_accessed=10**6, transcendentals=0),
        name="regress",
    )(flux, other, sums)


def clean_kernel(total_rows, flux, sky_ref, *refs):
    *terms, out, buf, sems = refs
    rows, specs, exposures, fibres = flux.shape
    device = lax.axis_index("wave")

    def got(slot):
        return sum(term[slot] for term in terms)

    sums = [got(slot) for slot in range(2 * specs)]
    moments = [sums[0][:, fibres + m : fibres + m + 1] for m in range(3)]
    upper_left, cross, lower_right = moments[0] + RIDGE, moments[1], moments[2] + RIDGE
    inverse = 1.0 / (upper_left * lower_right - cross * cross)
    start = position_of(device * rows, total_rows)
    step = 2.0 / (total_rows - 1)
    level, change = [], []
    for s in range(specs):
        r1, r2 = sums[s][:, :fibres], sums[specs + s][:, :fibres]
        slope_a = (lower_right * r1 - cross * r2) * inverse
        slope_b = (upper_left * r2 - cross * r1) * inverse
        level.append(slope_a + slope_b * start)
        change.append(slope_b * step)
    sky = sky_ref[...]
    chunks = sems.shape[0]
    bounds = [rows * c // chunks for c in range(chunks + 1)]
    for c in range(chunks):
        low, high = bounds[c], bounds[c + 1]
        for k in range(low, high):
            sky_k = jnp.broadcast_to(sky[:, k : k + 1], (exposures, fibres))
            for s in range(specs):
                buf[k, s] = flux[k, s] - level[s] * sky_k
                level[s] = level[s] + change[s]
        for e in range(exposures):
            pltpu.make_async_copy(
                buf.at[low:high, :, e], out.at[e, low:high], sems.at[c]
            ).start()
    for c in range(chunks):
        part = buf.at[bounds[c] : bounds[c + 1]]
        pltpu.make_async_copy(part, part, sems.at[c]).wait()


def clean_call(total_rows, flux, sky, terms):
    rows, specs, exposures, fibres = flux.shape
    return pl.pallas_call(
        functools.partial(clean_kernel, total_rows),
        out_shape=jax.ShapeDtypeStruct((exposures, rows, specs, fibres), F32),
        in_specs=[VM] * (2 + len(terms)),
        out_specs=HB,
        scratch_shapes=[
            pltpu.VMEM((rows, specs, exposures, fibres), F32),
            pltpu.SemaphoreType.DMA((5,)),
        ],
        compiler_params=pltpu.CompilerParams(vmem_limit_bytes=24 * 2**20),
        cost_estimate=pl.CostEstimate(flops=10**6, bytes_accessed=10**6, transcendentals=0),
        name="clean",
    )(flux, sky, *terms)


def powers(low, high):
    steps = []
    while low < high:
        steps.append(low)
        low *= 2
    return steps


def swap(values, partner):
    spec, wave = lax.axis_size("spec"), lax.axis_size("wave")
    pairs = []
    for s in range(spec):
        for i in range(wave):
            t, j = partner(s, i)
            if not 0 <= j < wave:
                t, j = s ^ 1, i
            if t < spec:
                pairs.append((s * wave + i, t * wave + j))
    return lax.ppermute(values, ("spec", "wave"), pairs)


def local(pixels, ivar, mask, psf_left, psf_right, sky_index):
    arrays = [jnp.transpose(x, (0, 2, 1, 3)) for x in (pixels, ivar, mask, psf_left, psf_right)]
    rows = pixels.shape[2]
    wave, spec = lax.axis_size("wave"), lax.axis_size("spec")
    total_rows = rows * wave
    hbm = [pltpu.with_memory_space_constraint(x, pltpu.HBM) for x in arrays]
    odd = lax.rem(lax.axis_index("wave"), 2) == 1

    def other_core(s, i):
        return (s, i ^ 1)

    near, far = edge_call(hbm)
    far = swap(far, lambda s, i: (s, i + 1 if i % 2 else i - 1))
    near = swap(near, other_core)
    factors = forward_call(near, hbm, sky_index)
    flux, sums = backward_call(wave, far, factors)
    got = swap(sums, other_core)
    flux, got = lax.optimization_barrier((flux, got))
    other = swap(flux, other_core)
    sums = jnp.where(odd, jnp.concatenate([got, sums]), jnp.concatenate([sums, got]))
    if spec == 4:
        first = swap(sums, lambda s, i: (s ^ (1 if i % 2 else 2), i))
        third = swap(sums, lambda s, i: (s ^ 3, i ^ 1))
        second = swap(first, other_core)
        sums = (sums + jnp.where(odd, first, second)) + (jnp.where(odd, second, first) + third)
    else:
        for k in powers(1, spec):
            sums = sums + swap(sums, lambda s, i: (s ^ k, i))
    regress, sky, sky_out = regress_call(total_rows, flux, other, sums)
    if wave == 8:
        first = swap(regress, lambda s, i: (s, i ^ (4 if i % 2 else 2)))
        third = swap(regress, lambda s, i: (s, i ^ 6 if i % 2 else -1))
        fetched = first + jnp.where(odd, third, 0.0)
        terms = [regress, fetched, swap(fetched, other_core)]
    else:
        for k in powers(2, wave):
            regress = regress + swap(regress, lambda s, i: (s, i ^ k if i % 2 else -1))
        terms = [jnp.where(odd, regress, swap(regress, other_core))]
    cleaned = clean_call(total_rows, flux, sky, terms)
    return (jnp.transpose(cleaned, (0, 2, 1, 3)), sky_out[:, :rows])


def solution(mesh):
    block = P(None, "spec", "wave", None)
    return jax.shard_map(
        local,
        mesh=mesh,
        in_specs=(block,) * 5 + (P("spec", None),),
        out_specs=(block, P(None, "wave")),
        check_vma=False,
    )
```

```python
import functools

import jax
import jax.numpy as jnp
from jax import lax
from jax.experimental import pallas as pl
from jax.experimental.pallas import tpu as pltpu
from jax.sharding import PartitionSpec as P

REG = 0.05
RIDGE = 1.0
HALO = 4
PARTS = 6
LANES = 128

F32 = jnp.float32
VM = pl.BlockSpec(memory_space=pltpu.VMEM)
SM = pl.BlockSpec(memory_space=pltpu.SMEM)
HB = pl.BlockSpec(memory_space=pltpu.HBM)


def in_vmem(shape, dtype=F32):
    return jax.ShapeDtypeStruct(shape, dtype)


def recip(values):
    return 1.0 / values


def weight_of(ivar, mask):
    return jnp.where(mask == 0, ivar, 0.0)


def edge_message(p, w, l, r):
    wl = [a * b for a, b in zip(w, l)]
    wr = [a * b for a, b in zip(w, r)]
    d0 = w[0] + wl[1] * l[1] + REG
    d1 = w[1] + wr[0] * r[0] + wl[2] * l[2] + REG
    d2 = w[2] + wr[1] * r[1] + wl[3] * l[3] + REG
    d3 = w[3] + wr[2] * r[2]
    d4 = wr[3] * r[3]
    raw = d4
    a01 = wr[0] + wl[1]
    a12 = wr[1] + wl[2]
    a23 = wr[2] + wl[3]
    a34 = wr[3]
    a02 = wl[1] * r[1]
    a13 = wl[2] * r[2]
    a24 = wl[3] * r[3]
    b0 = w[0] * p[0] + wl[1] * p[1]
    b1 = w[1] * p[1] + wr[0] * p[0] + wl[2] * p[2]
    b2 = w[2] * p[2] + wr[1] * p[1] + wl[3] * p[3]
    b3 = w[3] * p[3] + wr[2] * p[2]
    b4 = wr[3] * p[3]
    inv = recip(d0)
    near, far = a01 * inv, a02 * inv
    d1, a12, d2 = d1 - near * a01, a12 - near * a02, d2 - far * a02
    b1, b2 = b1 - near * b0, b2 - far * b0
    inv = recip(d1)
    near, far = a12 * inv, a13 * inv
    d2, a23, d3 = d2 - near * a12, a23 - near * a13, d3 - far * a13
    b2, b3 = b2 - near * b1, b3 - far * b1
    inv = recip(d2)
    near, far = a23 * inv, a24 * inv
    d3, a34, d4 = d3 - near * a23, a34 - near * a24, d4 - far * a24
    b3, b4 = b3 - near * b2, b4 - far * b2
    return (d3, a34, d4, b3, b4, raw)


def edge_kernel(pix, iva, msk, lef, rig, near_out, far_out, bufs, mbuf, sems):
    exposures, rows, specs, fibres = pix.shape
    odd = lax.rem(lax.axis_index("wave"), 2) == 1
    for end, start in enumerate((0, rows - HALO)):
        for e in range(exposures):
            for slot, ref in enumerate((pix, iva, lef, rig)):
                pltpu.make_async_copy(
                    ref.at[e, start : start + HALO], bufs.at[end, slot, :, :, e], sems.at[0, end]
                ).start()
            pltpu.make_async_copy(
                msk.at[e, start : start + HALO], mbuf.at[end, :, :, e], sems.at[1, end]
            ).start()
    for end in range(2):
        pltpu.make_async_copy(bufs.at[end], bufs.at[end], sems.at[0, end]).wait()
        pltpu.make_async_copy(mbuf.at[end], mbuf.at[end], sems.at[1, end]).wait()
        order = range(HALO - 1, -1, -1) if end == 0 else range(HALO)
        for s in range(specs):
            p = [bufs[end, 0, k, s] for k in order]
            w = [weight_of(bufs[end, 1, k, s], mbuf[end, k, s]) for k in order]
            l = [bufs[end, 2, k, s] for k in order]
            r = [bufs[end, 3, k, s] for k in order]
            if end == 0:
                for slot, value in enumerate(edge_message(p, w, r, l)):
                    near_out[slot, s] = value
                continue
            for slot, value in enumerate(edge_message(p, w, l, r)):
                top = near_out[slot, s]
                near_out[slot, s] = jnp.where(odd, top, value)
                far_out[slot, s] = jnp.where(odd, value, top)


def edge_call(arrays):
    exposures, rows, specs, fibres = arrays[0].shape
    message = in_vmem((PARTS, specs, exposures, fibres))
    return pl.pallas_call(
        edge_kernel,
        out_shape=(message, message),
        in_specs=[HB] * 5,
        out_specs=(VM, VM),
        scratch_shapes=[
            pltpu.VMEM((2, 4, HALO, specs, exposures, fibres), F32),
            pltpu.VMEM((2, HALO, specs, exposures, fibres), jnp.int32),
            pltpu.SemaphoreType.DMA((2, 2)),
        ],
        compiler_params=pltpu.CompilerParams(vmem_limit_bytes=8 * 2**20),
        cost_estimate=pl.CostEstimate(flops=10**6, bytes_accessed=10**6, transcendentals=0),
        name="edges",
    )(*arrays)


def forward_kernel(
    chunks, near, pix, iva, msk, lef, rig, sky_index, lower, lower_far, half, shares, tail, sky_mask, denom, bufs, mbuf, sems
):
    exposures, rows, specs, fibres = pix.shape
    odd = lax.rem(lax.axis_index("wave"), 2)
    spans = range(specs)
    bounds = [rows * c // chunks for c in range(chunks + 1)]

    def place(low, high):
        return pl.ds(odd * low + (1 - odd) * (rows - high), high - low)

    for c in range(chunks):
        here = place(bounds[c], bounds[c + 1])
        for e in range(exposures):
            for slot, ref in enumerate((pix, iva, lef, rig)):
                pltpu.make_async_copy(
                    ref.at[e, here], bufs.at[slot, here, :, e], sems.at[0, c]
                ).start()
            pltpu.make_async_copy(msk.at[e, here], mbuf.at[here, :, e], sems.at[1, c]).start()
    lane = lax.broadcasted_iota(jnp.int32, (exposures, fibres), 1)
    for s in spans:
        found = lane == sky_index[s, 0]
        for k in range(1, sky_index.shape[1]):
            found = found | (lane == sky_index[s, k])
        sky_mask[s] = jnp.where(found, 1.0, 0.0)

    spot = lax.broadcasted_iota(jnp.int32, (exposures, LANES), 1)
    before, after = 3 - odd, 2 + odd

    def share(k, parts, total):
        parts = [sky_mask[s] * parts[s] for s in spans]
        for s in spans:
            shares[k, s] = parts[s]
        row = odd * k + (1 - odd) * (rows - 1 - k)
        return jnp.where(spot == row, jnp.sum(sum(parts), axis=1, keepdims=True), total)

    made = [dict(d1=REG, b1=0.0, d2=REG, b2=0.0, r1=0.0) for _ in spans]
    offs = [[] for _ in spans]
    fars = [[] for _ in spans]
    states = [None] * specs
    total = jnp.zeros((exposures, LANES), F32)
    for c in range(chunks):
        here = place(bounds[c], bounds[c + 1])
        part, mpart = bufs.at[:, here], mbuf.at[here]
        pltpu.make_async_copy(part, part, sems.at[0, c]).wait()
        pltpu.make_async_copy(mpart, mpart, sems.at[1, c]).wait()
        for k in range(bounds[c], bounds[c + 1]):
            row = odd * k + (1 - odd) * (rows - 1 - k)
            diags = []
            for s in spans:
                p, l, r = bufs[0, row, s], bufs[before, row, s], bufs[after, row, s]
                w = weight_of(bufs[1, row, s], mbuf[row, s])
                wl, wr, wp = w * l, w * r, w * p
                m = made[s]
                d, b = m["d1"] + wl * l, m["b1"] + wl * p
                offs[s].append(m["r1"] + wl)
                fars[s].append(wl * r)
                made[s] = dict(
                    d1=w + m["d2"], b1=wp + m["b2"], d2=wr * r + REG, b2=wr * p, r1=wr
                )
                if k == 0:
                    d, b = d + near[0, s], b + near[3, s]
                    offs[s][0] = offs[s][0] + near[1, s]
                    inv = recip(d)
                    states[s] = (inv, None, None, b, None)
                elif k == 1:
                    diags.append(d + near[5, s])
                    d, b = d + near[2, s], b + near[4, s]
                    inv1, _, _, y1, _ = states[s]
                    upper = offs[s][0]
                    g = upper * inv1
                    inv, y = recip(d - g * upper), b - g * y1
                    lower[1, s], half[1, s] = g, y * inv
                    states[s] = (inv, inv1, g, y, y1)
                else:
                    diags.append(d)
                    f, g, y, states[s] = eliminate(states[s], d, offs[s][k - 1], b, fars[s][k - 2])
                    lower_far[k, s], lower[k, s], half[k, s] = f, g, y * states[s][0]
            if k > 0:
                total = share(k - 1, diags, total)
    for s in spans:
        m = made[s]
        tail_parts = states[s] + (
            m["d1"], offs[s][rows - 1], m["b1"], fars[s][rows - 2], m["d2"], m["r1"], m["b2"], fars[s][rows - 1]
        )
        for slot, value in enumerate(tail_parts):
            tail[slot, s] = value
    denom[...] = share(rows - 1, [made[s]["d1"] for s in spans], total)


TAIL = 13


def eliminate(state, d, a, b, far_a):
    inv1, inv2, mult1, y1, y2 = state
    f = far_a * inv2
    upper = a - far_a * mult1
    g = upper * inv1
    pivot = d - f * far_a - g * upper
    y = b - f * y2 - g * y1
    return f, g, y, (recip(pivot), inv1, g, y, y1)


def forward_call(near, arrays, sky_index):
    exposures, rows, specs, fibres = arrays[0].shape
    chunks = 5
    whole = in_vmem((rows, specs, exposures, fibres))
    return pl.pallas_call(
        functools.partial(forward_kernel, chunks),
        out_shape=(
            whole,
            whole,
            whole,
            whole,
            in_vmem((TAIL, specs, exposures, fibres)),
            in_vmem((specs, exposures, fibres)),
            in_vmem((exposures, LANES)),
        ),
        in_specs=[VM] + [HB] * 5 + [SM],
        out_specs=(VM,) * 7,
        scratch_shapes=[
            pltpu.VMEM((4, rows, specs, exposures, fibres), F32),
            pltpu.VMEM((rows, specs, exposures, fibres), jnp.int32),
            pltpu.SemaphoreType.DMA((2, chunks)),
        ],
        compiler_params=pltpu.CompilerParams(vmem_limit_bytes=24 * 2**20),
        cost_estimate=pl.CostEstimate(flops=10**7, bytes_accessed=10**7, transcendentals=0),
        name="forward",
    )(near, *arrays, sky_index)


def backward_kernel(wave, far, lower, lower_far, half, shares, tail, sky_mask, denom, flux, sums):
    rows, specs, exposures, fibres = lower.shape
    device = lax.axis_index("wave")
    odd = lax.rem(device, 2)
    at_end = (device == 0) | (device == wave - 1)
    lane = lax.broadcasted_iota(jnp.int32, (exposures, LANES), 1)
    spans = range(specs)

    def message(part, s):
        return jnp.where(at_end, 0.0, far[part, s])

    def place(k):
        return odd * k + (1 - odd) * (rows - 1 - k)

    def total(parts):
        return jnp.sum(parts, axis=1, keepdims=True)

    def spread(k, numer, parts, values):
        return jnp.where(lane == place(k), total(sum(parts[s] * values[s] for s in spans)), numer)

    after, extra = [], []
    for s in spans:
        t = [tail[slot, s] for slot in range(TAIL)]
        f, g, y, state = eliminate(t[:5], t[5] + message(2, s), t[6], t[7] + message(4, s), t[8])
        f1, g1, y1, last = eliminate(
            state, t[9] + message(0, s), t[10] + message(1, s), t[11] + message(3, s), t[12]
        )
        beyond = y1 * last[0]
        value = y * state[0] - g1 * beyond
        flux[place(rows - 1), s] = value
        after.append((value, beyond, g, f1, f))
        extra.append(sky_mask[s] * message(5, s))
    parts = [shares[rows - 1, s] + extra[s] for s in spans]
    numer = jnp.zeros((exposures, LANES), F32)
    numer = spread(rows - 1, numer, parts, [after[s][0] for s in spans])
    sums[1] = denom[...] + jnp.where(lane == place(rows - 1), total(sum(extra)), 0.0)

    def step(k, numer, after, bottom=False):
        results = []
        for s in spans:
            x1, x2, g1, f2, f1 = after[s]
            value = half[k, s] - g1 * x1 - f2 * x2
            flux[place(k - 1), s] = value
            results.append((value, x1) if bottom else (value, x1, lower[k, s], f1, lower_far[k, s]))
        parts = [shares[k - 1, s] for s in spans]
        return spread(k - 1, numer, parts, [r[0] for r in results]), tuple(results)

    for k in range(rows - 1, 1, -1):
        numer, after = step(k, numer, after)
    numer, after = step(1, numer, after, bottom=True)
    sums[0] = numer


def backward_call(wave, far, factors):
    rows, specs, exposures, fibres = factors[0].shape
    return pl.pallas_call(
        functools.partial(backward_kernel, wave),
        out_shape=(in_vmem((rows, specs, exposures, fibres)), in_vmem((2, exposures, LANES))),
        in_specs=[VM] * 8,
        out_specs=(VM, VM),
        compiler_params=pltpu.CompilerParams(vmem_limit_bytes=24 * 2**20),
        cost_estimate=pl.CostEstimate(flops=10**7, bytes_accessed=10**7, transcendentals=0),
        name="backward",
    )(far, *factors)


def position_of(index, total_rows):
    return 2.0 * jnp.asarray(index).astype(F32) / (total_rows - 1) - 1.0


def regress_kernel(total_rows, flux, other, sums, regress, sky_out):
    rows, specs, exposures, fibres = flux.shape
    lanes = regress.shape[2]
    device = lax.axis_index("wave")
    odd = lax.rem(device, 2)
    lane = lax.broadcasted_iota(jnp.int32, (exposures, LANES), 1)
    valid = lane < rows
    step = 2.0 / (total_rows - 1)
    plain = [0.0] * specs
    tilted = [0.0] * specs
    moments = [0.0] * 3
    for which, (ref, core) in enumerate(((flux, odd), (other, 1 - odd))):
        owner = device - odd + core
        sky = jnp.where(valid, sums[2 * core] / jnp.where(valid, sums[2 * core + 1], 1.0), 0.0)
        position = position_of(owner * rows + lane, total_rows)
        slanted = sky * position
        moments[0] += jnp.sum(sky * sky, axis=1, keepdims=True)
        moments[1] += jnp.sum(sky * slanted, axis=1, keepdims=True)
        moments[2] += jnp.sum(slanted * slanted, axis=1, keepdims=True)
        if which == 0:
            sky_out[...] = sky
        end = position_of(owner * rows + rows, total_rows)
        running = [None] * specs
        summed = [None] * specs
        for k in range(rows):
            sky_k = jnp.broadcast_to(sky[:, k : k + 1], (exposures, fibres))
            for s in range(specs):
                term = ref[k, s] * sky_k
                running[s] = term if k == 0 else running[s] + term
                summed[s] = running[s] if k == 0 else summed[s] + running[s]
        for s in range(specs):
            plain[s] += running[s]
            tilted[s] += end * running[s] - step * summed[s]
    wide = lax.broadcasted_iota(jnp.int32, (exposures, lanes - fibres), 1)
    held = jnp.where(wide == 0, moments[0], jnp.where(wide == 1, moments[1], moments[2]))
    for s in range(specs):
        regress[s, :, :fibres] = plain[s]
        regress[specs + s, :, :fibres] = tilted[s]
        for r in (s, specs + s):
            regress[r, :, fibres:] = held


def regress_call(total_rows, flux, other, sums):
    rows, specs, exposures, fibres = flux.shape
    lanes = -(-(fibres + 3) // LANES) * LANES
    return pl.pallas_call(
        functools.partial(regress_kernel, total_rows),
        out_shape=(
            in_vmem((2 * specs, exposures, lanes)),
            in_vmem((exposures, LANES)),
        ),
        in_specs=[VM] * 3,
        out_specs=(VM, VM),
        compiler_params=pltpu.CompilerParams(vmem_limit_bytes=24 * 2**20),
        cost_estimate=pl.CostEstimate(flops=10**6, bytes_accessed=10**6, transcendentals=0),
        name="regress",
    )(flux, other, sums)


def clean_kernel(total_rows, flux, sky_ref, *refs):
    *terms, out, sky_out, buf, sems, sky_sem = refs
    rows, specs, exposures, fibres = flux.shape
    sky_copy = pltpu.make_async_copy(sky_ref, sky_out, sky_sem)
    sky_copy.start()
    device = lax.axis_index("wave")

    def got(slot):
        return sum(term[slot] for term in terms)

    sums = [got(slot) for slot in range(2 * specs)]
    moments = [sums[0][:, fibres + m : fibres + m + 1] for m in range(3)]
    upper_left, cross, lower_right = moments[0] + RIDGE, moments[1], moments[2] + RIDGE
    inverse = 1.0 / (upper_left * lower_right - cross * cross)
    start = position_of(device * rows, total_rows)
    step = 2.0 / (total_rows - 1)
    level, change = [], []
    for s in range(specs):
        r1, r2 = sums[s][:, :fibres], sums[specs + s][:, :fibres]
        slope_a = (lower_right * r1 - cross * r2) * inverse
        slope_b = (upper_left * r2 - cross * r1) * inverse
        level.append(slope_a + slope_b * start)
        change.append(slope_b * step)
    sky = sky_ref[...]
    chunks = sems.shape[0]
    bounds = [rows * c // chunks for c in range(chunks + 1)]
    for c in range(chunks):
        low, high = bounds[c], bounds[c + 1]
        for k in range(low, high):
            sky_k = jnp.broadcast_to(sky[:, k : k + 1], (exposures, fibres))
            for s in range(specs):
                buf[k, s] = flux[k, s] - level[s] * sky_k
                level[s] = level[s] + change[s]
        for e in range(exposures):
            pltpu.make_async_copy(
                buf.at[low:high, :, e], out.at[e, low:high], sems.at[c]
            ).start()
    for c in range(chunks):
        part = buf.at[bounds[c] : bounds[c + 1]]
        pltpu.make_async_copy(part, part, sems.at[c]).wait()
    sky_copy.wait()


def clean_call(total_rows, flux, sky, terms):
    rows, specs, exposures, fibres = flux.shape
    return pl.pallas_call(
        functools.partial(clean_kernel, total_rows),
        out_shape=(
            jax.ShapeDtypeStruct((exposures, rows, specs, fibres), F32),
            jax.ShapeDtypeStruct((exposures, LANES), F32),
        ),
        in_specs=[VM] * (2 + len(terms)),
        out_specs=(HB, HB),
        scratch_shapes=[
            pltpu.VMEM((rows, specs, exposures, fibres), F32),
            pltpu.SemaphoreType.DMA((4,)),
            pltpu.SemaphoreType.DMA,
        ],
        compiler_params=pltpu.CompilerParams(vmem_limit_bytes=24 * 2**20),
        cost_estimate=pl.CostEstimate(flops=10**6, bytes_accessed=10**6, transcendentals=0),
        name="clean",
    )(flux, sky, *terms)


def powers(low, high):
    steps = []
    while low < high:
        steps.append(low)
        low *= 2
    return steps


def swap(values, partner):
    spec, wave = lax.axis_size("spec"), lax.axis_size("wave")
    pairs = []
    for s in range(spec):
        for i in range(wave):
            t, j = partner(s, i)
            if not 0 <= j < wave:
                t, j = s ^ 1, i
            if t < spec:
                pairs.append((s * wave + i, t * wave + j))
    return lax.ppermute(values, ("spec", "wave"), pairs)


def local(pixels, ivar, mask, psf_left, psf_right, sky_index):
    arrays = [jnp.transpose(x, (0, 2, 1, 3)) for x in (pixels, ivar, mask, psf_left, psf_right)]
    rows = pixels.shape[2]
    wave, spec = lax.axis_size("wave"), lax.axis_size("spec")
    total_rows = rows * wave
    hbm = [pltpu.with_memory_space_constraint(x, pltpu.HBM) for x in arrays]
    odd = lax.rem(lax.axis_index("wave"), 2) == 1

    def other_core(s, i):
        return (s, i ^ 1)

    near, far = edge_call(hbm)
    far = swap(far, lambda s, i: (s, i + 1 if i % 2 else i - 1))
    near = swap(near, other_core)
    factors = forward_call(near, hbm, sky_index)
    flux, sums = backward_call(wave, far, factors)
    got = swap(sums, other_core)
    flux, got = lax.optimization_barrier((flux, got))
    other = swap(flux, other_core)
    sums = jnp.where(odd, jnp.concatenate([got, sums]), jnp.concatenate([sums, got]))
    if spec == 4:
        first = swap(sums, lambda s, i: (s ^ (1 if i % 2 else 2), i))
        third = swap(sums, lambda s, i: (s ^ 3, i ^ 1))
        second = swap(first, other_core)
        sums = (sums + jnp.where(odd, first, second)) + (jnp.where(odd, second, first) + third)
    else:
        for k in powers(1, spec):
            sums = sums + swap(sums, lambda s, i: (s ^ k, i))
    regress, sky = regress_call(total_rows, flux, other, sums)
    if wave == 8:
        first = swap(regress, lambda s, i: (s, i ^ (4 if i % 2 else 2)))
        third = swap(regress, lambda s, i: (s, i ^ 6 if i % 2 else -1))
        fetched = first + jnp.where(odd, third, 0.0)
        terms = [regress, fetched, swap(fetched, other_core)]
    else:
        for k in powers(2, wave):
            regress = regress + swap(regress, lambda s, i: (s, i ^ k if i % 2 else -1))
        terms = [jnp.where(odd, regress, swap(regress, other_core))]
    cleaned, sky = clean_call(total_rows, flux, sky, terms)
    return (jnp.transpose(cleaned, (0, 2, 1, 3)), sky[:, :rows])


def solution(mesh):
    block = P(None, "spec", "wave", None)
    return jax.shard_map(
        local,
        mesh=mesh,
        in_specs=(block,) * 5 + (P("spec", None),),
        out_specs=(block, P(None, "wave")),
        check_vma=False,
    )
```

```python
import functools

import jax
import jax.numpy as jnp
from jax import lax
from jax.experimental import pallas as pl
from jax.experimental.pallas import tpu as pltpu
from jax.sharding import PartitionSpec as P

REG = 0.05
RIDGE = 1.0
HALO = 4
PARTS = 6
LANES = 128

F32 = jnp.float32
VM = pl.BlockSpec(memory_space=pltpu.VMEM)
SM = pl.BlockSpec(memory_space=pltpu.SMEM)
HB = pl.BlockSpec(memory_space=pltpu.HBM)


def in_vmem(shape, dtype=F32):
    return jax.ShapeDtypeStruct(shape, dtype)


def recip(values):
    return 1.0 / values


def weight_of(ivar, mask):
    return jnp.where(mask == 0, ivar, 0.0)


def edge_message(p, w, l, r):
    wl = [a * b for a, b in zip(w, l)]
    wr = [a * b for a, b in zip(w, r)]
    d0 = w[0] + wl[1] * l[1] + REG
    d1 = w[1] + wr[0] * r[0] + wl[2] * l[2] + REG
    d2 = w[2] + wr[1] * r[1] + wl[3] * l[3] + REG
    d3 = w[3] + wr[2] * r[2]
    d4 = wr[3] * r[3]
    raw = d4
    a01 = wr[0] + wl[1]
    a12 = wr[1] + wl[2]
    a23 = wr[2] + wl[3]
    a34 = wr[3]
    a02 = wl[1] * r[1]
    a13 = wl[2] * r[2]
    a24 = wl[3] * r[3]
    b0 = w[0] * p[0] + wl[1] * p[1]
    b1 = w[1] * p[1] + wr[0] * p[0] + wl[2] * p[2]
    b2 = w[2] * p[2] + wr[1] * p[1] + wl[3] * p[3]
    b3 = w[3] * p[3] + wr[2] * p[2]
    b4 = wr[3] * p[3]
    inv = recip(d0)
    near, far = a01 * inv, a02 * inv
    d1, a12, d2 = d1 - near * a01, a12 - near * a02, d2 - far * a02
    b1, b2 = b1 - near * b0, b2 - far * b0
    inv = recip(d1)
    near, far = a12 * inv, a13 * inv
    d2, a23, d3 = d2 - near * a12, a23 - near * a13, d3 - far * a13
    b2, b3 = b2 - near * b1, b3 - far * b1
    inv = recip(d2)
    near, far = a23 * inv, a24 * inv
    d3, a34, d4 = d3 - near * a23, a34 - near * a24, d4 - far * a24
    b3, b4 = b3 - near * b2, b4 - far * b2
    return (d3, a34, d4, b3, b4, raw)


def edge_kernel(pix, iva, msk, lef, rig, near_out, far_out, head, bufs, mhead, mbuf, sems):
    exposures, rows, specs, fibres = pix.shape
    size = head.shape[1]
    odd = lax.rem(lax.axis_index("wave"), 2)
    first, last = (1 - odd) * (rows - size), odd * (rows - HALO)
    for e in range(exposures):
        for slot, ref in enumerate((pix, iva, lef, rig)):
            pltpu.make_async_copy(
                ref.at[e, pl.ds(first, size)], head.at[slot, :, :, e], sems.at[0]
            ).start()
        pltpu.make_async_copy(msk.at[e, pl.ds(first, size)], mhead.at[:, :, e], sems.at[1]).start()
    for e in range(exposures):
        for slot, ref in enumerate((pix, iva, lef, rig)):
            pltpu.make_async_copy(
                ref.at[e, pl.ds(last, HALO)], bufs.at[slot, :, :, e], sems.at[2]
            ).start()
        pltpu.make_async_copy(msk.at[e, pl.ds(last, HALO)], mbuf.at[:, :, e], sems.at[3]).start()
    before, after = 3 - odd, 2 + odd
    pltpu.make_async_copy(head, head, sems.at[0]).wait()
    pltpu.make_async_copy(mhead, mhead, sems.at[1]).wait()
    for k in range(size):
        for s in range(specs):
            head[1, k, s] = weight_of(head[1, k, s], mhead[k, s])
    order = [odd * k + (1 - odd) * (size - 1 - k) for k in range(HALO - 1, -1, -1)]
    for s in range(specs):
        p, w, l, r = [[head[slot, k, s] for k in order] for slot in (0, 1, before, after)]
        for slot, value in enumerate(edge_message(p, w, r, l)):
            near_out[slot, s] = value
    pltpu.make_async_copy(bufs, bufs, sems.at[2]).wait()
    pltpu.make_async_copy(mbuf, mbuf, sems.at[3]).wait()
    order = [odd * k + (1 - odd) * (HALO - 1 - k) for k in range(HALO)]
    for s in range(specs):
        p, l, r = [[bufs[slot, k, s] for k in order] for slot in (0, before, after)]
        w = [weight_of(bufs[1, k, s], mbuf[k, s]) for k in order]
        for slot, value in enumerate(edge_message(p, w, l, r)):
            far_out[slot, s] = value


def edge_call(arrays):
    exposures, rows, specs, fibres = arrays[0].shape
    size = max(HALO, rows // 5)
    message = in_vmem((PARTS, specs, exposures, fibres))
    return pl.pallas_call(
        edge_kernel,
        out_shape=(message, message, in_vmem((4, size, specs, exposures, fibres))),
        in_specs=[HB] * 5,
        out_specs=(VM, VM, VM),
        scratch_shapes=[
            pltpu.VMEM((4, HALO, specs, exposures, fibres), F32),
            pltpu.VMEM((size, specs, exposures, fibres), jnp.int32),
            pltpu.VMEM((HALO, specs, exposures, fibres), jnp.int32),
            pltpu.SemaphoreType.DMA((4,)),
        ],
        compiler_params=pltpu.CompilerParams(vmem_limit_bytes=8 * 2**20),
        cost_estimate=pl.CostEstimate(flops=10**6, bytes_accessed=10**6, transcendentals=0),
        name="edges",
    )(*arrays)


def forward_kernel(
    chunks, near, head, pix, iva, msk, lef, rig, sky_index, lower, lower_far, half, shares, tail, sky_mask, denom, bufs, mbuf, sems
):
    exposures, rows, specs, fibres = pix.shape
    size = head.shape[1]
    odd = lax.rem(lax.axis_index("wave"), 2)
    spans = range(specs)
    bounds = [0] + [size + (rows - size) * c // chunks for c in range(chunks + 1)]

    def place(low, high):
        return pl.ds(odd * low + (1 - odd) * (rows - high), high - low)

    for c in range(1, chunks + 1):
        here = place(bounds[c], bounds[c + 1])
        for e in range(exposures):
            for slot, ref in enumerate((pix, iva, lef, rig)):
                pltpu.make_async_copy(
                    ref.at[e, here], bufs.at[slot, here, :, e], sems.at[0, c - 1]
                ).start()
            pltpu.make_async_copy(msk.at[e, here], mbuf.at[here, :, e], sems.at[1, c - 1]).start()
    lane = lax.broadcasted_iota(jnp.int32, (exposures, fibres), 1)
    for s in spans:
        found = lane == sky_index[s, 0]
        for k in range(1, sky_index.shape[1]):
            found = found | (lane == sky_index[s, k])
        sky_mask[s] = jnp.where(found, 1.0, 0.0)

    spot = lax.broadcasted_iota(jnp.int32, (exposures, LANES), 1)
    before, after = 3 - odd, 2 + odd

    def share(k, parts, total):
        parts = [sky_mask[s] * parts[s] for s in spans]
        for s in spans:
            shares[k, s] = parts[s]
        row = odd * k + (1 - odd) * (rows - 1 - k)
        return jnp.where(spot == row, jnp.sum(sum(parts), axis=1, keepdims=True), total)

    made = [dict(d1=REG, b1=0.0, d2=REG, b2=0.0, r1=0.0) for _ in spans]
    offs = [[] for _ in spans]
    fars = [[] for _ in spans]
    states = [None] * specs
    total = jnp.zeros((exposures, LANES), F32)
    for c in range(chunks + 1):
        if c > 0:
            here = place(bounds[c], bounds[c + 1])
            part, mpart = bufs.at[:, here], mbuf.at[here]
            pltpu.make_async_copy(part, part, sems.at[0, c - 1]).wait()
            pltpu.make_async_copy(mpart, mpart, sems.at[1, c - 1]).wait()
        for k in range(bounds[c], bounds[c + 1]):
            row = odd * k + (1 - odd) * (rows - 1 - k)
            top = odd * k + (1 - odd) * (size - 1 - k)
            diags = []
            for s in spans:
                if c == 0:
                    p, w, l, r = [head[slot, top, s] for slot in (0, 1, before, after)]
                else:
                    p, l, r = bufs[0, row, s], bufs[before, row, s], bufs[after, row, s]
                    w = weight_of(bufs[1, row, s], mbuf[row, s])
                wl, wr, wp = w * l, w * r, w * p
                m = made[s]
                d, b = m["d1"] + wl * l, m["b1"] + wl * p
                offs[s].append(m["r1"] + wl)
                fars[s].append(wl * r)
                made[s] = dict(
                    d1=w + m["d2"], b1=wp + m["b2"], d2=wr * r + REG, b2=wr * p, r1=wr
                )
                if k == 0:
                    d, b = d + near[0, s], b + near[3, s]
                    offs[s][0] = offs[s][0] + near[1, s]
                    inv = recip(d)
                    states[s] = (inv, None, None, b, None)
                elif k == 1:
                    diags.append(d + near[5, s])
                    d, b = d + near[2, s], b + near[4, s]
                    inv1, _, _, y1, _ = states[s]
                    upper = offs[s][0]
                    g = upper * inv1
                    inv, y = recip(d - g * upper), b - g * y1
                    lower[1, s], half[1, s] = g, y * inv
                    states[s] = (inv, inv1, g, y, y1)
                else:
                    diags.append(d)
                    f, g, y, states[s] = eliminate(states[s], d, offs[s][k - 1], b, fars[s][k - 2])
                    lower_far[k, s], lower[k, s], half[k, s] = f, g, y * states[s][0]
            if k > 0:
                total = share(k - 1, diags, total)
    for s in spans:
        m = made[s]
        tail_parts = states[s] + (
            m["d1"], offs[s][rows - 1], m["b1"], fars[s][rows - 2], m["d2"], m["r1"], m["b2"], fars[s][rows - 1]
        )
        for slot, value in enumerate(tail_parts):
            tail[slot, s] = value
    denom[...] = share(rows - 1, [made[s]["d1"] for s in spans], total)


TAIL = 13


def eliminate(state, d, a, b, far_a):
    inv1, inv2, mult1, y1, y2 = state
    f = far_a * inv2
    upper = a - far_a * mult1
    g = upper * inv1
    pivot = d - f * far_a - g * upper
    y = b - f * y2 - g * y1
    return f, g, y, (recip(pivot), inv1, g, y, y1)


def forward_call(near, head, arrays, sky_index):
    exposures, rows, specs, fibres = arrays[0].shape
    chunks = 4
    whole = in_vmem((rows, specs, exposures, fibres))
    return pl.pallas_call(
        functools.partial(forward_kernel, chunks),
        out_shape=(
            whole,
            whole,
            whole,
            whole,
            in_vmem((TAIL, specs, exposures, fibres)),
            in_vmem((specs, exposures, fibres)),
            in_vmem((exposures, LANES)),
        ),
        in_specs=[VM] * 2 + [HB] * 5 + [SM],
        out_specs=(VM,) * 7,
        scratch_shapes=[
            pltpu.VMEM((4, rows, specs, exposures, fibres), F32),
            pltpu.VMEM((rows, specs, exposures, fibres), jnp.int32),
            pltpu.SemaphoreType.DMA((2, chunks)),
        ],
        compiler_params=pltpu.CompilerParams(vmem_limit_bytes=24 * 2**20),
        cost_estimate=pl.CostEstimate(flops=10**7, bytes_accessed=10**7, transcendentals=0),
        name="forward",
    )(near, head, *arrays, sky_index)


def backward_kernel(wave, far, lower, lower_far, half, shares, tail, sky_mask, denom, flux, sums):
    rows, specs, exposures, fibres = lower.shape
    device = lax.axis_index("wave")
    odd = lax.rem(device, 2)
    at_end = (device == 0) | (device == wave - 1)
    lane = lax.broadcasted_iota(jnp.int32, (exposures, LANES), 1)
    spans = range(specs)

    def message(part, s):
        return jnp.where(at_end, 0.0, far[part, s])

    def place(k):
        return odd * k + (1 - odd) * (rows - 1 - k)

    def total(parts):
        return jnp.sum(parts, axis=1, keepdims=True)

    def spread(k, numer, parts, values):
        return jnp.where(lane == place(k), total(sum(parts[s] * values[s] for s in spans)), numer)

    after, extra = [], []
    for s in spans:
        t = [tail[slot, s] for slot in range(TAIL)]
        f, g, y, state = eliminate(t[:5], t[5] + message(2, s), t[6], t[7] + message(4, s), t[8])
        f1, g1, y1, last = eliminate(
            state, t[9] + message(0, s), t[10] + message(1, s), t[11] + message(3, s), t[12]
        )
        beyond = y1 * last[0]
        value = y * state[0] - g1 * beyond
        flux[place(rows - 1), s] = value
        after.append((value, beyond, g, f1, f))
        extra.append(sky_mask[s] * message(5, s))
    parts = [shares[rows - 1, s] + extra[s] for s in spans]
    numer = jnp.zeros((exposures, LANES), F32)
    numer = spread(rows - 1, numer, parts, [after[s][0] for s in spans])
    sums[1] = denom[...] + jnp.where(lane == place(rows - 1), total(sum(extra)), 0.0)

    def step(k, numer, after, bottom=False):
        results = []
        for s in spans:
            x1, x2, g1, f2, f1 = after[s]
            value = half[k, s] - g1 * x1 - f2 * x2
            flux[place(k - 1), s] = value
            results.append((value, x1) if bottom else (value, x1, lower[k, s], f1, lower_far[k, s]))
        parts = [shares[k - 1, s] for s in spans]
        return spread(k - 1, numer, parts, [r[0] for r in results]), tuple(results)

    for k in range(rows - 1, 1, -1):
        numer, after = step(k, numer, after)
    numer, after = step(1, numer, after, bottom=True)
    sums[0] = numer


def backward_call(wave, far, factors):
    rows, specs, exposures, fibres = factors[0].shape
    return pl.pallas_call(
        functools.partial(backward_kernel, wave),
        out_shape=(in_vmem((rows, specs, exposures, fibres)), in_vmem((2, exposures, LANES))),
        in_specs=[VM] * 8,
        out_specs=(VM, VM),
        compiler_params=pltpu.CompilerParams(vmem_limit_bytes=24 * 2**20),
        cost_estimate=pl.CostEstimate(flops=10**7, bytes_accessed=10**7, transcendentals=0),
        name="backward",
    )(far, *factors)


def position_of(index, total_rows):
    return 2.0 * jnp.asarray(index).astype(F32) / (total_rows - 1) - 1.0


def regress_kernel(total_rows, flux, other, sums, regress, sky_out):
    rows, specs, exposures, fibres = flux.shape
    lanes = regress.shape[2]
    device = lax.axis_index("wave")
    odd = lax.rem(device, 2)
    lane = lax.broadcasted_iota(jnp.int32, (exposures, LANES), 1)
    valid = lane < rows
    step = 2.0 / (total_rows - 1)
    plain = [0.0] * specs
    tilted = [0.0] * specs
    moments = [0.0] * 3
    for which, (ref, core) in enumerate(((flux, odd), (other, 1 - odd))):
        owner = device - odd + core
        sky = jnp.where(valid, sums[2 * core] / jnp.where(valid, sums[2 * core + 1], 1.0), 0.0)
        position = position_of(owner * rows + lane, total_rows)
        slanted = sky * position
        moments[0] += jnp.sum(sky * sky, axis=1, keepdims=True)
        moments[1] += jnp.sum(sky * slanted, axis=1, keepdims=True)
        moments[2] += jnp.sum(slanted * slanted, axis=1, keepdims=True)
        if which == 0:
            sky_out[...] = sky
        end = position_of(owner * rows + rows, total_rows)
        running = [None] * specs
        summed = [None] * specs
        for k in range(rows):
            sky_k = jnp.broadcast_to(sky[:, k : k + 1], (exposures, fibres))
            for s in range(specs):
                term = ref[k, s] * sky_k
                running[s] = term if k == 0 else running[s] + term
                summed[s] = running[s] if k == 0 else summed[s] + running[s]
        for s in range(specs):
            plain[s] += running[s]
            tilted[s] += end * running[s] - step * summed[s]
    wide = lax.broadcasted_iota(jnp.int32, (exposures, lanes - fibres), 1)
    held = jnp.where(wide == 0, moments[0], jnp.where(wide == 1, moments[1], moments[2]))
    for s in range(specs):
        regress[s, :, :fibres] = plain[s]
        regress[specs + s, :, :fibres] = tilted[s]
        for r in (s, specs + s):
            regress[r, :, fibres:] = held


def regress_call(total_rows, flux, other, sums):
    rows, specs, exposures, fibres = flux.shape
    lanes = -(-(fibres + 3) // LANES) * LANES
    return pl.pallas_call(
        functools.partial(regress_kernel, total_rows),
        out_shape=(
            in_vmem((2 * specs, exposures, lanes)),
            in_vmem((exposures, LANES)),
        ),
        in_specs=[VM] * 3,
        out_specs=(VM, VM),
        compiler_params=pltpu.CompilerParams(vmem_limit_bytes=24 * 2**20),
        cost_estimate=pl.CostEstimate(flops=10**6, bytes_accessed=10**6, transcendentals=0),
        name="regress",
    )(flux, other, sums)


def clean_kernel(total_rows, flux, sky_ref, *refs):
    *terms, out, sky_out, buf, sems, sky_sem = refs
    rows, specs, exposures, fibres = flux.shape
    sky_copy = pltpu.make_async_copy(sky_ref, sky_out, sky_sem)
    sky_copy.start()
    device = lax.axis_index("wave")

    def got(slot):
        return sum(term[slot] for term in terms)

    sums = [got(slot) for slot in range(2 * specs)]
    moments = [sums[0][:, fibres + m : fibres + m + 1] for m in range(3)]
    upper_left, cross, lower_right = moments[0] + RIDGE, moments[1], moments[2] + RIDGE
    inverse = 1.0 / (upper_left * lower_right - cross * cross)
    start = position_of(device * rows, total_rows)
    step = 2.0 / (total_rows - 1)
    level, change = [], []
    for s in range(specs):
        r1, r2 = sums[s][:, :fibres], sums[specs + s][:, :fibres]
        slope_a = (lower_right * r1 - cross * r2) * inverse
        slope_b = (upper_left * r2 - cross * r1) * inverse
        level.append(slope_a + slope_b * start)
        change.append(slope_b * step)
    sky = sky_ref[...]
    chunks = sems.shape[0]
    bounds = [rows * c // chunks for c in range(chunks + 1)]
    for c in range(chunks):
        low, high = bounds[c], bounds[c + 1]
        for k in range(low, high):
            sky_k = jnp.broadcast_to(sky[:, k : k + 1], (exposures, fibres))
            for s in range(specs):
                buf[k, s] = flux[k, s] - level[s] * sky_k
                level[s] = level[s] + change[s]
        for e in range(exposures):
            pltpu.make_async_copy(
                buf.at[low:high, :, e], out.at[e, low:high], sems.at[c]
            ).start()
    for c in range(chunks):
        part = buf.at[bounds[c] : bounds[c + 1]]
        pltpu.make_async_copy(part, part, sems.at[c]).wait()
    sky_copy.wait()


def clean_call(total_rows, flux, sky, terms):
    rows, specs, exposures, fibres = flux.shape
    return pl.pallas_call(
        functools.partial(clean_kernel, total_rows),
        out_shape=(
            jax.ShapeDtypeStruct((exposures, rows, specs, fibres), F32),
            jax.ShapeDtypeStruct((exposures, LANES), F32),
        ),
        in_specs=[VM] * (2 + len(terms)),
        out_specs=(HB, HB),
        scratch_shapes=[
            pltpu.VMEM((rows, specs, exposures, fibres), F32),
            pltpu.SemaphoreType.DMA((4,)),
            pltpu.SemaphoreType.DMA,
        ],
        compiler_params=pltpu.CompilerParams(vmem_limit_bytes=24 * 2**20),
        cost_estimate=pl.CostEstimate(flops=10**6, bytes_accessed=10**6, transcendentals=0),
        name="clean",
    )(flux, sky, *terms)


def powers(low, high):
    steps = []
    while low < high:
        steps.append(low)
        low *= 2
    return steps


def swap(values, partner):
    spec, wave = lax.axis_size("spec"), lax.axis_size("wave")
    pairs = []
    for s in range(spec):
        for i in range(wave):
            t, j = partner(s, i)
            if not 0 <= j < wave:
                t, j = s ^ 1, i
            if t < spec:
                pairs.append((s * wave + i, t * wave + j))
    return lax.ppermute(values, ("spec", "wave"), pairs)


def local(pixels, ivar, mask, psf_left, psf_right, sky_index):
    arrays = [jnp.transpose(x, (0, 2, 1, 3)) for x in (pixels, ivar, mask, psf_left, psf_right)]
    rows = pixels.shape[2]
    wave, spec = lax.axis_size("wave"), lax.axis_size("spec")
    total_rows = rows * wave
    hbm = [pltpu.with_memory_space_constraint(x, pltpu.HBM) for x in arrays]
    odd = lax.rem(lax.axis_index("wave"), 2) == 1

    def other_core(s, i):
        return (s, i ^ 1)

    near, far, head = edge_call(hbm)
    far = swap(far, lambda s, i: (s, i + 1 if i % 2 else i - 1))
    near = swap(near, other_core)
    factors = forward_call(near, head, hbm, sky_index)
    flux, sums = backward_call(wave, far, factors)
    got = swap(sums, other_core)
    flux, got = lax.optimization_barrier((flux, got))
    other = swap(flux, other_core)
    sums = jnp.where(odd, jnp.concatenate([got, sums]), jnp.concatenate([sums, got]))
    if spec == 4:
        first = swap(sums, lambda s, i: (s ^ (1 if i % 2 else 2), i))
        third = swap(sums, lambda s, i: (s ^ 3, i ^ 1))
        second = swap(first, other_core)
        sums = (sums + jnp.where(odd, first, second)) + (jnp.where(odd, second, first) + third)
    else:
        for k in powers(1, spec):
            sums = sums + swap(sums, lambda s, i: (s ^ k, i))
    regress, sky = regress_call(total_rows, flux, other, sums)
    if wave == 8:
        third = swap(regress, lambda s, i: (s, i ^ 6 if i % 2 else -1))
        first = swap(regress, lambda s, i: (s, i ^ (4 if i % 2 else 2)))
        fetched = jnp.where(odd, third, 0.0) + first
        terms = [regress, fetched, swap(fetched, other_core)]
    else:
        for k in powers(2, wave):
            regress = regress + swap(regress, lambda s, i: (s, i ^ k if i % 2 else -1))
        terms = [jnp.where(odd, regress, swap(regress, other_core))]
    cleaned, sky = clean_call(total_rows, flux, sky, terms)
    return (jnp.transpose(cleaned, (0, 2, 1, 3)), sky[:, :rows])


def solution(mesh):
    block = P(None, "spec", "wave", None)
    return jax.shard_map(
        local,
        mesh=mesh,
        in_specs=(block,) * 5 + (P("spec", None),),
        out_specs=(block, P(None, "wave")),
        check_vma=False,
    )
```

```python
import functools

import jax
import jax.numpy as jnp
from jax import lax
from jax.experimental import pallas as pl
from jax.experimental.pallas import tpu as pltpu
from jax.sharding import PartitionSpec as P

REG = 0.05
RIDGE = 1.0
HALO = 4
PARTS = 6
TAIL = 13
CUTS = (0, 14, 26, 35, 40)
LANES = 128

F32 = jnp.float32
VM = pl.BlockSpec(memory_space=pltpu.VMEM)
SM = pl.BlockSpec(memory_space=pltpu.SMEM)
HB = pl.BlockSpec(memory_space=pltpu.HBM)


def in_vmem(shape, dtype=F32):
    return jax.ShapeDtypeStruct(shape, dtype)


def recip(values):
    return 1.0 / values


def weight_of(ivar, mask):
    return jnp.where(mask == 0, ivar, 0.0)


def edge_message(p, w, l, r):
    wl = [a * b for a, b in zip(w, l)]
    wr = [a * b for a, b in zip(w, r)]
    d0 = w[0] + wl[1] * l[1] + REG
    d1 = w[1] + wr[0] * r[0] + wl[2] * l[2] + REG
    d2 = w[2] + wr[1] * r[1] + wl[3] * l[3] + REG
    d3 = w[3] + wr[2] * r[2]
    d4 = wr[3] * r[3]
    raw = d4
    a01 = wr[0] + wl[1]
    a12 = wr[1] + wl[2]
    a23 = wr[2] + wl[3]
    a34 = wr[3]
    a02 = wl[1] * r[1]
    a13 = wl[2] * r[2]
    a24 = wl[3] * r[3]
    b0 = w[0] * p[0] + wl[1] * p[1]
    b1 = w[1] * p[1] + wr[0] * p[0] + wl[2] * p[2]
    b2 = w[2] * p[2] + wr[1] * p[1] + wl[3] * p[3]
    b3 = w[3] * p[3] + wr[2] * p[2]
    b4 = wr[3] * p[3]
    inv = recip(d0)
    near, far = a01 * inv, a02 * inv
    d1, a12, d2 = d1 - near * a01, a12 - near * a02, d2 - far * a02
    b1, b2 = b1 - near * b0, b2 - far * b0
    inv = recip(d1)
    near, far = a12 * inv, a13 * inv
    d2, a23, d3 = d2 - near * a12, a23 - near * a13, d3 - far * a13
    b2, b3 = b2 - near * b1, b3 - far * b1
    inv = recip(d2)
    near, far = a23 * inv, a24 * inv
    d3, a34, d4 = d3 - near * a23, a34 - near * a24, d4 - far * a24
    b3, b4 = b3 - near * b2, b4 - far * b2
    return (d3, a34, d4, b3, b4, raw)


def edge_kernel(pix, iva, msk, lef, rig, near_out, far_out, head, bufs, mhead, mbuf, sems):
    exposures, rows, specs, fibres = pix.shape
    size = head.shape[1]
    odd = lax.rem(lax.axis_index("wave"), 2)
    first, last = (1 - odd) * (rows - size), odd * (rows - HALO)
    for e in range(exposures):
        for slot, ref in enumerate((pix, iva, lef, rig)):
            pltpu.make_async_copy(
                ref.at[e, pl.ds(first, size)], head.at[slot, :, :, e], sems.at[0]
            ).start()
        pltpu.make_async_copy(msk.at[e, pl.ds(first, size)], mhead.at[:, :, e], sems.at[1]).start()
    for e in range(exposures):
        for slot, ref in enumerate((pix, iva, lef, rig)):
            pltpu.make_async_copy(
                ref.at[e, pl.ds(last, HALO)], bufs.at[slot, :, :, e], sems.at[2]
            ).start()
        pltpu.make_async_copy(msk.at[e, pl.ds(last, HALO)], mbuf.at[:, :, e], sems.at[3]).start()
    before, after = 3 - odd, 2 + odd
    pltpu.make_async_copy(head, head, sems.at[0]).wait()
    pltpu.make_async_copy(mhead, mhead, sems.at[1]).wait()
    for k in range(size):
        for s in range(specs):
            head[1, k, s] = weight_of(head[1, k, s], mhead[k, s])
    order = [odd * k + (1 - odd) * (size - 1 - k) for k in range(HALO - 1, -1, -1)]
    for s in range(specs):
        p, w, l, r = [[head[slot, k, s] for k in order] for slot in (0, 1, before, after)]
        for slot, value in enumerate(edge_message(p, w, r, l)):
            near_out[slot, s] = value
    pltpu.make_async_copy(bufs, bufs, sems.at[2]).wait()
    pltpu.make_async_copy(mbuf, mbuf, sems.at[3]).wait()
    order = [odd * k + (1 - odd) * (HALO - 1 - k) for k in range(HALO)]
    for s in range(specs):
        p, l, r = [[bufs[slot, k, s] for k in order] for slot in (0, before, after)]
        w = [weight_of(bufs[1, k, s], mbuf[k, s]) for k in order]
        for slot, value in enumerate(edge_message(p, w, l, r)):
            far_out[slot, s] = value


def edge_call(arrays):
    exposures, rows, specs, fibres = arrays[0].shape
    size = max(HALO, rows // 5)
    message = in_vmem((PARTS, specs, exposures, fibres))
    return pl.pallas_call(
        edge_kernel,
        out_shape=(message, message, in_vmem((4, size, specs, exposures, fibres))),
        in_specs=[HB] * 5,
        out_specs=(VM, VM, VM),
        scratch_shapes=[
            pltpu.VMEM((4, HALO, specs, exposures, fibres), F32),
            pltpu.VMEM((size, specs, exposures, fibres), jnp.int32),
            pltpu.VMEM((HALO, specs, exposures, fibres), jnp.int32),
            pltpu.SemaphoreType.DMA((4,)),
        ],
        compiler_params=pltpu.CompilerParams(vmem_limit_bytes=8 * 2**20),
        cost_estimate=pl.CostEstimate(flops=10**6, bytes_accessed=10**6, transcendentals=0),
        name="edges",
    )(*arrays)


def forward_kernel(
    near, head, pix, iva, msk, lef, rig, sky_index, lower, lower_far, half, shares, tail, sky_mask, denom, bufs, mbuf, sems
):
    exposures, rows, specs, fibres = pix.shape
    size = head.shape[1]
    odd = lax.rem(lax.axis_index("wave"), 2)
    spans = range(specs)
    bounds = [0] + [size + (rows - size) * part // 40 for part in CUTS]

    def place(low, high):
        return pl.ds(odd * low + (1 - odd) * (rows - high), high - low)

    for c in range(1, len(CUTS)):
        here = place(bounds[c], bounds[c + 1])
        for e in range(exposures):
            for slot, ref in enumerate((pix, iva, lef, rig)):
                pltpu.make_async_copy(
                    ref.at[e, here], bufs.at[slot, here, :, e], sems.at[0, c - 1]
                ).start()
            pltpu.make_async_copy(msk.at[e, here], mbuf.at[here, :, e], sems.at[1, c - 1]).start()
    lane = lax.broadcasted_iota(jnp.int32, (exposures, fibres), 1)
    for s in spans:
        found = lane == sky_index[s, 0]
        for k in range(1, sky_index.shape[1]):
            found = found | (lane == sky_index[s, k])
        sky_mask[s] = jnp.where(found, 1.0, 0.0)

    spot = lax.broadcasted_iota(jnp.int32, (exposures, LANES), 1)
    before, after = 3 - odd, 2 + odd

    def share(k, parts, total):
        parts = [sky_mask[s] * parts[s] for s in spans]
        for s in spans:
            shares[k, s] = parts[s]
        row = odd * k + (1 - odd) * (rows - 1 - k)
        return jnp.where(spot == row, jnp.sum(sum(parts), axis=1, keepdims=True), total)

    made = [dict(d1=REG, b1=0.0, d2=REG, b2=0.0, r1=0.0) for _ in spans]
    offs = [[] for _ in spans]
    fars = [[] for _ in spans]
    states = [None] * specs
    total = jnp.zeros((exposures, LANES), F32)
    for c in range(len(CUTS)):
        if c > 0:
            here = place(bounds[c], bounds[c + 1])
            part, mpart = bufs.at[:, here], mbuf.at[here]
            pltpu.make_async_copy(part, part, sems.at[0, c - 1]).wait()
            pltpu.make_async_copy(mpart, mpart, sems.at[1, c - 1]).wait()
        for k in range(bounds[c], bounds[c + 1]):
            row = odd * k + (1 - odd) * (rows - 1 - k)
            top = odd * k + (1 - odd) * (size - 1 - k)
            diags = []
            for s in spans:
                if c == 0:
                    p, w, l, r = [head[slot, top, s] for slot in (0, 1, before, after)]
                else:
                    p, l, r = bufs[0, row, s], bufs[before, row, s], bufs[after, row, s]
                    w = weight_of(bufs[1, row, s], mbuf[row, s])
                wl, wr, wp = w * l, w * r, w * p
                m = made[s]
                d, b = m["d1"] + wl * l, m["b1"] + wl * p
                offs[s].append(m["r1"] + wl)
                fars[s].append(wl * r)
                made[s] = dict(
                    d1=w + m["d2"], b1=wp + m["b2"], d2=wr * r + REG, b2=wr * p, r1=wr
                )
                if k == 0:
                    d, b = d + near[0, s], b + near[3, s]
                    offs[s][0] = offs[s][0] + near[1, s]
                    inv = recip(d)
                    states[s] = (inv, None, None, b, None)
                elif k == 1:
                    diags.append(d + near[5, s])
                    d, b = d + near[2, s], b + near[4, s]
                    inv1, _, _, y1, _ = states[s]
                    upper = offs[s][0]
                    g = upper * inv1
                    inv, y = recip(d - g * upper), b - g * y1
                    lower[1, s], half[1, s] = g, y * inv
                    states[s] = (inv, inv1, g, y, y1)
                else:
                    diags.append(d)
                    f, g, y, states[s] = eliminate(states[s], d, offs[s][k - 1], b, fars[s][k - 2])
                    lower_far[k, s], lower[k, s], half[k, s] = f, g, y * states[s][0]
            if k > 0:
                total = share(k - 1, diags, total)
    for s in spans:
        m = made[s]
        tail_parts = states[s] + (
            m["d1"], offs[s][rows - 1], m["b1"], fars[s][rows - 2], m["d2"], m["r1"], m["b2"], fars[s][rows - 1]
        )
        for slot, value in enumerate(tail_parts):
            tail[slot, s] = value
    denom[...] = share(rows - 1, [made[s]["d1"] for s in spans], total)


def eliminate(state, d, a, b, far_a):
    inv1, inv2, mult1, y1, y2 = state
    f = far_a * inv2
    upper = a - far_a * mult1
    g = upper * inv1
    pivot = d - f * far_a - g * upper
    y = b - f * y2 - g * y1
    return f, g, y, (recip(pivot), inv1, g, y, y1)


def forward_call(near, head, arrays, sky_index):
    exposures, rows, specs, fibres = arrays[0].shape
    chunks = len(CUTS) - 1
    whole = in_vmem((rows, specs, exposures, fibres))
    return pl.pallas_call(
        forward_kernel,
        out_shape=(
            whole,
            whole,
            whole,
            whole,
            in_vmem((TAIL, specs, exposures, fibres)),
            in_vmem((specs, exposures, fibres)),
            in_vmem((exposures, LANES)),
        ),
        in_specs=[VM] * 2 + [HB] * 5 + [SM],
        out_specs=(VM,) * 7,
        scratch_shapes=[
            pltpu.VMEM((4, rows, specs, exposures, fibres), F32),
            pltpu.VMEM((rows, specs, exposures, fibres), jnp.int32),
            pltpu.SemaphoreType.DMA((2, chunks)),
        ],
        compiler_params=pltpu.CompilerParams(vmem_limit_bytes=24 * 2**20),
        cost_estimate=pl.CostEstimate(flops=10**7, bytes_accessed=10**7, transcendentals=0),
        name="forward",
    )(near, head, *arrays, sky_index)


def backward_kernel(wave, far, lower, lower_far, half, shares, tail, sky_mask, denom, flux, sums):
    rows, specs, exposures, fibres = lower.shape
    device = lax.axis_index("wave")
    odd = lax.rem(device, 2)
    at_end = (device == 0) | (device == wave - 1)
    lane = lax.broadcasted_iota(jnp.int32, (exposures, LANES), 1)
    spans = range(specs)

    def message(part, s):
        return jnp.where(at_end, 0.0, far[part, s])

    def place(k):
        return odd * k + (1 - odd) * (rows - 1 - k)

    def total(parts):
        return jnp.sum(parts, axis=1, keepdims=True)

    def spread(k, numer, parts, values):
        return jnp.where(lane == place(k), total(sum(parts[s] * values[s] for s in spans)), numer)

    after, extra = [], []
    for s in spans:
        t = [tail[slot, s] for slot in range(TAIL)]
        f, g, y, state = eliminate(t[:5], t[5] + message(2, s), t[6], t[7] + message(4, s), t[8])
        f1, g1, y1, last = eliminate(
            state, t[9] + message(0, s), t[10] + message(1, s), t[11] + message(3, s), t[12]
        )
        beyond = y1 * last[0]
        value = y * state[0] - g1 * beyond
        flux[place(rows - 1), s] = value
        after.append((value, beyond, g, f1, f))
        extra.append(sky_mask[s] * message(5, s))
    parts = [shares[rows - 1, s] + extra[s] for s in spans]
    numer = jnp.zeros((exposures, LANES), F32)
    numer = spread(rows - 1, numer, parts, [after[s][0] for s in spans])
    sums[1] = denom[...] + jnp.where(lane == place(rows - 1), total(sum(extra)), 0.0)

    def step(k, numer, after, bottom=False):
        results = []
        for s in spans:
            x1, x2, g1, f2, f1 = after[s]
            value = half[k, s] - g1 * x1 - f2 * x2
            flux[place(k - 1), s] = value
            results.append((value, x1) if bottom else (value, x1, lower[k, s], f1, lower_far[k, s]))
        parts = [shares[k - 1, s] for s in spans]
        return spread(k - 1, numer, parts, [r[0] for r in results]), tuple(results)

    for k in range(rows - 1, 1, -1):
        numer, after = step(k, numer, after)
    numer, after = step(1, numer, after, bottom=True)
    sums[0] = numer


def backward_call(wave, far, factors):
    rows, specs, exposures, fibres = factors[0].shape
    return pl.pallas_call(
        functools.partial(backward_kernel, wave),
        out_shape=(in_vmem((rows, specs, exposures, fibres)), in_vmem((2, exposures, LANES))),
        in_specs=[VM] * 8,
        out_specs=(VM, VM),
        compiler_params=pltpu.CompilerParams(vmem_limit_bytes=24 * 2**20),
        cost_estimate=pl.CostEstimate(flops=10**7, bytes_accessed=10**7, transcendentals=0),
        name="backward",
    )(far, *factors)


def position_of(index, total_rows):
    return 2.0 * jnp.asarray(index).astype(F32) / (total_rows - 1) - 1.0


def regress_kernel(total_rows, flux, other, sums, regress, sky_out):
    rows, specs, exposures, fibres = flux.shape
    lanes = regress.shape[2]
    device = lax.axis_index("wave")
    odd = lax.rem(device, 2)
    lane = lax.broadcasted_iota(jnp.int32, (exposures, LANES), 1)
    valid = lane < rows
    step = 2.0 / (total_rows - 1)
    plain = [0.0] * specs
    tilted = [0.0] * specs
    moments = [0.0] * 3
    for which, (ref, core) in enumerate(((flux, odd), (other, 1 - odd))):
        owner = device - odd + core
        sky = jnp.where(valid, sums[2 * core] / jnp.where(valid, sums[2 * core + 1], 1.0), 0.0)
        position = position_of(owner * rows + lane, total_rows)
        slanted = sky * position
        moments[0] += jnp.sum(sky * sky, axis=1, keepdims=True)
        moments[1] += jnp.sum(sky * slanted, axis=1, keepdims=True)
        moments[2] += jnp.sum(slanted * slanted, axis=1, keepdims=True)
        if which == 0:
            sky_out[...] = sky
        end = position_of(owner * rows + rows, total_rows)
        running = [None] * specs
        summed = [None] * specs
        for k in range(rows):
            sky_k = jnp.broadcast_to(sky[:, k : k + 1], (exposures, fibres))
            for s in range(specs):
                term = ref[k, s] * sky_k
                running[s] = term if k == 0 else running[s] + term
                summed[s] = running[s] if k == 0 else summed[s] + running[s]
        for s in range(specs):
            plain[s] += running[s]
            tilted[s] += end * running[s] - step * summed[s]
    wide = lax.broadcasted_iota(jnp.int32, (exposures, lanes - fibres), 1)
    held = jnp.where(wide == 0, moments[0], jnp.where(wide == 1, moments[1], moments[2]))
    for s in range(specs):
        regress[s, :, :fibres] = plain[s]
        regress[specs + s, :, :fibres] = tilted[s]
        for r in (s, specs + s):
            regress[r, :, fibres:] = held


def regress_call(total_rows, flux, other, sums):
    rows, specs, exposures, fibres = flux.shape
    lanes = -(-(fibres + 3) // LANES) * LANES
    return pl.pallas_call(
        functools.partial(regress_kernel, total_rows),
        out_shape=(
            in_vmem((2 * specs, exposures, lanes)),
            in_vmem((exposures, LANES)),
        ),
        in_specs=[VM] * 3,
        out_specs=(VM, VM),
        compiler_params=pltpu.CompilerParams(vmem_limit_bytes=24 * 2**20),
        cost_estimate=pl.CostEstimate(flops=10**6, bytes_accessed=10**6, transcendentals=0),
        name="regress",
    )(flux, other, sums)


def clean_kernel(total_rows, flux, sky_ref, *refs):
    *terms, out, sky_out, buf, sems, sky_sem = refs
    rows, specs, exposures, fibres = flux.shape
    sky_copy = pltpu.make_async_copy(sky_ref, sky_out, sky_sem)
    sky_copy.start()
    device = lax.axis_index("wave")

    def got(slot):
        return sum(term[slot] for term in terms)

    sums = [got(slot) for slot in range(2 * specs)]
    moments = [sums[0][:, fibres + m : fibres + m + 1] for m in range(3)]
    upper_left, cross, lower_right = moments[0] + RIDGE, moments[1], moments[2] + RIDGE
    inverse = 1.0 / (upper_left * lower_right - cross * cross)
    start = position_of(device * rows, total_rows)
    step = 2.0 / (total_rows - 1)
    level, change = [], []
    for s in range(specs):
        r1, r2 = sums[s][:, :fibres], sums[specs + s][:, :fibres]
        slope_a = (lower_right * r1 - cross * r2) * inverse
        slope_b = (upper_left * r2 - cross * r1) * inverse
        level.append(slope_a + slope_b * start)
        change.append(slope_b * step)
    sky = sky_ref[...]
    chunks = sems.shape[0]
    bounds = [rows * c // chunks for c in range(chunks + 1)]
    for c in range(chunks):
        low, high = bounds[c], bounds[c + 1]
        for k in range(low, high):
            sky_k = jnp.broadcast_to(sky[:, k : k + 1], (exposures, fibres))
            for s in range(specs):
                buf[k, s] = flux[k, s] - level[s] * sky_k
                level[s] = level[s] + change[s]
        for e in range(exposures):
            pltpu.make_async_copy(
                buf.at[low:high, :, e], out.at[e, low:high], sems.at[c]
            ).start()
    for c in range(chunks):
        part = buf.at[bounds[c] : bounds[c + 1]]
        pltpu.make_async_copy(part, part, sems.at[c]).wait()
    sky_copy.wait()


def clean_call(total_rows, flux, sky, terms):
    rows, specs, exposures, fibres = flux.shape
    return pl.pallas_call(
        functools.partial(clean_kernel, total_rows),
        out_shape=(
            jax.ShapeDtypeStruct((exposures, rows, specs, fibres), F32),
            jax.ShapeDtypeStruct((exposures, LANES), F32),
        ),
        in_specs=[VM] * (2 + len(terms)),
        out_specs=(HB, HB),
        scratch_shapes=[
            pltpu.VMEM((rows, specs, exposures, fibres), F32),
            pltpu.SemaphoreType.DMA((4,)),
            pltpu.SemaphoreType.DMA,
        ],
        compiler_params=pltpu.CompilerParams(vmem_limit_bytes=24 * 2**20),
        cost_estimate=pl.CostEstimate(flops=10**6, bytes_accessed=10**6, transcendentals=0),
        name="clean",
    )(flux, sky, *terms)


def powers(low, high):
    steps = []
    while low < high:
        steps.append(low)
        low *= 2
    return steps


def swap(values, partner):
    spec, wave = lax.axis_size("spec"), lax.axis_size("wave")
    pairs = []
    for s in range(spec):
        for i in range(wave):
            t, j = partner(s, i)
            if not 0 <= j < wave:
                t, j = s ^ 1, i
            if t < spec:
                pairs.append((s * wave + i, t * wave + j))
    return lax.ppermute(values, ("spec", "wave"), pairs)


def local(pixels, ivar, mask, psf_left, psf_right, sky_index):
    arrays = [jnp.transpose(x, (0, 2, 1, 3)) for x in (pixels, ivar, mask, psf_left, psf_right)]
    rows = pixels.shape[2]
    wave, spec = lax.axis_size("wave"), lax.axis_size("spec")
    total_rows = rows * wave
    hbm = [pltpu.with_memory_space_constraint(x, pltpu.HBM) for x in arrays]
    odd = lax.rem(lax.axis_index("wave"), 2) == 1

    def other_core(s, i):
        return (s, i ^ 1)

    near, far, head = edge_call(hbm)
    far = swap(far, lambda s, i: (s, i + 1 if i % 2 else i - 1))
    near = swap(near, other_core)
    factors = forward_call(near, head, hbm, sky_index)
    flux, sums = backward_call(wave, far, factors)
    got = swap(sums, other_core)
    flux, got = lax.optimization_barrier((flux, got))
    other = swap(flux, other_core)
    sums = jnp.where(odd, jnp.concatenate([got, sums]), jnp.concatenate([sums, got]))
    if spec == 4:
        first = swap(sums, lambda s, i: (s ^ (1 if i % 2 else 2), i))
        third = swap(sums, lambda s, i: (s ^ 3, i ^ 1))
        second = swap(first, other_core)
        sums = (sums + jnp.where(odd, first, second)) + (jnp.where(odd, second, first) + third)
    else:
        for k in powers(1, spec):
            sums = sums + swap(sums, lambda s, i: (s ^ k, i))
    regress, sky = regress_call(total_rows, flux, other, sums)
    if wave == 8:
        first = swap(regress, lambda s, i: (s, i ^ (6 if i % 2 else 2)))
        third = swap(regress, lambda s, i: (s, i ^ 4 if i % 2 else -1))
        fetched = first + jnp.where(odd, third, 0.0)
        terms = [regress, fetched, swap(fetched, other_core)]
    else:
        for k in powers(2, wave):
            regress = regress + swap(regress, lambda s, i: (s, i ^ k if i % 2 else -1))
        terms = [jnp.where(odd, regress, swap(regress, other_core))]
    cleaned, sky = clean_call(total_rows, flux, sky, terms)
    return (jnp.transpose(cleaned, (0, 2, 1, 3)), sky[:, :rows])


def solution(mesh):
    block = P(None, "spec", "wave", None)
    return jax.shard_map(
        local,
        mesh=mesh,
        in_specs=(block,) * 5 + (P("spec", None),),
        out_specs=(block, P(None, "wave")),
        check_vma=False,
    )
```

```python
import functools

import jax
import jax.numpy as jnp
from jax import lax
from jax.experimental import pallas as pl
from jax.experimental.pallas import tpu as pltpu
from jax.sharding import PartitionSpec as P

REG = 0.05
RIDGE = 1.0
HALO = 4
PARTS = 6
TAIL = 13
CUTS = (0, 14, 26, 35, 40)
LANES = 128

F32 = jnp.float32
VM = pl.BlockSpec(memory_space=pltpu.VMEM)
SM = pl.BlockSpec(memory_space=pltpu.SMEM)
HB = pl.BlockSpec(memory_space=pltpu.HBM)


def in_vmem(shape, dtype=F32):
    return jax.ShapeDtypeStruct(shape, dtype)


def recip(values):
    return 1.0 / values


def weight_of(ivar, mask):
    return jnp.where(mask == 0, ivar, 0.0)


def edge_message(p, w, l, r):
    wl = [a * b for a, b in zip(w, l)]
    wr = [a * b for a, b in zip(w, r)]
    d0 = w[0] + wl[1] * l[1] + REG
    d1 = w[1] + wr[0] * r[0] + wl[2] * l[2] + REG
    d2 = w[2] + wr[1] * r[1] + wl[3] * l[3] + REG
    d3 = w[3] + wr[2] * r[2]
    d4 = wr[3] * r[3]
    raw = d4
    a01 = wr[0] + wl[1]
    a12 = wr[1] + wl[2]
    a23 = wr[2] + wl[3]
    a34 = wr[3]
    a02 = wl[1] * r[1]
    a13 = wl[2] * r[2]
    a24 = wl[3] * r[3]
    b0 = w[0] * p[0] + wl[1] * p[1]
    b1 = w[1] * p[1] + wr[0] * p[0] + wl[2] * p[2]
    b2 = w[2] * p[2] + wr[1] * p[1] + wl[3] * p[3]
    b3 = w[3] * p[3] + wr[2] * p[2]
    b4 = wr[3] * p[3]
    inv = recip(d0)
    near, far = a01 * inv, a02 * inv
    d1, a12, d2 = d1 - near * a01, a12 - near * a02, d2 - far * a02
    b1, b2 = b1 - near * b0, b2 - far * b0
    inv = recip(d1)
    near, far = a12 * inv, a13 * inv
    d2, a23, d3 = d2 - near * a12, a23 - near * a13, d3 - far * a13
    b2, b3 = b2 - near * b1, b3 - far * b1
    inv = recip(d2)
    near, far = a23 * inv, a24 * inv
    d3, a34, d4 = d3 - near * a23, a34 - near * a24, d4 - far * a24
    b3, b4 = b3 - near * b2, b4 - far * b2
    return (d3, a34, d4, b3, b4, raw)


def edge_kernel(pix, iva, msk, lef, rig, near_out, far_out, head, bufs, mhead, mbuf, sems):
    exposures, rows, specs, fibres = pix.shape
    size = head.shape[1]
    odd = lax.rem(lax.axis_index("wave"), 2)
    first, last = (1 - odd) * (rows - size), odd * (rows - HALO)
    for e in range(exposures):
        for slot, ref in enumerate((pix, iva, lef, rig)):
            pltpu.make_async_copy(
                ref.at[e, pl.ds(first, size)], head.at[slot, :, :, e], sems.at[0]
            ).start()
        pltpu.make_async_copy(msk.at[e, pl.ds(first, size)], mhead.at[:, :, e], sems.at[1]).start()
    for e in range(exposures):
        for slot, ref in enumerate((pix, iva, lef, rig)):
            pltpu.make_async_copy(
                ref.at[e, pl.ds(last, HALO)], bufs.at[slot, :, :, e], sems.at[2]
            ).start()
        pltpu.make_async_copy(msk.at[e, pl.ds(last, HALO)], mbuf.at[:, :, e], sems.at[3]).start()
    before, after = 3 - odd, 2 + odd
    pltpu.make_async_copy(head, head, sems.at[0]).wait()
    pltpu.make_async_copy(mhead, mhead, sems.at[1]).wait()
    for k in range(size):
        for s in range(specs):
            head[1, k, s] = weight_of(head[1, k, s], mhead[k, s])
    order = [odd * k + (1 - odd) * (size - 1 - k) for k in range(HALO - 1, -1, -1)]
    for s in range(specs):
        p, w, l, r = [[head[slot, k, s] for k in order] for slot in (0, 1, before, after)]
        for slot, value in enumerate(edge_message(p, w, r, l)):
            near_out[slot, s] = value
    pltpu.make_async_copy(bufs, bufs, sems.at[2]).wait()
    pltpu.make_async_copy(mbuf, mbuf, sems.at[3]).wait()
    order = [odd * k + (1 - odd) * (HALO - 1 - k) for k in range(HALO)]
    for s in range(specs):
        p, l, r = [[bufs[slot, k, s] for k in order] for slot in (0, before, after)]
        w = [weight_of(bufs[1, k, s], mbuf[k, s]) for k in order]
        for slot, value in enumerate(edge_message(p, w, l, r)):
            far_out[slot, s] = value


def edge_call(arrays):
    exposures, rows, specs, fibres = arrays[0].shape
    size = max(HALO, rows // 5)
    message = in_vmem((PARTS, specs, exposures, fibres))
    return pl.pallas_call(
        edge_kernel,
        out_shape=(message, message, in_vmem((4, size, specs, exposures, fibres))),
        in_specs=[HB] * 5,
        out_specs=(VM, VM, VM),
        scratch_shapes=[
            pltpu.VMEM((4, HALO, specs, exposures, fibres), F32),
            pltpu.VMEM((size, specs, exposures, fibres), jnp.int32),
            pltpu.VMEM((HALO, specs, exposures, fibres), jnp.int32),
            pltpu.SemaphoreType.DMA((4,)),
        ],
        compiler_params=pltpu.CompilerParams(vmem_limit_bytes=8 * 2**20),
        cost_estimate=pl.CostEstimate(flops=10**6, bytes_accessed=10**6, transcendentals=0),
        name="edges",
    )(*arrays)


def forward_kernel(
    near, head, pix, iva, msk, lef, rig, sky_index, lower, lower_far, half, shares, tail, sky_mask, denom, bufs, mbuf, sems
):
    exposures, rows, specs, fibres = pix.shape
    size = head.shape[1]
    odd = lax.rem(lax.axis_index("wave"), 2)
    spans = range(specs)
    bounds = [0] + [size + (rows - size) * part // 40 for part in CUTS]

    def place(low, high):
        return pl.ds(odd * low + (1 - odd) * (rows - high), high - low)

    for c in range(1, len(CUTS)):
        here = place(bounds[c], bounds[c + 1])
        for e in range(exposures):
            for slot, ref in enumerate((pix, iva, lef, rig)):
                pltpu.make_async_copy(
                    ref.at[e, here], bufs.at[slot, here, :, e], sems.at[0, c - 1]
                ).start()
            pltpu.make_async_copy(msk.at[e, here], mbuf.at[here, :, e], sems.at[1, c - 1]).start()
    lane = lax.broadcasted_iota(jnp.int32, (exposures, fibres), 1)
    for s in spans:
        found = lane == sky_index[s, 0]
        for k in range(1, sky_index.shape[1]):
            found = found | (lane == sky_index[s, k])
        sky_mask[s] = jnp.where(found, 1.0, 0.0)

    spot = lax.broadcasted_iota(jnp.int32, (exposures, LANES), 1)
    before, after = 3 - odd, 2 + odd

    def share(k, parts, total):
        parts = [sky_mask[s] * parts[s] for s in spans]
        for s in spans:
            shares[k, s] = parts[s]
        row = odd * k + (1 - odd) * (rows - 1 - k)
        return jnp.where(spot == row, jnp.sum(sum(parts), axis=1, keepdims=True), total)

    made = [dict(d1=REG, b1=0.0, d2=REG, b2=0.0, r1=0.0) for _ in spans]
    offs = [[] for _ in spans]
    fars = [[] for _ in spans]
    states = [None] * specs
    total = jnp.zeros((exposures, LANES), F32)
    for c in range(len(CUTS)):
        if c > 0:
            here = place(bounds[c], bounds[c + 1])
            part, mpart = bufs.at[:, here], mbuf.at[here]
            pltpu.make_async_copy(part, part, sems.at[0, c - 1]).wait()
            pltpu.make_async_copy(mpart, mpart, sems.at[1, c - 1]).wait()
        for k in range(bounds[c], bounds[c + 1]):
            row = odd * k + (1 - odd) * (rows - 1 - k)
            top = odd * k + (1 - odd) * (size - 1 - k)
            diags = []
            for s in spans:
                if c == 0:
                    p, w, l, r = [head[slot, top, s] for slot in (0, 1, before, after)]
                else:
                    p, l, r = bufs[0, row, s], bufs[before, row, s], bufs[after, row, s]
                    w = weight_of(bufs[1, row, s], mbuf[row, s])
                wl, wr, wp = w * l, w * r, w * p
                m = made[s]
                d, b = m["d1"] + wl * l, m["b1"] + wl * p
                offs[s].append(m["r1"] + wl)
                fars[s].append(wl * r)
                made[s] = dict(
                    d1=w + m["d2"], b1=wp + m["b2"], d2=wr * r + REG, b2=wr * p, r1=wr
                )
                if k == 0:
                    d, b = d + near[0, s], b + near[3, s]
                    offs[s][0] = offs[s][0] + near[1, s]
                    inv = recip(d)
                    states[s] = (inv, None, None, b, None)
                elif k == 1:
                    diags.append(d + near[5, s])
                    d, b = d + near[2, s], b + near[4, s]
                    inv1, _, _, y1, _ = states[s]
                    upper = offs[s][0]
                    g = upper * inv1
                    inv, y = recip(d - g * upper), b - g * y1
                    lower[1, s], half[1, s] = g, y * inv
                    states[s] = (inv, inv1, g, y, y1)
                else:
                    diags.append(d)
                    f, g, y, states[s] = eliminate(states[s], d, offs[s][k - 1], b, fars[s][k - 2])
                    lower_far[k, s], lower[k, s], half[k, s] = f, g, y * states[s][0]
            if k > 0:
                total = share(k - 1, diags, total)
    for s in spans:
        m = made[s]
        tail_parts = states[s] + (
            m["d1"], offs[s][rows - 1], m["b1"], fars[s][rows - 2], m["d2"], m["r1"], m["b2"], fars[s][rows - 1]
        )
        for slot, value in enumerate(tail_parts):
            tail[slot, s] = value
    denom[...] = share(rows - 1, [made[s]["d1"] for s in spans], total)


def eliminate(state, d, a, b, far_a):
    inv1, inv2, mult1, y1, y2 = state
    f = far_a * inv2
    upper = a - far_a * mult1
    g = upper * inv1
    pivot = d - f * far_a - g * upper
    y = b - f * y2 - g * y1
    return f, g, y, (recip(pivot), inv1, g, y, y1)


def forward_call(near, head, arrays, sky_index):
    exposures, rows, specs, fibres = arrays[0].shape
    chunks = len(CUTS) - 1
    whole = in_vmem((rows, specs, exposures, fibres))
    return pl.pallas_call(
        forward_kernel,
        out_shape=(
            whole,
            whole,
            whole,
            whole,
            in_vmem((TAIL, specs, exposures, fibres)),
            in_vmem((specs, exposures, fibres)),
            in_vmem((exposures, LANES)),
        ),
        in_specs=[VM] * 2 + [HB] * 5 + [SM],
        out_specs=(VM,) * 7,
        scratch_shapes=[
            pltpu.VMEM((4, rows, specs, exposures, fibres), F32),
            pltpu.VMEM((rows, specs, exposures, fibres), jnp.int32),
            pltpu.SemaphoreType.DMA((2, chunks)),
        ],
        compiler_params=pltpu.CompilerParams(vmem_limit_bytes=24 * 2**20),
        cost_estimate=pl.CostEstimate(flops=10**7, bytes_accessed=10**7, transcendentals=0),
        name="forward",
    )(near, head, *arrays, sky_index)


def backward_kernel(wave, far, lower, lower_far, half, shares, tail, sky_mask, denom, flux, sums):
    rows, specs, exposures, fibres = lower.shape
    device = lax.axis_index("wave")
    odd = lax.rem(device, 2)
    at_end = (device == 0) | (device == wave - 1)
    lane = lax.broadcasted_iota(jnp.int32, (exposures, LANES), 1)
    spans = range(specs)

    def message(part, s):
        return jnp.where(at_end, 0.0, far[part, s])

    def place(k):
        return odd * k + (1 - odd) * (rows - 1 - k)

    def total(parts):
        return jnp.sum(parts, axis=1, keepdims=True)

    def spread(k, numer, parts, values):
        return jnp.where(lane == place(k), total(sum(parts[s] * values[s] for s in spans)), numer)

    after, extra = [], []
    for s in spans:
        t = [tail[slot, s] for slot in range(TAIL)]
        f, g, y, state = eliminate(t[:5], t[5] + message(2, s), t[6], t[7] + message(4, s), t[8])
        f1, g1, y1, last = eliminate(
            state, t[9] + message(0, s), t[10] + message(1, s), t[11] + message(3, s), t[12]
        )
        beyond = y1 * last[0]
        value = y * state[0] - g1 * beyond
        flux[place(rows - 1), s] = value
        after.append((value, beyond, g, f1, f))
        extra.append(sky_mask[s] * message(5, s))
    parts = [shares[rows - 1, s] + extra[s] for s in spans]
    numer = jnp.zeros((exposures, LANES), F32)
    numer = spread(rows - 1, numer, parts, [after[s][0] for s in spans])
    sums[1] = denom[...] + jnp.where(lane == place(rows - 1), total(sum(extra)), 0.0)

    def step(k, numer, after, bottom=False):
        results = []
        for s in spans:
            x1, x2, g1, f2, f1 = after[s]
            value = half[k, s] - g1 * x1 - f2 * x2
            flux[place(k - 1), s] = value
            results.append((value, x1) if bottom else (value, x1, lower[k, s], f1, lower_far[k, s]))
        parts = [shares[k - 1, s] for s in spans]
        return spread(k - 1, numer, parts, [r[0] for r in results]), tuple(results)

    for k in range(rows - 1, 1, -1):
        numer, after = step(k, numer, after)
    numer, after = step(1, numer, after, bottom=True)
    sums[0] = numer


def backward_call(wave, far, factors):
    rows, specs, exposures, fibres = factors[0].shape
    return pl.pallas_call(
        functools.partial(backward_kernel, wave),
        out_shape=(in_vmem((rows, specs, exposures, fibres)), in_vmem((2, exposures, LANES))),
        in_specs=[VM] * 8,
        out_specs=(VM, VM),
        compiler_params=pltpu.CompilerParams(vmem_limit_bytes=24 * 2**20),
        cost_estimate=pl.CostEstimate(flops=10**7, bytes_accessed=10**7, transcendentals=0),
        name="backward",
    )(far, *factors)


def position_of(index, total_rows):
    return 2.0 * jnp.asarray(index).astype(F32) / (total_rows - 1) - 1.0


def regress_kernel(total_rows, flux, other, sums, regress, sky_out):
    rows, specs, exposures, fibres = flux.shape
    lanes = regress.shape[2]
    device = lax.axis_index("wave")
    odd = lax.rem(device, 2)
    lane = lax.broadcasted_iota(jnp.int32, (exposures, LANES), 1)
    valid = lane < rows
    step = 2.0 / (total_rows - 1)
    plain = [0.0] * specs
    tilted = [0.0] * specs
    moments = [0.0] * 3
    for which, (ref, core) in enumerate(((flux, odd), (other, 1 - odd))):
        owner = device - odd + core
        sky = jnp.where(valid, sums[2 * core] / jnp.where(valid, sums[2 * core + 1], 1.0), 0.0)
        position = position_of(owner * rows + lane, total_rows)
        slanted = sky * position
        moments[0] += jnp.sum(sky * sky, axis=1, keepdims=True)
        moments[1] += jnp.sum(sky * slanted, axis=1, keepdims=True)
        moments[2] += jnp.sum(slanted * slanted, axis=1, keepdims=True)
        if which == 0:
            sky_out[...] = sky
        end = position_of(owner * rows + rows, total_rows)
        running = [None] * specs
        summed = [None] * specs
        for k in range(rows):
            sky_k = jnp.broadcast_to(sky[:, k : k + 1], (exposures, fibres))
            for s in range(specs):
                term = ref[k, s] * sky_k
                running[s] = term if k == 0 else running[s] + term
                summed[s] = running[s] if k == 0 else summed[s] + running[s]
        for s in range(specs):
            plain[s] += running[s]
            tilted[s] += end * running[s] - step * summed[s]
    wide = lax.broadcasted_iota(jnp.int32, (exposures, lanes - fibres), 1)
    held = jnp.where(wide == 0, moments[0], jnp.where(wide == 1, moments[1], moments[2]))
    for s in range(specs):
        regress[s, :, :fibres] = plain[s]
        regress[specs + s, :, :fibres] = tilted[s]
        for r in (s, specs + s):
            regress[r, :, fibres:] = held


def regress_call(total_rows, flux, other, sums):
    rows, specs, exposures, fibres = flux.shape
    lanes = -(-(fibres + 3) // LANES) * LANES
    return pl.pallas_call(
        functools.partial(regress_kernel, total_rows),
        out_shape=(
            in_vmem((2 * specs, exposures, lanes)),
            in_vmem((exposures, LANES)),
        ),
        in_specs=[VM] * 3,
        out_specs=(VM, VM),
        compiler_params=pltpu.CompilerParams(vmem_limit_bytes=24 * 2**20),
        cost_estimate=pl.CostEstimate(flops=10**6, bytes_accessed=10**6, transcendentals=0),
        name="regress",
    )(flux, other, sums)


def clean_kernel(total_rows, flux, sky_ref, *refs):
    *terms, out, sky_out, buf, sems, sky_sem = refs
    rows, specs, exposures, fibres = flux.shape
    sky_copy = pltpu.make_async_copy(sky_ref, sky_out, sky_sem)
    sky_copy.start()
    device = lax.axis_index("wave")

    def got(slot):
        return sum(term[slot] for term in terms)

    sums = [got(slot) for slot in range(2 * specs)]
    moments = [sums[0][:, fibres + m : fibres + m + 1] for m in range(3)]
    upper_left, cross, lower_right = moments[0] + RIDGE, moments[1], moments[2] + RIDGE
    inverse = 1.0 / (upper_left * lower_right - cross * cross)
    start = position_of(device * rows, total_rows)
    step = 2.0 / (total_rows - 1)
    level, change = [], []
    for s in range(specs):
        r1, r2 = sums[s][:, :fibres], sums[specs + s][:, :fibres]
        slope_a = (lower_right * r1 - cross * r2) * inverse
        slope_b = (upper_left * r2 - cross * r1) * inverse
        level.append(slope_a + slope_b * start)
        change.append(slope_b * step)
    sky = sky_ref[...]
    chunks = sems.shape[0]
    bounds = [rows * c // chunks for c in range(chunks + 1)]
    for c in range(chunks):
        low, high = bounds[c], bounds[c + 1]
        for k in range(low, high):
            sky_k = jnp.broadcast_to(sky[:, k : k + 1], (exposures, fibres))
            for s in range(specs):
                buf[k, s] = flux[k, s] - level[s] * sky_k
                level[s] = level[s] + change[s]
        for e in range(exposures):
            pltpu.make_async_copy(
                buf.at[low:high, :, e], out.at[e, low:high], sems.at[c]
            ).start()
    for c in range(chunks):
        part = buf.at[bounds[c] : bounds[c + 1]]
        pltpu.make_async_copy(part, part, sems.at[c]).wait()
    sky_copy.wait()


def clean_call(total_rows, flux, sky, terms):
    rows, specs, exposures, fibres = flux.shape
    return pl.pallas_call(
        functools.partial(clean_kernel, total_rows),
        out_shape=(
            jax.ShapeDtypeStruct((exposures, rows, specs, fibres), F32),
            jax.ShapeDtypeStruct((exposures, LANES), F32),
        ),
        in_specs=[VM] * (2 + len(terms)),
        out_specs=(HB, HB),
        scratch_shapes=[
            pltpu.VMEM((rows, specs, exposures, fibres), F32),
            pltpu.SemaphoreType.DMA((4,)),
            pltpu.SemaphoreType.DMA,
        ],
        compiler_params=pltpu.CompilerParams(vmem_limit_bytes=24 * 2**20),
        cost_estimate=pl.CostEstimate(flops=10**6, bytes_accessed=10**6, transcendentals=0),
        name="clean",
    )(flux, sky, *terms)


def powers(low, high):
    steps = []
    while low < high:
        steps.append(low)
        low *= 2
    return steps


def swap(values, partner):
    spec, wave = lax.axis_size("spec"), lax.axis_size("wave")
    pairs = []
    for s in range(spec):
        for i in range(wave):
            t, j = partner(s, i)
            if not 0 <= j < wave:
                t, j = s ^ 1, i
            if t < spec:
                pairs.append((s * wave + i, t * wave + j))
    return lax.ppermute(values, ("spec", "wave"), pairs)


def local(pixels, ivar, mask, psf_left, psf_right, sky_index):
    arrays = [jnp.transpose(x, (0, 2, 1, 3)) for x in (pixels, ivar, mask, psf_left, psf_right)]
    rows = pixels.shape[2]
    wave, spec = lax.axis_size("wave"), lax.axis_size("spec")
    total_rows = rows * wave
    hbm = [pltpu.with_memory_space_constraint(x, pltpu.HBM) for x in arrays]
    odd = lax.rem(lax.axis_index("wave"), 2) == 1

    def other_core(s, i):
        return (s, i ^ 1)

    near, far, head = edge_call(hbm)
    far = swap(far, lambda s, i: (s, i + 1 if i % 2 else i - 1))
    near = swap(near, other_core)
    factors = forward_call(near, head, hbm, sky_index)
    flux, sums = backward_call(wave, far, factors)
    got = swap(sums, other_core)
    flux, got = lax.optimization_barrier((flux, got))
    other = swap(flux, other_core)
    sums = jnp.where(odd, jnp.concatenate([got, sums]), jnp.concatenate([sums, got]))
    if spec == 4:
        first = swap(sums, lambda s, i: (s ^ (1 if i % 2 else 2), i))
        third = swap(sums, lambda s, i: (s ^ 3, i ^ 1))
        second = swap(first, other_core)
        sums = (sums + jnp.where(odd, first, second)) + (jnp.where(odd, second, first) + third)
    else:
        for k in powers(1, spec):
            sums = sums + swap(sums, lambda s, i: (s ^ k, i))
    regress, sky = regress_call(total_rows, flux, other, sums)
    if wave == 8:
        first = swap(regress, lambda s, i: (s, i ^ (6 if i % 2 else 2)))
        third = swap(regress, lambda s, i: (s, i ^ (5 if i % 2 else 1)))
        fetched = first + jnp.where(odd, 0.0, third)
        terms = [regress, fetched, swap(fetched, other_core)]
    else:
        for k in powers(2, wave):
            regress = regress + swap(regress, lambda s, i: (s, i ^ k if i % 2 else -1))
        terms = [jnp.where(odd, regress, swap(regress, other_core))]
    cleaned, sky = clean_call(total_rows, flux, sky, terms)
    return (jnp.transpose(cleaned, (0, 2, 1, 3)), sky[:, :rows])


def solution(mesh):
    block = P(None, "spec", "wave", None)
    return jax.shard_map(
        local,
        mesh=mesh,
        in_specs=(block,) * 5 + (P("spec", None),),
        out_specs=(block, P(None, "wave")),
        check_vma=False,
    )
```

```python
import functools

import jax
import jax.numpy as jnp
from jax import lax
from jax.experimental import pallas as pl
from jax.experimental.pallas import tpu as pltpu
from jax.sharding import PartitionSpec as P

REG = 0.05
RIDGE = 1.0
HALO = 4
PARTS = 6
TAIL = 13
CUTS = (0, 14, 26, 35, 40)
LANES = 128

F32 = jnp.float32
VM = pl.BlockSpec(memory_space=pltpu.VMEM)
SM = pl.BlockSpec(memory_space=pltpu.SMEM)
HB = pl.BlockSpec(memory_space=pltpu.HBM)


def in_vmem(shape, dtype=F32):
    return jax.ShapeDtypeStruct(shape, dtype)


def recip(values):
    return 1.0 / values


def weight_of(ivar, mask):
    return jnp.where(mask == 0, ivar, 0.0)


def edge_message(p, w, l, r):
    wl = [a * b for a, b in zip(w, l)]
    wr = [a * b for a, b in zip(w, r)]
    d0 = w[0] + wl[1] * l[1] + REG
    d1 = w[1] + wr[0] * r[0] + wl[2] * l[2] + REG
    d2 = w[2] + wr[1] * r[1] + wl[3] * l[3] + REG
    d3 = w[3] + wr[2] * r[2]
    d4 = wr[3] * r[3]
    raw = d4
    a01 = wr[0] + wl[1]
    a12 = wr[1] + wl[2]
    a23 = wr[2] + wl[3]
    a34 = wr[3]
    a02 = wl[1] * r[1]
    a13 = wl[2] * r[2]
    a24 = wl[3] * r[3]
    b0 = w[0] * p[0] + wl[1] * p[1]
    b1 = w[1] * p[1] + wr[0] * p[0] + wl[2] * p[2]
    b2 = w[2] * p[2] + wr[1] * p[1] + wl[3] * p[3]
    b3 = w[3] * p[3] + wr[2] * p[2]
    b4 = wr[3] * p[3]
    inv = recip(d0)
    near, far = a01 * inv, a02 * inv
    d1, a12, d2 = d1 - near * a01, a12 - near * a02, d2 - far * a02
    b1, b2 = b1 - near * b0, b2 - far * b0
    inv = recip(d1)
    near, far = a12 * inv, a13 * inv
    d2, a23, d3 = d2 - near * a12, a23 - near * a13, d3 - far * a13
    b2, b3 = b2 - near * b1, b3 - far * b1
    inv = recip(d2)
    near, far = a23 * inv, a24 * inv
    d3, a34, d4 = d3 - near * a23, a34 - near * a24, d4 - far * a24
    b3, b4 = b3 - near * b2, b4 - far * b2
    return (d3, a34, d4, b3, b4, raw)


def edge_kernel(pix, iva, msk, lef, rig, near_out, far_out, head, bufs, mhead, mbuf, sems):
    exposures, rows, specs, fibres = pix.shape
    size = head.shape[1]
    odd = lax.rem(lax.axis_index("wave"), 2)
    first, last = (1 - odd) * (rows - size), odd * (rows - HALO)
    for e in range(exposures):
        for slot, ref in enumerate((pix, iva, lef, rig)):
            pltpu.make_async_copy(
                ref.at[e, pl.ds(first, size)], head.at[slot, :, :, e], sems.at[0]
            ).start()
        pltpu.make_async_copy(msk.at[e, pl.ds(first, size)], mhead.at[:, :, e], sems.at[1]).start()
    for e in range(exposures):
        for slot, ref in enumerate((pix, iva, lef, rig)):
            pltpu.make_async_copy(
                ref.at[e, pl.ds(last, HALO)], bufs.at[slot, :, :, e], sems.at[2]
            ).start()
        pltpu.make_async_copy(msk.at[e, pl.ds(last, HALO)], mbuf.at[:, :, e], sems.at[3]).start()
    before, after = 3 - odd, 2 + odd
    pltpu.make_async_copy(head, head, sems.at[0]).wait()
    pltpu.make_async_copy(mhead, mhead, sems.at[1]).wait()
    for k in range(size):
        for s in range(specs):
            head[1, k, s] = weight_of(head[1, k, s], mhead[k, s])
    order = [odd * k + (1 - odd) * (size - 1 - k) for k in range(HALO - 1, -1, -1)]
    for s in range(specs):
        p, w, l, r = [[head[slot, k, s] for k in order] for slot in (0, 1, before, after)]
        for slot, value in enumerate(edge_message(p, w, r, l)):
            near_out[slot, s] = value
    pltpu.make_async_copy(bufs, bufs, sems.at[2]).wait()
    pltpu.make_async_copy(mbuf, mbuf, sems.at[3]).wait()
    order = [odd * k + (1 - odd) * (HALO - 1 - k) for k in range(HALO)]
    for s in range(specs):
        p, l, r = [[bufs[slot, k, s] for k in order] for slot in (0, before, after)]
        w = [weight_of(bufs[1, k, s], mbuf[k, s]) for k in order]
        for slot, value in enumerate(edge_message(p, w, l, r)):
            far_out[slot, s] = value


def edge_call(arrays):
    exposures, rows, specs, fibres = arrays[0].shape
    size = max(HALO, rows // 5)
    message = in_vmem((PARTS, specs, exposures, fibres))
    return pl.pallas_call(
        edge_kernel,
        out_shape=(message, message, in_vmem((4, size, specs, exposures, fibres))),
        in_specs=[HB] * 5,
        out_specs=(VM, VM, VM),
        scratch_shapes=[
            pltpu.VMEM((4, HALO, specs, exposures, fibres), F32),
            pltpu.VMEM((size, specs, exposures, fibres), jnp.int32),
            pltpu.VMEM((HALO, specs, exposures, fibres), jnp.int32),
            pltpu.SemaphoreType.DMA((4,)),
        ],
        compiler_params=pltpu.CompilerParams(vmem_limit_bytes=8 * 2**20),
        cost_estimate=pl.CostEstimate(flops=10**6, bytes_accessed=10**6, transcendentals=0),
        name="edges",
    )(*arrays)


def forward_kernel(
    near, head, pix, iva, msk, lef, rig, sky_index, lower, lower_far, half, shares, tail, sky_mask, denom, bufs, mbuf, sems
):
    exposures, rows, specs, fibres = pix.shape
    size = head.shape[1]
    odd = lax.rem(lax.axis_index("wave"), 2)
    spans = range(specs)
    bounds = [0] + [size + (rows - size) * part // 40 for part in CUTS]

    def place(low, high):
        return pl.ds(odd * low + (1 - odd) * (rows - high), high - low)

    for c in range(1, len(CUTS)):
        here = place(bounds[c], bounds[c + 1])
        for e in range(exposures):
            for slot, ref in enumerate((pix, iva, lef, rig)):
                pltpu.make_async_copy(
                    ref.at[e, here], bufs.at[slot, here, :, e], sems.at[0, c - 1]
                ).start()
            pltpu.make_async_copy(msk.at[e, here], mbuf.at[here, :, e], sems.at[1, c - 1]).start()
    lane = lax.broadcasted_iota(jnp.int32, (exposures, fibres), 1)
    for s in spans:
        found = lane == sky_index[s, 0]
        for k in range(1, sky_index.shape[1]):
            found = found | (lane == sky_index[s, k])
        sky_mask[s] = jnp.where(found, 1.0, 0.0)

    spot = lax.broadcasted_iota(jnp.int32, (exposures, LANES), 1)
    before, after = 3 - odd, 2 + odd

    def share(k, parts, total):
        parts = [sky_mask[s] * parts[s] for s in spans]
        for s in spans:
            shares[k, s] = parts[s]
        row = odd * k + (1 - odd) * (rows - 1 - k)
        return jnp.where(spot == row, jnp.sum(sum(parts), axis=1, keepdims=True), total)

    made = [dict(d1=REG, b1=0.0, d2=REG, b2=0.0, r1=0.0) for _ in spans]
    offs = [[] for _ in spans]
    fars = [[] for _ in spans]
    states = [None] * specs
    total = jnp.zeros((exposures, LANES), F32)
    for c in range(len(CUTS)):
        if c > 0:
            here = place(bounds[c], bounds[c + 1])
            part, mpart = bufs.at[:, here], mbuf.at[here]
            pltpu.make_async_copy(part, part, sems.at[0, c - 1]).wait()
            pltpu.make_async_copy(mpart, mpart, sems.at[1, c - 1]).wait()
        for k in range(bounds[c], bounds[c + 1]):
            row = odd * k + (1 - odd) * (rows - 1 - k)
            top = odd * k + (1 - odd) * (size - 1 - k)
            diags = []
            for s in spans:
                if c == 0:
                    p, w, l, r = [head[slot, top, s] for slot in (0, 1, before, after)]
                else:
                    p, l, r = bufs[0, row, s], bufs[before, row, s], bufs[after, row, s]
                    w = weight_of(bufs[1, row, s], mbuf[row, s])
                wl, wr, wp = w * l, w * r, w * p
                m = made[s]
                d, b = m["d1"] + wl * l, m["b1"] + wl * p
                offs[s].append(m["r1"] + wl)
                fars[s].append(wl * r)
                made[s] = dict(
                    d1=w + m["d2"], b1=wp + m["b2"], d2=wr * r + REG, b2=wr * p, r1=wr
                )
                if k == 0:
                    d, b = d + near[0, s], b + near[3, s]
                    offs[s][0] = offs[s][0] + near[1, s]
                    inv = recip(d)
                    states[s] = (inv, None, None, b, None)
                elif k == 1:
                    diags.append(d + near[5, s])
                    d, b = d + near[2, s], b + near[4, s]
                    inv1, _, _, y1, _ = states[s]
                    upper = offs[s][0]
                    g = upper * inv1
                    inv, y = recip(d - g * upper), b - g * y1
                    lower[1, s], half[1, s] = g, y * inv
                    states[s] = (inv, inv1, g, y, y1)
                else:
                    diags.append(d)
                    f, g, y, states[s] = eliminate(states[s], d, offs[s][k - 1], b, fars[s][k - 2])
                    lower_far[k, s], lower[k, s], half[k, s] = f, g, y * states[s][0]
            if k > 0:
                total = share(k - 1, diags, total)
    for s in spans:
        m = made[s]
        tail_parts = states[s] + (
            m["d1"], offs[s][rows - 1], m["b1"], fars[s][rows - 2], m["d2"], m["r1"], m["b2"], fars[s][rows - 1]
        )
        for slot, value in enumerate(tail_parts):
            tail[slot, s] = value
    denom[...] = share(rows - 1, [made[s]["d1"] for s in spans], total)


def eliminate(state, d, a, b, far_a):
    inv1, inv2, mult1, y1, y2 = state
    f = far_a * inv2
    upper = a - far_a * mult1
    g = upper * inv1
    pivot = d - f * far_a - g * upper
    y = b - f * y2 - g * y1
    return f, g, y, (recip(pivot), inv1, g, y, y1)


def forward_call(near, head, arrays, sky_index):
    exposures, rows, specs, fibres = arrays[0].shape
    chunks = len(CUTS) - 1
    whole = in_vmem((rows, specs, exposures, fibres))
    return pl.pallas_call(
        forward_kernel,
        out_shape=(
            whole,
            whole,
            whole,
            whole,
            in_vmem((TAIL, specs, exposures, fibres)),
            in_vmem((specs, exposures, fibres)),
            in_vmem((exposures, LANES)),
        ),
        in_specs=[VM] * 2 + [HB] * 5 + [SM],
        out_specs=(VM,) * 7,
        scratch_shapes=[
            pltpu.VMEM((4, rows, specs, exposures, fibres), F32),
            pltpu.VMEM((rows, specs, exposures, fibres), jnp.int32),
            pltpu.SemaphoreType.DMA((2, chunks)),
        ],
        compiler_params=pltpu.CompilerParams(vmem_limit_bytes=24 * 2**20),
        cost_estimate=pl.CostEstimate(flops=10**7, bytes_accessed=10**7, transcendentals=0),
        name="forward",
    )(near, head, *arrays, sky_index)


def backward_kernel(wave, far, lower, lower_far, half, shares, tail, sky_mask, denom, flux, sums):
    rows, specs, exposures, fibres = lower.shape
    device = lax.axis_index("wave")
    odd = lax.rem(device, 2)
    at_end = (device == 0) | (device == wave - 1)
    lane = lax.broadcasted_iota(jnp.int32, (exposures, LANES), 1)
    spans = range(specs)

    def message(part, s):
        return jnp.where(at_end, 0.0, far[part, s])

    def place(k):
        return odd * k + (1 - odd) * (rows - 1 - k)

    def total(parts):
        return jnp.sum(parts, axis=1, keepdims=True)

    def spread(k, numer, parts, values):
        return jnp.where(lane == place(k), total(sum(parts[s] * values[s] for s in spans)), numer)

    after, extra = [], []
    for s in spans:
        t = [tail[slot, s] for slot in range(TAIL)]
        f, g, y, state = eliminate(t[:5], t[5] + message(2, s), t[6], t[7] + message(4, s), t[8])
        f1, g1, y1, last = eliminate(
            state, t[9] + message(0, s), t[10] + message(1, s), t[11] + message(3, s), t[12]
        )
        beyond = y1 * last[0]
        value = y * state[0] - g1 * beyond
        flux[place(rows - 1), s] = value
        after.append((value, beyond, g, f1, f))
        extra.append(sky_mask[s] * message(5, s))
    parts = [shares[rows - 1, s] + extra[s] for s in spans]
    numer = jnp.zeros((exposures, LANES), F32)
    numer = spread(rows - 1, numer, parts, [after[s][0] for s in spans])
    sums[1] = denom[...] + jnp.where(lane == place(rows - 1), total(sum(extra)), 0.0)

    def step(k, numer, after, bottom=False):
        results = []
        for s in spans:
            x1, x2, g1, f2, f1 = after[s]
            value = half[k, s] - g1 * x1 - f2 * x2
            flux[place(k - 1), s] = value
            results.append((value, x1) if bottom else (value, x1, lower[k, s], f1, lower_far[k, s]))
        parts = [shares[k - 1, s] for s in spans]
        return spread(k - 1, numer, parts, [r[0] for r in results]), tuple(results)

    for k in range(rows - 1, 1, -1):
        numer, after = step(k, numer, after)
    numer, after = step(1, numer, after, bottom=True)
    sums[0] = numer


def backward_call(wave, far, factors):
    rows, specs, exposures, fibres = factors[0].shape
    return pl.pallas_call(
        functools.partial(backward_kernel, wave),
        out_shape=(in_vmem((rows, specs, exposures, fibres)), in_vmem((2, exposures, LANES))),
        in_specs=[VM] * 8,
        out_specs=(VM, VM),
        compiler_params=pltpu.CompilerParams(vmem_limit_bytes=24 * 2**20),
        cost_estimate=pl.CostEstimate(flops=10**7, bytes_accessed=10**7, transcendentals=0),
        name="backward",
    )(far, *factors)


def position_of(index, total_rows):
    return 2.0 * jnp.asarray(index).astype(F32) / (total_rows - 1) - 1.0


def regress_kernel(total_rows, flux, other, sums, regress, sky_out):
    rows, specs, exposures, fibres = flux.shape
    lanes = regress.shape[2]
    device = lax.axis_index("wave")
    odd = lax.rem(device, 2)
    lane = lax.broadcasted_iota(jnp.int32, (exposures, LANES), 1)
    valid = lane < rows
    step = 2.0 / (total_rows - 1)
    plain = [0.0] * specs
    tilted = [0.0] * specs
    moments = [0.0] * 3
    for which, (ref, core) in enumerate(((flux, odd), (other, 1 - odd))):
        owner = device - odd + core
        sky = jnp.where(valid, sums[2 * core] / jnp.where(valid, sums[2 * core + 1], 1.0), 0.0)
        position = position_of(owner * rows + lane, total_rows)
        slanted = sky * position
        moments[0] += jnp.sum(sky * sky, axis=1, keepdims=True)
        moments[1] += jnp.sum(sky * slanted, axis=1, keepdims=True)
        moments[2] += jnp.sum(slanted * slanted, axis=1, keepdims=True)
        if which == 0:
            sky_out[...] = sky
        end = position_of(owner * rows + rows, total_rows)
        running = [None] * specs
        summed = [None] * specs
        for k in range(rows):
            sky_k = jnp.broadcast_to(sky[:, k : k + 1], (exposures, fibres))
            for s in range(specs):
                term = ref[k, s] * sky_k
                running[s] = term if k == 0 else running[s] + term
                summed[s] = running[s] if k == 0 else summed[s] + running[s]
        for s in range(specs):
            plain[s] += running[s]
            tilted[s] += end * running[s] - step * summed[s]
    wide = lax.broadcasted_iota(jnp.int32, (exposures, lanes - fibres), 1)
    held = jnp.where(wide == 0, moments[0], jnp.where(wide == 1, moments[1], moments[2]))
    for s in range(specs):
        regress[s, :, :fibres] = plain[s]
        regress[specs + s, :, :fibres] = tilted[s]
        for r in (s, specs + s):
            regress[r, :, fibres:] = held


def regress_call(total_rows, flux, other, sums):
    rows, specs, exposures, fibres = flux.shape
    lanes = -(-(fibres + 3) // LANES) * LANES
    return pl.pallas_call(
        functools.partial(regress_kernel, total_rows),
        out_shape=(
            in_vmem((2 * specs, exposures, lanes)),
            in_vmem((exposures, LANES)),
        ),
        in_specs=[VM] * 3,
        out_specs=(VM, VM),
        compiler_params=pltpu.CompilerParams(vmem_limit_bytes=24 * 2**20),
        cost_estimate=pl.CostEstimate(flops=10**6, bytes_accessed=10**6, transcendentals=0),
        name="regress",
    )(flux, other, sums)


def clean_kernel(total_rows, flux, sky_ref, *refs):
    *terms, out, sky_out, buf, sems, sky_sem = refs
    rows, specs, exposures, fibres = flux.shape
    sky_copy = pltpu.make_async_copy(sky_ref, sky_out, sky_sem)
    sky_copy.start()
    device = lax.axis_index("wave")

    def got(slot):
        return sum(term[slot] for term in terms)

    sums = [got(slot) for slot in range(2 * specs)]
    moments = [sums[0][:, fibres + m : fibres + m + 1] for m in range(3)]
    upper_left, cross, lower_right = moments[0] + RIDGE, moments[1], moments[2] + RIDGE
    inverse = 1.0 / (upper_left * lower_right - cross * cross)
    start = position_of(device * rows, total_rows)
    step = 2.0 / (total_rows - 1)
    level, change = [], []
    for s in range(specs):
        r1, r2 = sums[s][:, :fibres], sums[specs + s][:, :fibres]
        slope_a = (lower_right * r1 - cross * r2) * inverse
        slope_b = (upper_left * r2 - cross * r1) * inverse
        level.append(slope_a + slope_b * start)
        change.append(slope_b * step)
    sky = sky_ref[...]
    chunks = sems.shape[0]
    bounds = [rows * c // chunks for c in range(chunks + 1)]
    for c in range(chunks):
        low, high = bounds[c], bounds[c + 1]
        for k in range(low, high):
            sky_k = jnp.broadcast_to(sky[:, k : k + 1], (exposures, fibres))
            for s in range(specs):
                buf[k, s] = flux[k, s] - level[s] * sky_k
                level[s] = level[s] + change[s]
        for e in range(exposures):
            pltpu.make_async_copy(
                buf.at[low:high, :, e], out.at[e, low:high], sems.at[c]
            ).start()
    for c in range(chunks):
        part = buf.at[bounds[c] : bounds[c + 1]]
        pltpu.make_async_copy(part, part, sems.at[c]).wait()
    sky_copy.wait()


def clean_call(total_rows, flux, sky, terms):
    rows, specs, exposures, fibres = flux.shape
    return pl.pallas_call(
        functools.partial(clean_kernel, total_rows),
        out_shape=(
            jax.ShapeDtypeStruct((exposures, rows, specs, fibres), F32),
            jax.ShapeDtypeStruct((exposures, LANES), F32),
        ),
        in_specs=[VM] * (2 + len(terms)),
        out_specs=(HB, HB),
        scratch_shapes=[
            pltpu.VMEM((rows, specs, exposures, fibres), F32),
            pltpu.SemaphoreType.DMA((4,)),
            pltpu.SemaphoreType.DMA,
        ],
        compiler_params=pltpu.CompilerParams(vmem_limit_bytes=24 * 2**20),
        cost_estimate=pl.CostEstimate(flops=10**6, bytes_accessed=10**6, transcendentals=0),
        name="clean",
    )(flux, sky, *terms)


def powers(low, high):
    steps = []
    while low < high:
        steps.append(low)
        low *= 2
    return steps


def swap(values, partner):
    spec, wave = lax.axis_size("spec"), lax.axis_size("wave")
    pairs = []
    for s in range(spec):
        for i in range(wave):
            t, j = partner(s, i)
            if not 0 <= j < wave:
                t, j = s ^ 1, i
            if t < spec:
                pairs.append((s * wave + i, t * wave + j))
    return lax.ppermute(values, ("spec", "wave"), pairs)


def local(pixels, ivar, mask, psf_left, psf_right, sky_index):
    arrays = [jnp.transpose(x, (0, 2, 1, 3)) for x in (pixels, ivar, mask, psf_left, psf_right)]
    rows = pixels.shape[2]
    wave, spec = lax.axis_size("wave"), lax.axis_size("spec")
    total_rows = rows * wave
    hbm = [pltpu.with_memory_space_constraint(x, pltpu.HBM) for x in arrays]
    odd = lax.rem(lax.axis_index("wave"), 2) == 1

    def other_core(s, i):
        return (s, i ^ 1)

    near, far, head = edge_call(hbm)
    far = swap(far, lambda s, i: (s, i + 1 if i % 2 else i - 1))
    near = swap(near, other_core)
    factors = forward_call(near, head, hbm, sky_index)
    flux, sums = backward_call(wave, far, factors)
    got = swap(sums, other_core)
    flux, got = lax.optimization_barrier((flux, got))
    other = swap(flux, other_core)
    sums = jnp.where(odd, jnp.concatenate([got, sums]), jnp.concatenate([sums, got]))
    if spec == 4:
        first = swap(sums, lambda s, i: (s ^ (2 if i % 2 else 1), i ^ 1))
        third = swap(sums, lambda s, i: (s ^ 3, i ^ 1))
        second = swap(first, other_core)
        sums = (sums + jnp.where(odd, first, second)) + (jnp.where(odd, second, first) + third)
    else:
        for k in powers(1, spec):
            sums = sums + swap(sums, lambda s, i: (s ^ k, i))
    regress, sky = regress_call(total_rows, flux, other, sums)
    if wave == 8:
        first = swap(regress, lambda s, i: (s, i ^ (6 if i % 2 else 4)))
        third = swap(regress, lambda s, i: (s, i ^ (3 if i % 2 else 1)))
        fetched = first + jnp.where(odd, 0.0, third)
        terms = [regress, fetched, swap(fetched, other_core)]
    else:
        for k in powers(2, wave):
            regress = regress + swap(regress, lambda s, i: (s, i ^ k if i % 2 else -1))
        terms = [jnp.where(odd, regress, swap(regress, other_core))]
    cleaned, sky = clean_call(total_rows, flux, sky, terms)
    return (jnp.transpose(cleaned, (0, 2, 1, 3)), sky[:, :rows])


def solution(mesh):
    block = P(None, "spec", "wave", None)
    return jax.shard_map(
        local,
        mesh=mesh,
        in_specs=(block,) * 5 + (P("spec", None),),
        out_specs=(block, P(None, "wave")),
        check_vma=False,
    )
```

```python
import functools

import jax
import jax.numpy as jnp
from jax import lax
from jax.experimental import pallas as pl
from jax.experimental.pallas import tpu as pltpu
from jax.sharding import PartitionSpec as P

REG = 0.05
RIDGE = 1.0
HALO = 4
PARTS = 6
TAIL = 13
CUTS = (0, 14, 26, 35, 40)
LANES = 128

F32 = jnp.float32
VM = pl.BlockSpec(memory_space=pltpu.VMEM)
SM = pl.BlockSpec(memory_space=pltpu.SMEM)
HB = pl.BlockSpec(memory_space=pltpu.HBM)


def in_vmem(shape, dtype=F32):
    return jax.ShapeDtypeStruct(shape, dtype)


def recip(values):
    return 1.0 / values


def weight_of(ivar, mask):
    return jnp.where(mask == 0, ivar, 0.0)


def edge_message(p, w, l, r):
    wl = [a * b for a, b in zip(w, l)]
    wr = [a * b for a, b in zip(w, r)]
    d0 = w[0] + wl[1] * l[1] + REG
    d1 = w[1] + wr[0] * r[0] + wl[2] * l[2] + REG
    d2 = w[2] + wr[1] * r[1] + wl[3] * l[3] + REG
    d3 = w[3] + wr[2] * r[2]
    d4 = wr[3] * r[3]
    raw = d4
    a01 = wr[0] + wl[1]
    a12 = wr[1] + wl[2]
    a23 = wr[2] + wl[3]
    a34 = wr[3]
    a02 = wl[1] * r[1]
    a13 = wl[2] * r[2]
    a24 = wl[3] * r[3]
    b0 = w[0] * p[0] + wl[1] * p[1]
    b1 = w[1] * p[1] + wr[0] * p[0] + wl[2] * p[2]
    b2 = w[2] * p[2] + wr[1] * p[1] + wl[3] * p[3]
    b3 = w[3] * p[3] + wr[2] * p[2]
    b4 = wr[3] * p[3]
    inv = recip(d0)
    near, far = a01 * inv, a02 * inv
    d1, a12, d2 = d1 - near * a01, a12 - near * a02, d2 - far * a02
    b1, b2 = b1 - near * b0, b2 - far * b0
    inv = recip(d1)
    near, far = a12 * inv, a13 * inv
    d2, a23, d3 = d2 - near * a12, a23 - near * a13, d3 - far * a13
    b2, b3 = b2 - near * b1, b3 - far * b1
    inv = recip(d2)
    near, far = a23 * inv, a24 * inv
    d3, a34, d4 = d3 - near * a23, a34 - near * a24, d4 - far * a24
    b3, b4 = b3 - near * b2, b4 - far * b2
    return (d3, a34, d4, b3, b4, raw)


def edge_kernel(pix, iva, msk, lef, rig, near_out, far_out, head, bufs, mhead, mbuf, sems):
    exposures, rows, specs, fibres = pix.shape
    size = head.shape[1]
    odd = lax.rem(lax.axis_index("wave"), 2)
    first, last = (1 - odd) * (rows - size), odd * (rows - HALO)
    for e in range(exposures):
        for slot, ref in enumerate((pix, iva, lef, rig)):
            pltpu.make_async_copy(
                ref.at[e, pl.ds(first, size)], head.at[slot, :, :, e], sems.at[0]
            ).start()
        pltpu.make_async_copy(msk.at[e, pl.ds(first, size)], mhead.at[:, :, e], sems.at[1]).start()
    for e in range(exposures):
        for slot, ref in enumerate((pix, iva, lef, rig)):
            pltpu.make_async_copy(
                ref.at[e, pl.ds(last, HALO)], bufs.at[slot, :, :, e], sems.at[2]
            ).start()
        pltpu.make_async_copy(msk.at[e, pl.ds(last, HALO)], mbuf.at[:, :, e], sems.at[3]).start()
    before, after = 3 - odd, 2 + odd
    pltpu.make_async_copy(head, head, sems.at[0]).wait()
    pltpu.make_async_copy(mhead, mhead, sems.at[1]).wait()
    for k in range(size):
        for s in range(specs):
            head[1, k, s] = weight_of(head[1, k, s], mhead[k, s])
    order = [odd * k + (1 - odd) * (size - 1 - k) for k in range(HALO - 1, -1, -1)]
    for s in range(specs):
        p, w, l, r = [[head[slot, k, s] for k in order] for slot in (0, 1, before, after)]
        for slot, value in enumerate(edge_message(p, w, r, l)):
            near_out[slot, s] = value
    pltpu.make_async_copy(bufs, bufs, sems.at[2]).wait()
    pltpu.make_async_copy(mbuf, mbuf, sems.at[3]).wait()
    order = [odd * k + (1 - odd) * (HALO - 1 - k) for k in range(HALO)]
    for s in range(specs):
        p, l, r = [[bufs[slot, k, s] for k in order] for slot in (0, before, after)]
        w = [weight_of(bufs[1, k, s], mbuf[k, s]) for k in order]
        for slot, value in enumerate(edge_message(p, w, l, r)):
            far_out[slot, s] = value


def edge_call(arrays):
    exposures, rows, specs, fibres = arrays[0].shape
    size = max(HALO, rows // 5)
    message = in_vmem((PARTS, specs, exposures, fibres))
    return pl.pallas_call(
        edge_kernel,
        out_shape=(message, message, in_vmem((4, size, specs, exposures, fibres))),
        in_specs=[HB] * 5,
        out_specs=(VM, VM, VM),
        scratch_shapes=[
            pltpu.VMEM((4, HALO, specs, exposures, fibres), F32),
            pltpu.VMEM((size, specs, exposures, fibres), jnp.int32),
            pltpu.VMEM((HALO, specs, exposures, fibres), jnp.int32),
            pltpu.SemaphoreType.DMA((4,)),
        ],
        compiler_params=pltpu.CompilerParams(vmem_limit_bytes=8 * 2**20),
        cost_estimate=pl.CostEstimate(flops=10**6, bytes_accessed=10**6, transcendentals=0),
        name="edges",
    )(*arrays)


def forward_kernel(
    near, head, pix, iva, msk, lef, rig, sky_index, lower, lower_far, half, shares, tail, sky_mask, denom, bufs, mbuf, sems
):
    exposures, rows, specs, fibres = pix.shape
    size = head.shape[1]
    odd = lax.rem(lax.axis_index("wave"), 2)
    spans = range(specs)
    bounds = [0] + [size + (rows - size) * part // 40 for part in CUTS]

    def place(low, high):
        return pl.ds(odd * low + (1 - odd) * (rows - high), high - low)

    for c in range(1, len(CUTS)):
        here = place(bounds[c], bounds[c + 1])
        for e in range(exposures):
            for slot, ref in enumerate((pix, iva, lef, rig)):
                pltpu.make_async_copy(
                    ref.at[e, here], bufs.at[slot, here, :, e], sems.at[0, c - 1]
                ).start()
            pltpu.make_async_copy(msk.at[e, here], mbuf.at[here, :, e], sems.at[1, c - 1]).start()
    lane = lax.broadcasted_iota(jnp.int32, (exposures, fibres), 1)
    for s in spans:
        found = lane == sky_index[s, 0]
        for k in range(1, sky_index.shape[1]):
            found = found | (lane == sky_index[s, k])
        sky_mask[s] = jnp.where(found, 1.0, 0.0)

    spot = lax.broadcasted_iota(jnp.int32, (exposures, LANES), 1)
    before, after = 3 - odd, 2 + odd

    def share(k, parts, total):
        parts = [sky_mask[s] * parts[s] for s in spans]
        for s in spans:
            shares[k, s] = parts[s]
        row = odd * k + (1 - odd) * (rows - 1 - k)
        return jnp.where(spot == row, jnp.sum(sum(parts), axis=1, keepdims=True), total)

    made = [dict(d1=REG, b1=0.0, d2=REG, b2=0.0, r1=0.0) for _ in spans]
    offs = [[] for _ in spans]
    fars = [[] for _ in spans]
    states = [None] * specs
    total = jnp.zeros((exposures, LANES), F32)
    for c in range(len(CUTS)):
        if c > 0:
            here = place(bounds[c], bounds[c + 1])
            part, mpart = bufs.at[:, here], mbuf.at[here]
            pltpu.make_async_copy(part, part, sems.at[0, c - 1]).wait()
            pltpu.make_async_copy(mpart, mpart, sems.at[1, c - 1]).wait()
        for k in range(bounds[c], bounds[c + 1]):
            row = odd * k + (1 - odd) * (rows - 1 - k)
            top = odd * k + (1 - odd) * (size - 1 - k)
            diags = []
            for s in spans:
                if c == 0:
                    p, w, l, r = [head[slot, top, s] for slot in (0, 1, before, after)]
                else:
                    p, l, r = bufs[0, row, s], bufs[before, row, s], bufs[after, row, s]
                    w = weight_of(bufs[1, row, s], mbuf[row, s])
                wl, wr, wp = w * l, w * r, w * p
                m = made[s]
                d, b = m["d1"] + wl * l, m["b1"] + wl * p
                offs[s].append(m["r1"] + wl)
                fars[s].append(wl * r)
                made[s] = dict(
                    d1=w + m["d2"], b1=wp + m["b2"], d2=wr * r + REG, b2=wr * p, r1=wr
                )
                if k == 0:
                    d, b = d + near[0, s], b + near[3, s]
                    offs[s][0] = offs[s][0] + near[1, s]
                    inv = recip(d)
                    states[s] = (inv, None, None, b, None)
                elif k == 1:
                    diags.append(d + near[5, s])
                    d, b = d + near[2, s], b + near[4, s]
                    inv1, _, _, y1, _ = states[s]
                    upper = offs[s][0]
                    g = upper * inv1
                    inv, y = recip(d - g * upper), b - g * y1
                    lower[1, s], half[1, s] = g, y * inv
                    states[s] = (inv, inv1, g, y, y1)
                else:
                    diags.append(d)
                    f, g, y, states[s] = eliminate(states[s], d, offs[s][k - 1], b, fars[s][k - 2])
                    lower_far[k, s], lower[k, s], half[k, s] = f, g, y * states[s][0]
            if k > 0:
                total = share(k - 1, diags, total)
    for s in spans:
        m = made[s]
        tail_parts = states[s] + (
            m["d1"], offs[s][rows - 1], m["b1"], fars[s][rows - 2], m["d2"], m["r1"], m["b2"], fars[s][rows - 1]
        )
        for slot, value in enumerate(tail_parts):
            tail[slot, s] = value
    denom[...] = share(rows - 1, [made[s]["d1"] for s in spans], total)


def eliminate(state, d, a, b, far_a):
    inv1, inv2, mult1, y1, y2 = state
    f = far_a * inv2
    upper = a - far_a * mult1
    g = upper * inv1
    pivot = d - f * far_a - g * upper
    y = b - f * y2 - g * y1
    return f, g, y, (recip(pivot), inv1, g, y, y1)


def forward_call(near, head, arrays, sky_index):
    exposures, rows, specs, fibres = arrays[0].shape
    chunks = len(CUTS) - 1
    whole = in_vmem((rows, specs, exposures, fibres))
    return pl.pallas_call(
        forward_kernel,
        out_shape=(
            whole,
            whole,
            whole,
            whole,
            in_vmem((TAIL, specs, exposures, fibres)),
            in_vmem((specs, exposures, fibres)),
            in_vmem((exposures, LANES)),
        ),
        in_specs=[VM] * 2 + [HB] * 5 + [SM],
        out_specs=(VM,) * 7,
        scratch_shapes=[
            pltpu.VMEM((4, rows, specs, exposures, fibres), F32),
            pltpu.VMEM((rows, specs, exposures, fibres), jnp.int32),
            pltpu.SemaphoreType.DMA((2, chunks)),
        ],
        compiler_params=pltpu.CompilerParams(vmem_limit_bytes=24 * 2**20),
        cost_estimate=pl.CostEstimate(flops=10**7, bytes_accessed=10**7, transcendentals=0),
        name="forward",
    )(near, head, *arrays, sky_index)


def backward_kernel(wave, far, lower, lower_far, half, shares, tail, sky_mask, denom, flux, sums):
    rows, specs, exposures, fibres = lower.shape
    device = lax.axis_index("wave")
    odd = lax.rem(device, 2)
    at_end = (device == 0) | (device == wave - 1)
    lane = lax.broadcasted_iota(jnp.int32, (exposures, LANES), 1)
    spans = range(specs)

    def message(part, s):
        return jnp.where(at_end, 0.0, far[part, s])

    def place(k):
        return odd * k + (1 - odd) * (rows - 1 - k)

    def total(parts):
        return jnp.sum(parts, axis=1, keepdims=True)

    def spread(k, numer, parts, values):
        return jnp.where(lane == place(k), total(sum(parts[s] * values[s] for s in spans)), numer)

    after, extra = [], []
    for s in spans:
        t = [tail[slot, s] for slot in range(TAIL)]
        f, g, y, state = eliminate(t[:5], t[5] + message(2, s), t[6], t[7] + message(4, s), t[8])
        f1, g1, y1, last = eliminate(
            state, t[9] + message(0, s), t[10] + message(1, s), t[11] + message(3, s), t[12]
        )
        beyond = y1 * last[0]
        value = y * state[0] - g1 * beyond
        flux[place(rows - 1), s] = value
        after.append((value, beyond, g, f1, f))
        extra.append(sky_mask[s] * message(5, s))
    parts = [shares[rows - 1, s] + extra[s] for s in spans]
    numer = jnp.zeros((exposures, LANES), F32)
    numer = spread(rows - 1, numer, parts, [after[s][0] for s in spans])
    sums[1] = denom[...] + jnp.where(lane == place(rows - 1), total(sum(extra)), 0.0)

    def step(k, numer, after, bottom=False):
        results = []
        for s in spans:
            x1, x2, g1, f2, f1 = after[s]
            value = half[k, s] - g1 * x1 - f2 * x2
            flux[place(k - 1), s] = value
            results.append((value, x1) if bottom else (value, x1, lower[k, s], f1, lower_far[k, s]))
        parts = [shares[k - 1, s] for s in spans]
        return spread(k - 1, numer, parts, [r[0] for r in results]), tuple(results)

    for k in range(rows - 1, 1, -1):
        numer, after = step(k, numer, after)
    numer, after = step(1, numer, after, bottom=True)
    sums[0] = numer


def backward_call(wave, far, factors):
    rows, specs, exposures, fibres = factors[0].shape
    return pl.pallas_call(
        functools.partial(backward_kernel, wave),
        out_shape=(in_vmem((rows, specs, exposures, fibres)), in_vmem((2, exposures, LANES))),
        in_specs=[VM] * 8,
        out_specs=(VM, VM),
        compiler_params=pltpu.CompilerParams(vmem_limit_bytes=24 * 2**20),
        cost_estimate=pl.CostEstimate(flops=10**7, bytes_accessed=10**7, transcendentals=0),
        name="backward",
    )(far, *factors)


def position_of(index, total_rows):
    return 2.0 * jnp.asarray(index).astype(F32) / (total_rows - 1) - 1.0


def regress_kernel(total_rows, flux, other, sums, regress, sky_out):
    rows, specs, exposures, fibres = flux.shape
    lanes = regress.shape[2]
    device = lax.axis_index("wave")
    odd = lax.rem(device, 2)
    lane = lax.broadcasted_iota(jnp.int32, (exposures, LANES), 1)
    valid = lane < rows
    step = 2.0 / (total_rows - 1)
    plain = [0.0] * specs
    tilted = [0.0] * specs
    moments = [0.0] * 3
    for which, (ref, core) in enumerate(((flux, odd), (other, 1 - odd))):
        owner = device - odd + core
        sky = jnp.where(valid, sums[2 * core] / jnp.where(valid, sums[2 * core + 1], 1.0), 0.0)
        position = position_of(owner * rows + lane, total_rows)
        slanted = sky * position
        moments[0] += jnp.sum(sky * sky, axis=1, keepdims=True)
        moments[1] += jnp.sum(sky * slanted, axis=1, keepdims=True)
        moments[2] += jnp.sum(slanted * slanted, axis=1, keepdims=True)
        if which == 0:
            sky_out[...] = sky
        end = position_of(owner * rows + rows, total_rows)
        running = [None] * specs
        summed = [None] * specs
        for k in range(rows):
            sky_k = jnp.broadcast_to(sky[:, k : k + 1], (exposures, fibres))
            for s in range(specs):
                term = ref[k, s] * sky_k
                running[s] = term if k == 0 else running[s] + term
                summed[s] = running[s] if k == 0 else summed[s] + running[s]
        for s in range(specs):
            plain[s] += running[s]
            tilted[s] += end * running[s] - step * summed[s]
    wide = lax.broadcasted_iota(jnp.int32, (exposures, lanes - fibres), 1)
    held = jnp.where(wide == 0, moments[0], jnp.where(wide == 1, moments[1], moments[2]))
    for s in range(specs):
        regress[s, :, :fibres] = plain[s]
        regress[specs + s, :, :fibres] = tilted[s]
        for r in (s, specs + s):
            regress[r, :, fibres:] = held


def regress_call(total_rows, flux, other, sums):
    rows, specs, exposures, fibres = flux.shape
    lanes = -(-(fibres + 3) // LANES) * LANES
    return pl.pallas_call(
        functools.partial(regress_kernel, total_rows),
        out_shape=(
            in_vmem((2 * specs, exposures, lanes)),
            in_vmem((exposures, LANES)),
        ),
        in_specs=[VM] * 3,
        out_specs=(VM, VM),
        compiler_params=pltpu.CompilerParams(vmem_limit_bytes=24 * 2**20),
        cost_estimate=pl.CostEstimate(flops=10**6, bytes_accessed=10**6, transcendentals=0),
        name="regress",
    )(flux, other, sums)


def clean_kernel(total_rows, flux, sky_ref, *refs):
    *terms, out, sky_out, buf, sems, sky_sem = refs
    rows, specs, exposures, fibres = flux.shape
    sky_copy = pltpu.make_async_copy(sky_ref, sky_out, sky_sem)
    sky_copy.start()
    device = lax.axis_index("wave")

    def got(slot):
        return sum(term[slot] for term in terms)

    sums = [got(slot) for slot in range(2 * specs)]
    moments = [sums[0][:, fibres + m : fibres + m + 1] for m in range(3)]
    upper_left, cross, lower_right = moments[0] + RIDGE, moments[1], moments[2] + RIDGE
    inverse = 1.0 / (upper_left * lower_right - cross * cross)
    start = position_of(device * rows, total_rows)
    step = 2.0 / (total_rows - 1)
    level, change = [], []
    for s in range(specs):
        r1, r2 = sums[s][:, :fibres], sums[specs + s][:, :fibres]
        slope_a = (lower_right * r1 - cross * r2) * inverse
        slope_b = (upper_left * r2 - cross * r1) * inverse
        level.append(slope_a + slope_b * start)
        change.append(slope_b * step)
    sky = sky_ref[...]
    chunks = sems.shape[0]
    bounds = [rows * c // chunks for c in range(chunks + 1)]
    for c in range(chunks):
        low, high = bounds[c], bounds[c + 1]
        for k in range(low, high):
            sky_k = jnp.broadcast_to(sky[:, k : k + 1], (exposures, fibres))
            for s in range(specs):
                buf[k, s] = flux[k, s] - level[s] * sky_k
                level[s] = level[s] + change[s]
        for e in range(exposures):
            pltpu.make_async_copy(
                buf.at[low:high, :, e], out.at[e, low:high], sems.at[c]
            ).start()
    for c in range(chunks):
        part = buf.at[bounds[c] : bounds[c + 1]]
        pltpu.make_async_copy(part, part, sems.at[c]).wait()
    sky_copy.wait()


def clean_call(total_rows, flux, sky, terms):
    rows, specs, exposures, fibres = flux.shape
    return pl.pallas_call(
        functools.partial(clean_kernel, total_rows),
        out_shape=(
            jax.ShapeDtypeStruct((exposures, rows, specs, fibres), F32),
            jax.ShapeDtypeStruct((exposures, LANES), F32),
        ),
        in_specs=[VM] * (2 + len(terms)),
        out_specs=(HB, HB),
        scratch_shapes=[
            pltpu.VMEM((rows, specs, exposures, fibres), F32),
            pltpu.SemaphoreType.DMA((4,)),
            pltpu.SemaphoreType.DMA,
        ],
        compiler_params=pltpu.CompilerParams(vmem_limit_bytes=24 * 2**20),
        cost_estimate=pl.CostEstimate(flops=10**6, bytes_accessed=10**6, transcendentals=0),
        name="clean",
    )(flux, sky, *terms)


def powers(low, high):
    steps = []
    while low < high:
        steps.append(low)
        low *= 2
    return steps


def swap(values, partner):
    spec, wave = lax.axis_size("spec"), lax.axis_size("wave")
    pairs = []
    for s in range(spec):
        for i in range(wave):
            t, j = partner(s, i)
            if not 0 <= j < wave:
                t, j = s ^ 1, i
            if t < spec:
                pairs.append((s * wave + i, t * wave + j))
    return lax.ppermute(values, ("spec", "wave"), pairs)


def local(pixels, ivar, mask, psf_left, psf_right, sky_index):
    arrays = [jnp.transpose(x, (0, 2, 1, 3)) for x in (pixels, ivar, mask, psf_left, psf_right)]
    rows = pixels.shape[2]
    wave, spec = lax.axis_size("wave"), lax.axis_size("spec")
    total_rows = rows * wave
    hbm = [pltpu.with_memory_space_constraint(x, pltpu.HBM) for x in arrays]
    odd = lax.rem(lax.axis_index("wave"), 2) == 1

    def other_core(s, i):
        return (s, i ^ 1)

    near, far, head = edge_call(hbm)
    far = swap(far, lambda s, i: (s, i + 1 if i % 2 else i - 1))
    near = swap(near, other_core)
    factors = forward_call(near, head, hbm, sky_index)
    flux, sums = backward_call(wave, far, factors)
    got = swap(sums, other_core)
    flux, got = lax.optimization_barrier((flux, got))
    other = swap(flux, other_core)
    sums = jnp.where(odd, jnp.concatenate([got, sums]), jnp.concatenate([sums, got]))
    if spec == 4:
        first = swap(sums, lambda s, i: (s ^ (2 if i % 2 else 1), i ^ 1))
        third = swap(sums, lambda s, i: (s ^ 3, i ^ 1))
        second = swap(first, other_core)
        sums = (sums + jnp.where(odd, first, second)) + (jnp.where(odd, second, first) + third)
    else:
        for k in powers(1, spec):
            sums = sums + swap(sums, lambda s, i: (s ^ k, i))
    regress, sky = regress_call(total_rows, flux, other, sums)
    if wave == 8:
        routes = ((1, 0, 3, 2), (2, 3, 1, 0))
        third_route = (3, 2, 0, 1)
        first = swap(regress, lambda s, i: (s, 2 * routes[i % 2][i // 2] + i % 2))
        third = swap(regress, lambda s, i: (s, 2 * third_route[i // 2] + 1 - i % 2))
        terms = [regress, first, swap(first, other_core), third]
    else:
        for k in powers(2, wave):
            regress = regress + swap(regress, lambda s, i: (s, i ^ k if i % 2 else -1))
        terms = [jnp.where(odd, regress, swap(regress, other_core))]
    cleaned, sky = clean_call(total_rows, flux, sky, terms)
    return (jnp.transpose(cleaned, (0, 2, 1, 3)), sky[:, :rows])


def solution(mesh):
    block = P(None, "spec", "wave", None)
    return jax.shard_map(
        local,
        mesh=mesh,
        in_specs=(block,) * 5 + (P("spec", None),),
        out_specs=(block, P(None, "wave")),
        check_vma=False,
    )
```

```python
import functools

import jax
import jax.numpy as jnp
from jax import lax
from jax.experimental import pallas as pl
from jax.experimental.pallas import tpu as pltpu
from jax.sharding import PartitionSpec as P

REG = 0.05
RIDGE = 1.0
HALO = 4
PARTS = 6
TAIL = 13
CUTS = (0, 14, 26, 35, 40)
LANES = 128

F32 = jnp.float32
VM = pl.BlockSpec(memory_space=pltpu.VMEM)
SM = pl.BlockSpec(memory_space=pltpu.SMEM)
HB = pl.BlockSpec(memory_space=pltpu.HBM)


def in_vmem(shape, dtype=F32):
    return jax.ShapeDtypeStruct(shape, dtype)


def recip(values):
    return 1.0 / values


def weight_of(ivar, mask):
    return jnp.where(mask == 0, ivar, 0.0)


def edge_message(p, w, l, r):
    wl = [a * b for a, b in zip(w, l)]
    wr = [a * b for a, b in zip(w, r)]
    d0 = w[0] + wl[1] * l[1] + REG
    d1 = w[1] + wr[0] * r[0] + wl[2] * l[2] + REG
    d2 = w[2] + wr[1] * r[1] + wl[3] * l[3] + REG
    d3 = w[3] + wr[2] * r[2]
    d4 = wr[3] * r[3]
    raw = d4
    a01 = wr[0] + wl[1]
    a12 = wr[1] + wl[2]
    a23 = wr[2] + wl[3]
    a34 = wr[3]
    a02 = wl[1] * r[1]
    a13 = wl[2] * r[2]
    a24 = wl[3] * r[3]
    b0 = w[0] * p[0] + wl[1] * p[1]
    b1 = w[1] * p[1] + wr[0] * p[0] + wl[2] * p[2]
    b2 = w[2] * p[2] + wr[1] * p[1] + wl[3] * p[3]
    b3 = w[3] * p[3] + wr[2] * p[2]
    b4 = wr[3] * p[3]
    inv = recip(d0)
    near, far = a01 * inv, a02 * inv
    d1, a12, d2 = d1 - near * a01, a12 - near * a02, d2 - far * a02
    b1, b2 = b1 - near * b0, b2 - far * b0
    inv = recip(d1)
    near, far = a12 * inv, a13 * inv
    d2, a23, d3 = d2 - near * a12, a23 - near * a13, d3 - far * a13
    b2, b3 = b2 - near * b1, b3 - far * b1
    inv = recip(d2)
    near, far = a23 * inv, a24 * inv
    d3, a34, d4 = d3 - near * a23, a34 - near * a24, d4 - far * a24
    b3, b4 = b3 - near * b2, b4 - far * b2
    return (d3, a34, d4, b3, b4, raw)


def edge_kernel(pix, iva, msk, lef, rig, near_out, far_out, head, bufs, mhead, mbuf, sems):
    exposures, rows, specs, fibres = pix.shape
    size = head.shape[1]
    odd = lax.rem(lax.axis_index("wave"), 2)
    first, last = (1 - odd) * (rows - size), odd * (rows - HALO)
    for e in range(exposures):
        for slot, ref in enumerate((pix, iva, lef, rig)):
            pltpu.make_async_copy(
                ref.at[e, pl.ds(first, size)], head.at[slot, :, :, e], sems.at[0]
            ).start()
        pltpu.make_async_copy(msk.at[e, pl.ds(first, size)], mhead.at[:, :, e], sems.at[1]).start()
    for e in range(exposures):
        for slot, ref in enumerate((pix, iva, lef, rig)):
            pltpu.make_async_copy(
                ref.at[e, pl.ds(last, HALO)], bufs.at[slot, :, :, e], sems.at[2]
            ).start()
        pltpu.make_async_copy(msk.at[e, pl.ds(last, HALO)], mbuf.at[:, :, e], sems.at[3]).start()
    before, after = 3 - odd, 2 + odd
    pltpu.make_async_copy(head, head, sems.at[0]).wait()
    pltpu.make_async_copy(mhead, mhead, sems.at[1]).wait()
    for k in range(size):
        for s in range(specs):
            head[1, k, s] = weight_of(head[1, k, s], mhead[k, s])
    order = [odd * k + (1 - odd) * (size - 1 - k) for k in range(HALO - 1, -1, -1)]
    for s in range(specs):
        p, w, l, r = [[head[slot, k, s] for k in order] for slot in (0, 1, before, after)]
        for slot, value in enumerate(edge_message(p, w, r, l)):
            near_out[slot, s] = value
    pltpu.make_async_copy(bufs, bufs, sems.at[2]).wait()
    pltpu.make_async_copy(mbuf, mbuf, sems.at[3]).wait()
    order = [odd * k + (1 - odd) * (HALO - 1 - k) for k in range(HALO)]
    for s in range(specs):
        p, l, r = [[bufs[slot, k, s] for k in order] for slot in (0, before, after)]
        w = [weight_of(bufs[1, k, s], mbuf[k, s]) for k in order]
        for slot, value in enumerate(edge_message(p, w, l, r)):
            far_out[slot, s] = value


def edge_call(arrays):
    exposures, rows, specs, fibres = arrays[0].shape
    size = max(HALO, rows * 4 // 25)
    message = in_vmem((PARTS, specs, exposures, fibres))
    return pl.pallas_call(
        edge_kernel,
        out_shape=(message, message, in_vmem((4, size, specs, exposures, fibres))),
        in_specs=[HB] * 5,
        out_specs=(VM, VM, VM),
        scratch_shapes=[
            pltpu.VMEM((4, HALO, specs, exposures, fibres), F32),
            pltpu.VMEM((size, specs, exposures, fibres), jnp.int32),
            pltpu.VMEM((HALO, specs, exposures, fibres), jnp.int32),
            pltpu.SemaphoreType.DMA((4,)),
        ],
        compiler_params=pltpu.CompilerParams(vmem_limit_bytes=8 * 2**20),
        cost_estimate=pl.CostEstimate(flops=10**6, bytes_accessed=10**6, transcendentals=0),
        name="edges",
    )(*arrays)


def forward_kernel(
    near, head, pix, iva, msk, lef, rig, sky_index, lower, lower_far, half, shares, tail, sky_mask, denom, bufs, mbuf, sems
):
    exposures, rows, specs, fibres = pix.shape
    size = head.shape[1]
    odd = lax.rem(lax.axis_index("wave"), 2)
    spans = range(specs)
    bounds = [0] + [size + (rows - size) * part // 40 for part in CUTS]

    def place(low, high):
        return pl.ds(odd * low + (1 - odd) * (rows - high), high - low)

    for c in range(1, len(CUTS)):
        here = place(bounds[c], bounds[c + 1])
        for e in range(exposures):
            for slot, ref in enumerate((pix, iva, lef, rig)):
                pltpu.make_async_copy(
                    ref.at[e, here], bufs.at[slot, here, :, e], sems.at[0, c - 1]
                ).start()
            pltpu.make_async_copy(msk.at[e, here], mbuf.at[here, :, e], sems.at[1, c - 1]).start()
    lane = lax.broadcasted_iota(jnp.int32, (exposures, fibres), 1)
    for s in spans:
        found = lane == sky_index[s, 0]
        for k in range(1, sky_index.shape[1]):
            found = found | (lane == sky_index[s, k])
        sky_mask[s] = jnp.where(found, 1.0, 0.0)

    spot = lax.broadcasted_iota(jnp.int32, (exposures, LANES), 1)
    before, after = 3 - odd, 2 + odd

    def share(k, parts, total):
        parts = [sky_mask[s] * parts[s] for s in spans]
        for s in spans:
            shares[k, s] = parts[s]
        row = odd * k + (1 - odd) * (rows - 1 - k)
        return jnp.where(spot == row, jnp.sum(sum(parts), axis=1, keepdims=True), total)

    made = [dict(d1=REG, b1=0.0, d2=REG, b2=0.0, r1=0.0) for _ in spans]
    offs = [[] for _ in spans]
    fars = [[] for _ in spans]
    states = [None] * specs
    total = jnp.zeros((exposures, LANES), F32)
    for c in range(len(CUTS)):
        if c > 0:
            here = place(bounds[c], bounds[c + 1])
            part, mpart = bufs.at[:, here], mbuf.at[here]
            pltpu.make_async_copy(part, part, sems.at[0, c - 1]).wait()
            pltpu.make_async_copy(mpart, mpart, sems.at[1, c - 1]).wait()
        for k in range(bounds[c], bounds[c + 1]):
            row = odd * k + (1 - odd) * (rows - 1 - k)
            top = odd * k + (1 - odd) * (size - 1 - k)
            diags = []
            for s in spans:
                if c == 0:
                    p, w, l, r = [head[slot, top, s] for slot in (0, 1, before, after)]
                else:
                    p, l, r = bufs[0, row, s], bufs[before, row, s], bufs[after, row, s]
                    w = weight_of(bufs[1, row, s], mbuf[row, s])
                wl, wr, wp = w * l, w * r, w * p
                m = made[s]
                d, b = m["d1"] + wl * l, m["b1"] + wl * p
                offs[s].append(m["r1"] + wl)
                fars[s].append(wl * r)
                made[s] = dict(
                    d1=w + m["d2"], b1=wp + m["b2"], d2=wr * r + REG, b2=wr * p, r1=wr
                )
                if k == 0:
                    d, b = d + near[0, s], b + near[3, s]
                    offs[s][0] = offs[s][0] + near[1, s]
                    inv = recip(d)
                    states[s] = (inv, None, None, b, None)
                elif k == 1:
                    diags.append(d + near[5, s])
                    d, b = d + near[2, s], b + near[4, s]
                    inv1, _, _, y1, _ = states[s]
                    upper = offs[s][0]
                    g = upper * inv1
                    inv, y = recip(d - g * upper), b - g * y1
                    lower[1, s], half[1, s] = g, y * inv
                    states[s] = (inv, inv1, g, y, y1)
                else:
                    diags.append(d)
                    f, g, y, states[s] = eliminate(states[s], d, offs[s][k - 1], b, fars[s][k - 2])
                    lower_far[k, s], lower[k, s], half[k, s] = f, g, y * states[s][0]
            if k > 0:
                total = share(k - 1, diags, total)
    for s in spans:
        m = made[s]
        tail_parts = states[s] + (
            m["d1"], offs[s][rows - 1], m["b1"], fars[s][rows - 2], m["d2"], m["r1"], m["b2"], fars[s][rows - 1]
        )
        for slot, value in enumerate(tail_parts):
            tail[slot, s] = value
    denom[...] = share(rows - 1, [made[s]["d1"] for s in spans], total)


def eliminate(state, d, a, b, far_a):
    inv1, inv2, mult1, y1, y2 = state
    f = far_a * inv2
    upper = a - far_a * mult1
    g = upper * inv1
    pivot = d - f * far_a - g * upper
    y = b - f * y2 - g * y1
    return f, g, y, (recip(pivot), inv1, g, y, y1)


def forward_call(near, head, arrays, sky_index):
    exposures, rows, specs, fibres = arrays[0].shape
    chunks = len(CUTS) - 1
    whole = in_vmem((rows, specs, exposures, fibres))
    return pl.pallas_call(
        forward_kernel,
        out_shape=(
            whole,
            whole,
            whole,
            whole,
            in_vmem((TAIL, specs, exposures, fibres)),
            in_vmem((specs, exposures, fibres)),
            in_vmem((exposures, LANES)),
        ),
        in_specs=[VM] * 2 + [HB] * 5 + [SM],
        out_specs=(VM,) * 7,
        scratch_shapes=[
            pltpu.VMEM((4, rows, specs, exposures, fibres), F32),
            pltpu.VMEM((rows, specs, exposures, fibres), jnp.int32),
            pltpu.SemaphoreType.DMA((2, chunks)),
        ],
        compiler_params=pltpu.CompilerParams(vmem_limit_bytes=24 * 2**20),
        cost_estimate=pl.CostEstimate(flops=10**7, bytes_accessed=10**7, transcendentals=0),
        name="forward",
    )(near, head, *arrays, sky_index)


def backward_kernel(wave, far, lower, lower_far, half, shares, tail, sky_mask, denom, flux, sums):
    rows, specs, exposures, fibres = lower.shape
    device = lax.axis_index("wave")
    odd = lax.rem(device, 2)
    at_end = (device == 0) | (device == wave - 1)
    lane = lax.broadcasted_iota(jnp.int32, (exposures, LANES), 1)
    spans = range(specs)

    def message(part, s):
        return jnp.where(at_end, 0.0, far[part, s])

    def place(k):
        return odd * k + (1 - odd) * (rows - 1 - k)

    def total(parts):
        return jnp.sum(parts, axis=1, keepdims=True)

    def spread(k, numer, parts, values):
        return jnp.where(lane == place(k), total(sum(parts[s] * values[s] for s in spans)), numer)

    after, extra = [], []
    for s in spans:
        t = [tail[slot, s] for slot in range(TAIL)]
        f, g, y, state = eliminate(t[:5], t[5] + message(2, s), t[6], t[7] + message(4, s), t[8])
        f1, g1, y1, last = eliminate(
            state, t[9] + message(0, s), t[10] + message(1, s), t[11] + message(3, s), t[12]
        )
        beyond = y1 * last[0]
        value = y * state[0] - g1 * beyond
        flux[place(rows - 1), s] = value
        after.append((value, beyond, g, f1, f))
        extra.append(sky_mask[s] * message(5, s))
    parts = [shares[rows - 1, s] + extra[s] for s in spans]
    numer = jnp.zeros((exposures, LANES), F32)
    numer = spread(rows - 1, numer, parts, [after[s][0] for s in spans])
    sums[1] = denom[...] + jnp.where(lane == place(rows - 1), total(sum(extra)), 0.0)

    def step(k, numer, after, bottom=False):
        results = []
        for s in spans:
            x1, x2, g1, f2, f1 = after[s]
            value = half[k, s] - g1 * x1 - f2 * x2
            flux[place(k - 1), s] = value
            results.append((value, x1) if bottom else (value, x1, lower[k, s], f1, lower_far[k, s]))
        parts = [shares[k - 1, s] for s in spans]
        return spread(k - 1, numer, parts, [r[0] for r in results]), tuple(results)

    for k in range(rows - 1, 1, -1):
        numer, after = step(k, numer, after)
    numer, after = step(1, numer, after, bottom=True)
    sums[0] = numer


def backward_call(wave, far, factors):
    rows, specs, exposures, fibres = factors[0].shape
    return pl.pallas_call(
        functools.partial(backward_kernel, wave),
        out_shape=(in_vmem((rows, specs, exposures, fibres)), in_vmem((2, exposures, LANES))),
        in_specs=[VM] * 8,
        out_specs=(VM, VM),
        compiler_params=pltpu.CompilerParams(vmem_limit_bytes=24 * 2**20),
        cost_estimate=pl.CostEstimate(flops=10**7, bytes_accessed=10**7, transcendentals=0),
        name="backward",
    )(far, *factors)


def position_of(index, total_rows):
    return 2.0 * jnp.asarray(index).astype(F32) / (total_rows - 1) - 1.0


def regress_kernel(total_rows, flux, other, sums, regress, sky_out):
    rows, specs, exposures, fibres = flux.shape
    lanes = regress.shape[2]
    device = lax.axis_index("wave")
    odd = lax.rem(device, 2)
    lane = lax.broadcasted_iota(jnp.int32, (exposures, LANES), 1)
    valid = lane < rows
    step = 2.0 / (total_rows - 1)
    plain = [0.0] * specs
    tilted = [0.0] * specs
    moments = [0.0] * 3
    for which, (ref, core) in enumerate(((flux, odd), (other, 1 - odd))):
        owner = device - odd + core
        sky = jnp.where(valid, sums[2 * core] / jnp.where(valid, sums[2 * core + 1], 1.0), 0.0)
        position = position_of(owner * rows + lane, total_rows)
        slanted = sky * position
        moments[0] += jnp.sum(sky * sky, axis=1, keepdims=True)
        moments[1] += jnp.sum(sky * slanted, axis=1, keepdims=True)
        moments[2] += jnp.sum(slanted * slanted, axis=1, keepdims=True)
        if which == 0:
            sky_out[...] = sky
        end = position_of(owner * rows + rows, total_rows)
        running = [None] * specs
        summed = [None] * specs
        for k in range(rows):
            sky_k = jnp.broadcast_to(sky[:, k : k + 1], (exposures, fibres))
            for s in range(specs):
                term = ref[k, s] * sky_k
                running[s] = term if k == 0 else running[s] + term
                summed[s] = running[s] if k == 0 else summed[s] + running[s]
        for s in range(specs):
            plain[s] += running[s]
            tilted[s] += end * running[s] - step * summed[s]
    wide = lax.broadcasted_iota(jnp.int32, (exposures, lanes - fibres), 1)
    held = jnp.where(wide == 0, moments[0], jnp.where(wide == 1, moments[1], moments[2]))
    for s in range(specs):
        regress[s, :, :fibres] = plain[s]
        regress[specs + s, :, :fibres] = tilted[s]
        for r in (s, specs + s):
            regress[r, :, fibres:] = held


def regress_call(total_rows, flux, other, sums):
    rows, specs, exposures, fibres = flux.shape
    lanes = -(-(fibres + 3) // LANES) * LANES
    return pl.pallas_call(
        functools.partial(regress_kernel, total_rows),
        out_shape=(
            in_vmem((2 * specs, exposures, lanes)),
            in_vmem((exposures, LANES)),
        ),
        in_specs=[VM] * 3,
        out_specs=(VM, VM),
        compiler_params=pltpu.CompilerParams(vmem_limit_bytes=24 * 2**20),
        cost_estimate=pl.CostEstimate(flops=10**6, bytes_accessed=10**6, transcendentals=0),
        name="regress",
    )(flux, other, sums)


def clean_kernel(total_rows, flux, sky_ref, *refs):
    *terms, out, sky_out, buf, sems, sky_sem = refs
    rows, specs, exposures, fibres = flux.shape
    sky_copy = pltpu.make_async_copy(sky_ref, sky_out, sky_sem)
    sky_copy.start()
    device = lax.axis_index("wave")

    def got(slot):
        return sum(term[slot] for term in terms)

    sums = [got(slot) for slot in range(2 * specs)]
    moments = [sums[0][:, fibres + m : fibres + m + 1] for m in range(3)]
    upper_left, cross, lower_right = moments[0] + RIDGE, moments[1], moments[2] + RIDGE
    inverse = 1.0 / (upper_left * lower_right - cross * cross)
    start = position_of(device * rows, total_rows)
    step = 2.0 / (total_rows - 1)
    level, change = [], []
    for s in range(specs):
        r1, r2 = sums[s][:, :fibres], sums[specs + s][:, :fibres]
        slope_a = (lower_right * r1 - cross * r2) * inverse
        slope_b = (upper_left * r2 - cross * r1) * inverse
        level.append(slope_a + slope_b * start)
        change.append(slope_b * step)
    sky = sky_ref[...]
    chunks = sems.shape[0]
    bounds = [rows * c // chunks for c in range(chunks + 1)]
    for c in range(chunks):
        low, high = bounds[c], bounds[c + 1]
        for k in range(low, high):
            sky_k = jnp.broadcast_to(sky[:, k : k + 1], (exposures, fibres))
            for s in range(specs):
                buf[k, s] = flux[k, s] - level[s] * sky_k
                level[s] = level[s] + change[s]
        for e in range(exposures):
            pltpu.make_async_copy(
                buf.at[low:high, :, e], out.at[e, low:high], sems.at[c]
            ).start()
    for c in range(chunks):
        part = buf.at[bounds[c] : bounds[c + 1]]
        pltpu.make_async_copy(part, part, sems.at[c]).wait()
    sky_copy.wait()


def clean_call(total_rows, flux, sky, terms):
    rows, specs, exposures, fibres = flux.shape
    return pl.pallas_call(
        functools.partial(clean_kernel, total_rows),
        out_shape=(
            jax.ShapeDtypeStruct((exposures, rows, specs, fibres), F32),
            jax.ShapeDtypeStruct((exposures, LANES), F32),
        ),
        in_specs=[VM] * (2 + len(terms)),
        out_specs=(HB, HB),
        scratch_shapes=[
            pltpu.VMEM((rows, specs, exposures, fibres), F32),
            pltpu.SemaphoreType.DMA((4,)),
            pltpu.SemaphoreType.DMA,
        ],
        compiler_params=pltpu.CompilerParams(vmem_limit_bytes=24 * 2**20),
        cost_estimate=pl.CostEstimate(flops=10**6, bytes_accessed=10**6, transcendentals=0),
        name="clean",
    )(flux, sky, *terms)


def powers(low, high):
    steps = []
    while low < high:
        steps.append(low)
        low *= 2
    return steps


def swap(values, partner):
    spec, wave = lax.axis_size("spec"), lax.axis_size("wave")
    pairs = []
    for s in range(spec):
        for i in range(wave):
            t, j = partner(s, i)
            if not 0 <= j < wave:
                t, j = s ^ 1, i
            if t < spec:
                pairs.append((s * wave + i, t * wave + j))
    return lax.ppermute(values, ("spec", "wave"), pairs)


def local(pixels, ivar, mask, psf_left, psf_right, sky_index):
    arrays = [jnp.transpose(x, (0, 2, 1, 3)) for x in (pixels, ivar, mask, psf_left, psf_right)]
    rows = pixels.shape[2]
    wave, spec = lax.axis_size("wave"), lax.axis_size("spec")
    total_rows = rows * wave
    hbm = [pltpu.with_memory_space_constraint(x, pltpu.HBM) for x in arrays]
    odd = lax.rem(lax.axis_index("wave"), 2) == 1

    def other_core(s, i):
        return (s, i ^ 1)

    near, far, head = edge_call(hbm)
    far = swap(far, lambda s, i: (s, i + 1 if i % 2 else i - 1))
    near = swap(near, other_core)
    factors = forward_call(near, head, hbm, sky_index)
    flux, sums = backward_call(wave, far, factors)
    got = swap(sums, other_core)
    flux, got = lax.optimization_barrier((flux, got))
    other = swap(flux, other_core)
    sums = jnp.where(odd, jnp.concatenate([got, sums]), jnp.concatenate([sums, got]))
    if spec == 4:
        first = swap(sums, lambda s, i: (s ^ (2 if i % 2 else 1), i ^ 1))
        third = swap(sums, lambda s, i: (s ^ 3, i ^ 1))
        second = swap(first, other_core)
        sums = (sums + jnp.where(odd, first, second)) + (jnp.where(odd, second, first) + third)
    else:
        for k in powers(1, spec):
            sums = sums + swap(sums, lambda s, i: (s ^ k, i))
    regress, sky = regress_call(total_rows, flux, other, sums)
    if wave == 8:
        routes = ((1, 0, 3, 2), (2, 3, 1, 0))
        third_route = (3, 2, 0, 1)
        first = swap(regress, lambda s, i: (s, 2 * routes[i % 2][i // 2] + i % 2))
        third = swap(regress, lambda s, i: (s, 2 * third_route[i // 2] + 1 - i % 2))
        terms = [regress, first, swap(first, other_core), third]
    else:
        for k in powers(2, wave):
            regress = regress + swap(regress, lambda s, i: (s, i ^ k if i % 2 else -1))
        terms = [jnp.where(odd, regress, swap(regress, other_core))]
    cleaned, sky = clean_call(total_rows, flux, sky, terms)
    return (jnp.transpose(cleaned, (0, 2, 1, 3)), sky[:, :rows])


def solution(mesh):
    block = P(None, "spec", "wave", None)
    return jax.shard_map(
        local,
        mesh=mesh,
        in_specs=(block,) * 5 + (P("spec", None),),
        out_specs=(block, P(None, "wave")),
        check_vma=False,
    )
```
